32 devices in a mesh: grp: 4 (over y, core), gx: 2 (over x), gy: 4 (over z).
Axes of the slice: x: 2, y: 2, z: 4, core: 2. Of those that a mesh axis runs over, the one named last changes fastest.
Arguments:
- terminal: float32 [4, 8, 64, 512], P(None, 'gx', 'gy', 'grp'), may hold values from -6 to 6
- diffusion: float32 [4], replicated, may hold values from 0.03 to 0.1
- velocity: float32 [8, 64, 512], P('gx', 'gy', 'grp'), may hold values from 0.02 to 0.3
- material: int32 [8, 64, 512], P('gx', 'gy', 'grp'), may hold values from 0 to 7
- rates: float32 [8, 8], replicated, may hold values from 0.005 to 0.04
- stoich: int32 [8, 4], replicated, may hold values from -1 to 1
- plan: int32 [8], replicated, may hold values from 0 to 15, as said below
- basis: bfloat16 [4, 8, 64, 512, 256], P('grp', 'gx', 'gy')
Outputs:
- coefficients: float32 [8, 256], replicated
- adjoint: float32 [4, 8, 64, 512], P(None, 'gx', 'gy', 'grp')
The draws below stay inside these ranges and needn't reach their ends.
Inputs may be any that keep to these rules, and one draw needn't show every extreme that they name: `plan`: 8 different step numbers in increasing order.
All inputs are finite; a program needn't handle non-finite values.
Results may differ from the reference program's by a relative error of at most 0.0045.
Values sent between devices are 32-bit elements; how exact they have to be, the bound alone decides.
No kernel may reach another device: no remote copies, remote signals or barrier semaphores. Data moves between devices by JAX's collectives and lax.ppermute only.
A program may use at most 64 MiB of HBM per device.

```python
import math
import jax
import jax.numpy as jnp
from jax import lax

SPEC = 4
MODES = 256
REACT = 8
MATS = 8
STEPS = 16
SNAPS = 8
NX = 8
NY = 64
NZ = 512


def draw_plan(key, part):
    order = jax.random.permutation(jax.random.fold_in(key, 5), STEPS)
    return jnp.sort(order[:SNAPS]).astype(jnp.int32)


def draw_basis(key, part):
    total_rows = SPEC * NX * NY * NZ
    base = jax.random.fold_in(key, 11)
    share = jax.random.normal(jax.random.fold_in(base, 1), (MODES,), jnp.float32) * (2.0 / MODES) ** 0.5

    def make_block(index):
        noise_key = jax.random.fold_in(jax.random.fold_in(base, 2), index)
        common_key = jax.random.fold_in(jax.random.fold_in(base, 3), index)
        noise = jax.random.normal(noise_key, (NY * NZ, MODES), jnp.float32)
        common = jax.random.normal(common_key, (NY * NZ, 1), jnp.float32)
        return ((noise + common * share[None, :]) * total_rows ** (-0.5)).astype(jnp.bfloat16)
    return lax.map(make_block, jnp.arange(SPEC * NX)).reshape(SPEC, NX, NY, NZ, MODES)


def set_ends(result, key, least, top_value):
    index_at = [jax.random.randint(jax.random.fold_in(key, axis), (), 0, length) for axis, length in enumerate(result.shape)]
    main_axis = result.shape.index(max(result.shape))
    neighbour = index_at[:main_axis] + [(index_at[main_axis] + 1) % result.shape[main_axis]] + index_at[main_axis + 1:]
    return result.at[tuple(index_at)].set(least).at[tuple(neighbour)].set(top_value)


def levels(stream_key, extent, split, least, largest):
    level = 1.0
    for dim, shards_of in split:
        draws = jax.random.uniform(jax.random.fold_in(jax.random.fold_in(stream_key, 6), dim), (shards_of,), jnp.float32, least / len(split), largest / len(split))
        level = level * jnp.repeat(jnp.exp(draws), extent[dim] // shards_of).reshape((-1,) + (1,) * (len(extent) - 1 - dim))
    return level


def normal_values(key, shape, scale, most, shards=(), kind=jnp.bfloat16):
    drawn = scale * jax.random.normal(key, shape, jnp.float32)
    if shards:
        drawn = drawn * levels(key, shape, shards, -0.22, 0.18)
    return jnp.clip(drawn, -most, most).astype(kind)


def setup_inputs(seed: int = 0) -> dict:
    arg_keys = jax.random.split(jax.random.key(seed), 9)
    return {
        "terminal": normal_values(arg_keys[0], (SPEC, NX, NY, NZ), 1.0, 6.0, ((1, 2), (2, 4), (3, 4)), jnp.float32),
        "diffusion": jnp.clip(jnp.exp(jax.random.uniform(arg_keys[1], (SPEC,), jnp.float32, math.log(0.03), math.log(0.1))), 0.03, 0.1),
        "velocity": jnp.clip(0.02 + 0.28 * jax.random.uniform(arg_keys[2], (NX, NY, NZ), jnp.float32) ** levels(arg_keys[2], (NX, NY, NZ), ((0, 2), (1, 4), (2, 4)), -0.2, 0.2), 0.02, 0.3),
        "material": set_ends(jax.random.randint(arg_keys[3], (NX, NY, NZ), 0, MATS), jax.random.fold_in(arg_keys[3], 1), 0, MATS - 1).astype(jnp.int32),
        "rates": jnp.clip(jnp.exp(jax.random.uniform(arg_keys[4], (MATS, REACT), jnp.float32, math.log(0.005), math.log(0.04))), 0.005, 0.04),
        "stoich": set_ends(jax.random.randint(arg_keys[5], (REACT, SPEC), -1, 2), jax.random.fold_in(arg_keys[5], 1), -1, 1).astype(jnp.int32),
        "plan": draw_plan(jax.random.fold_in(arg_keys[8], 71), 0),
        "basis": draw_basis(jax.random.fold_in(arg_keys[8], 71), 0),
    }


def reaction_table(rates, stoich):
    react_count, spec = stoich.shape
    owner = jnp.arange(react_count) % spec
    pick = (owner[:, None] == jnp.arange(spec)[None, :]).astype(jnp.float32)
    return jnp.einsum("mr,ra,rs->mas", rates.astype(jnp.float32), pick, stoich.astype(jnp.float32), precision=lax.Precision.HIGHEST)


def advance(padded, diffusion, velocity, react):
    center = padded[:, 1:-1, 1:-1, 1:-1]
    ahead = padded[:, 2:, 1:-1, 1:-1]
    beside = ahead + padded[:, :-2, 1:-1, 1:-1]
    beside = beside + padded[:, 1:-1, 2:, 1:-1] + padded[:, 1:-1, :-2, 1:-1]
    beside = beside + padded[:, 1:-1, 1:-1, 2:] + padded[:, 1:-1, 1:-1, :-2]
    spec = center.shape[0]
    sources = []
    for first in range(spec):
        total = react[first * spec] * center[0]
        for second in range(1, spec):
            total = total + react[first * spec + second] * center[second]
        sources.append(total)
    source = jnp.stack(sources)
    return center + diffusion[:, None, None, None] * (beside - 6.0 * center) + velocity[None] * (ahead - center) + source


def reference(terminal, diffusion, velocity, material, rates, stoich, plan, basis):
    table = reaction_table(rates, stoich).reshape(MATS, SPEC * SPEC)
    react = jnp.moveaxis(table[material], -1, 0)

    def single(lam, index):
        padded = jnp.pad(lam, ((0, 0), (1, 1), (1, 1), (1, 1)))
        lam = advance(padded, diffusion, velocity, react)
        return lam, lam

    final, states = lax.scan(single, terminal, jnp.arange(STEPS))
    snaps = states[plan]
    blocks = SPEC * NX
    width = NY * NZ
    ubl = basis.reshape(blocks, width, MODES)
    abl = jnp.transpose(snaps.reshape(SNAPS, blocks, width), (1, 0, 2))

    def first_part(pair):
        upart, apart = pair
        return jnp.dot(apart.astype(jnp.bfloat16), upart, preferred_element_type=jnp.float32)

    first = jnp.sum(lax.map(first_part, (ubl, abl)), axis=0)
    first_low = first.astype(jnp.bfloat16)

    def second_part(pair):
        upart, apart = pair
        proj = lax.dot_general(first_low, upart, (((1,), (1,)), ((), ())), preferred_element_type=jnp.float32)
        rest = apart - proj
        return jnp.dot(rest.astype(jnp.bfloat16), upart, preferred_element_type=jnp.float32)

    second = jnp.sum(lax.map(second_part, (ubl, abl)), axis=0)
    return first + second, final
```

```python
import functools

import jax
import jax.numpy as jnp
from jax import lax
from jax.experimental import pallas as pl
from jax.experimental.pallas import tpu as pltpu
from jax.sharding import PartitionSpec as P

STEPS = 16
LANES = 128
GROUPS = LANES // STEPS
VMEM_LIMIT = 60 * 1024 * 1024


def pairs(axis, first):
    count = lax.axis_size(axis)
    lower = range(first, count - 1, 2)
    return [(i, i + 1) for i in lower] + [(i + 1, i) for i in lower]


def exchange(value, axis, flips):
    count = lax.axis_size(axis)
    return lax.ppermute(value, axis, [(i, i ^ flips) for i in range(count)])


def sum_over(value, axis):
    count = lax.axis_size(axis)
    if count == 4:
        near, far, other = (exchange(value, axis, flips) for flips in (1, 2, 3))
        return (value + near) + (far + other)
    flips = 1
    while flips < count:
        value = value + exchange(value, axis, flips)
        flips *= 2
    return value


def sum_all(value):
    for axis in ("grp", "gx", "gy"):
        value = sum_over(value, axis)
    return value


def reaction_table(rates, stoich):
    react_count, spec = stoich.shape
    owner = jnp.arange(react_count) % spec
    pick = (owner[:, None] == jnp.arange(spec)[None, :]).astype(jnp.float32)
    return jnp.einsum(
        "mr,ra,rs->asm", rates, pick, stoich.astype(jnp.float32), precision=lax.Precision.HIGHEST
    )


def whole(count):
    return [pl.BlockSpec(memory_space=pltpu.VMEM)] * count


def scalars(count):
    return [pl.BlockSpec(memory_space=pltpu.SMEM)] * count


def edges_kernel(blocks_x, ids, *refs):
    blocks, (out_a, out_b) = refs[:-2], refs[-2:]
    fields, cells_y, cells_x, cells_z = blocks[0].shape
    per_block = cells_y // GROUPS
    even = ids[0] % 2 == 0
    place = lax.broadcasted_iota(jnp.int32, (blocks_x * cells_x, LANES), 1) // STEPS

    def field_body(field, _):
        for slot in range(len(blocks) // blocks_x):
            mine = blocks[slot * blocks_x : (slot + 1) * blocks_x]
            for part in range(per_block):
                top = bottom = None
                for group in range(GROUPS):
                    row = part * GROUPS + group
                    last = jnp.concatenate(
                        [b[field, row, :, cells_z - LANES :] for b in mine], axis=0
                    )
                    start = jnp.concatenate([b[field, row, :, :LANES] for b in mine], axis=0)
                    high = pltpu.roll(last, (STEPS * (group + 1)) % LANES, 1)
                    low = pltpu.roll(start, STEPS * group, 1) if group else start
                    top = high if top is None else jnp.where(place == group, high, top)
                    bottom = low if bottom is None else jnp.where(place == group, low, bottom)
                out_a[field, slot * per_block + part] = jnp.where(even, top, bottom)
                out_b[field, slot * per_block + part] = jnp.where(even, bottom, top)
        return 0

    lax.fori_loop(0, fields, field_body, 0)


def steps_kernel(blocks_x, ids, plan, diffusion, table, *refs):
    count_blocks = 3 * blocks_x
    blocks = refs[:count_blocks]
    side_a, side_b = refs[count_blocks : count_blocks + 2]
    adjoint = refs[count_blocks + 2]
    kept = refs[count_blocks + 3 : -3]
    state, matrix, speed = refs[-3:]
    spec, rows, all_x, wide = state.shape
    _, cells_y, cells_x, cells_z = blocks[0].shape
    grp, at_x, at_y, count_grp, count_y = (ids[i] for i in range(5))
    snaps = kept[0].shape[2]
    per_block = cells_y // GROUPS
    even_z = grp % 2 == 0
    even_y = at_y % 2 == 0
    starts = (
        cells_y,
        jnp.where(even_y, 2 * cells_y, 0),
        jnp.where(even_y, 0, 2 * cells_y),
    )
    lane = lax.broadcasted_iota(jnp.int32, (all_x, LANES), 1)
    is_right = lane < LANES // 2
    has_right = grp < count_grp - 1
    has_left = grp > 0
    beyond = jnp.where(
        is_right, jnp.where(has_right, 1.0, 0.0), jnp.where(has_left, 1.0, 0.0)
    ).astype(jnp.float32)
    inside = jnp.concatenate(
        [jnp.ones((all_x, LANES), jnp.float32)] * (cells_z // LANES) + [beyond], axis=1
    )
    row_x = lax.broadcasted_iota(jnp.int32, (all_x, wide), 0)
    place_x = (row_x + at_x * cells_x) % all_x
    is_first = place_x == 0
    is_last = place_x == all_x - 1

    for slot in range(3):
        mine = blocks[slot * blocks_x : (slot + 1) * blocks_x]
        for part in range(per_block):

            def load(field, part=part, slot=slot, mine=mine):
                packed_a = side_a[field, slot * per_block + part]
                packed_b = side_b[field, slot * per_block + part]
                right = jnp.where(even_z, packed_a, packed_b)
                left = jnp.where(even_z, packed_b, packed_a)
                out = []
                for group in range(GROUPS):
                    row = part * GROUPS + group
                    own = jnp.concatenate([b[field, row] for b in mine], axis=0)
                    after = pltpu.roll(right, (LANES - STEPS * group) % LANES, 1) if group else right
                    before = pltpu.roll(left, LANES - STEPS * (group + 1), 1) if group < GROUPS - 1 else left
                    out.append(jnp.concatenate([own, jnp.where(is_right, after, before)], axis=1))
                return out

            first_row = starts[slot] + part * GROUPS

            def species_body(s, _, load=load, first_row=first_row):
                for group, tile in enumerate(load(s)):
                    state[s, first_row + group] = tile
                return 0

            lax.fori_loop(0, spec, species_body, 0)
            winds = load(spec)
            kinds = load(spec + 1)
            for group in range(GROUPS):
                speed[first_row + group] = winds[group] * inside
                matrix[0, first_row + group] = kinds[group]

    def coefficients(row, _):
        kind = matrix[0, row].astype(jnp.int32)
        wind = speed[row]
        for a in range(spec):
            stay = inside * (1.0 - 6.0 * diffusion[a]) - wind
            for s in range(spec):
                tab = table[a * spec + s]
                tiles = [
                    jnp.concatenate(
                        [
                            jnp.take_along_axis(tab, kind[x : x + 8, z : z + LANES], axis=0)
                            for z in range(0, wide, LANES)
                        ],
                        axis=1,
                    )
                    for x in range(0, all_x, 8)
                ]
                value = jnp.concatenate(tiles, axis=0) * inside
                matrix[a * spec + s, row] = value + stay if a == s else value
        return 0

    lowest = jnp.where(at_y > 0, 0, cells_y)
    highest = jnp.where(at_y < count_y - 1, rows, rows - cells_y)
    lax.fori_loop(lowest, highest, coefficients, 0)

    def step(index, _):
        low = jnp.maximum(index + 1, lowest)
        high = jnp.minimum(rows - 1 - index, highest)

        def row_body(row, carry):
            before, here = carry
            after = [state[s, row + 1] for s in range(spec)]
            wind = speed[row]
            for a in range(spec):
                ahead = jnp.where(is_last, 0.0, pltpu.roll(here[a], all_x - 1, 0))
                behind = jnp.where(is_first, 0.0, pltpu.roll(here[a], 1, 0))
                beside = (before[a] + after[a]) + (ahead + behind)
                beside = beside + (pltpu.roll(here[a], 1, 1) + pltpu.roll(here[a], wide - 1, 1))
                mix = matrix[a * spec, row] * here[0]
                for s in range(1, spec):
                    mix = mix + matrix[a * spec + s, row] * here[s]
                state[a, row] = mix + wind * ahead + (diffusion[a] * inside) * beside
            return here, after

        def rows_at(row):
            return [state[s, row] for s in range(spec)]

        lax.fori_loop(low, high, row_body, (rows_at(low - 1), rows_at(low)))
        slot = jnp.int32(0)
        hit = jnp.int32(0)
        for j in range(snaps):
            slot = slot + jnp.where(plan[j] < index, 1, 0)
            hit = hit + jnp.where(plan[j] == index, 1, 0)

        @pl.when(hit > 0)
        def _():
            def keep(y, _):
                for flips in range(len(kept)):
                    tile = state[grp ^ flips, cells_y + y, :cells_x, :cells_z]
                    for x in range(cells_x):
                        kept[flips][x, y, pl.ds(slot, 1), :] = tile[x : x + 1]
                return 0

            lax.fori_loop(0, cells_y, keep, 0)

        return 0

    lax.fori_loop(0, STEPS, step, 0)

    def leave(s, _):
        for y in range(cells_y):
            tile = state[s, cells_y + y, :cells_x, :cells_z]
            for x in range(cells_x):
                adjoint[s, x, y : y + 1, :] = tile[x : x + 1]
        return 0

    lax.fori_loop(0, spec, leave, 0)


def product_kernel(_, part, basis, total, out):
    @pl.when(pl.program_id(0) == 0)
    def _():
        out[...] = total[...]

    _, cells_y, snaps, cells_z = part.shape
    values = part[0]
    high = values.astype(jnp.bfloat16)
    low = values - high.astype(jnp.float32)
    left = jnp.concatenate([high.astype(jnp.float32), low], axis=1).astype(jnp.bfloat16)
    acc = out[...]
    for y in range(0, cells_y, 2):
        acc = acc + jnp.dot(
            jnp.concatenate([left[y], left[y + 1]], axis=1),
            basis[0, 0, y : y + 2].reshape(2 * cells_z, basis.shape[-1]),
            preferred_element_type=jnp.float32,
        )
    out[...] = acc


def product(zone, part, basis, total):
    cells_x, cells_y, snaps, cells_z = part.shape
    modes = basis.shape[-1]
    return pl.pallas_call(
        product_kernel,
        out_shape=jax.ShapeDtypeStruct((2 * snaps, modes), jnp.float32),
        grid_spec=pltpu.PrefetchScalarGridSpec(
            num_scalar_prefetch=1,
            grid=(cells_x,),
            in_specs=[
                pl.BlockSpec((1, cells_y, snaps, cells_z), lambda x, z: (x, 0, 0, 0)),
                pl.BlockSpec((1, 1, cells_y, cells_z, modes), lambda x, z: (0, x, 0, z[0], 0)),
                pl.BlockSpec((2 * snaps, modes), lambda x, z: (0, 0)),
            ],
            out_specs=pl.BlockSpec((2 * snaps, modes), lambda x, z: (0, 0)),
        ),
        cost_estimate=pl.CostEstimate(
            flops=4 * snaps * cells_x * cells_y * cells_z * modes,
            bytes_accessed=2 * cells_x * cells_y * cells_z * modes,
            transcendentals=0,
        ),
        name="product",
    )(zone, part, basis, total)


def body(terminal, diffusion, velocity, material, rates, stoich, plan, basis):
    spec, cells_x, cells_y, cells_z = terminal.shape
    snaps, modes = plan.shape[0], basis.shape[-1]
    count_grp, count_x, count_y = (lax.axis_size(axis) for axis in ("grp", "gx", "gy"))
    grp = lax.axis_index("grp")
    ids = jnp.stack(
        [grp, lax.axis_index("gx"), lax.axis_index("gy"), jnp.int32(count_grp), jnp.int32(count_y)]
    ).astype(jnp.int32)
    table = reaction_table(rates, stoich).reshape(spec * spec, rates.shape[0], 1)
    table = jnp.broadcast_to(table, table.shape[:2] + (LANES,))

    own = jnp.concatenate(
        [terminal, velocity[None], material.astype(jnp.float32)[None]], axis=0
    ).transpose(0, 2, 1, 3)
    blocks = [own]
    for shift in range(1, count_x):
        blocks.append(
            lax.ppermute(own, "gx", [(i, (i - shift) % count_x) for i in range(count_x)])
        )
    blocks_a = [lax.ppermute(b, "gy", pairs("gy", 0)) for b in blocks]
    blocks_b = [lax.ppermute(b, "gy", pairs("gy", 1)) for b in blocks]
    blocks = blocks + blocks_a + blocks_b
    fields, all_x = spec + 2, cells_x * count_x
    packed = jax.ShapeDtypeStruct((fields, 3 * cells_y // GROUPS, all_x, LANES), jnp.float32)
    edge_a, edge_b = pl.pallas_call(
        functools.partial(edges_kernel, count_x),
        out_shape=(packed, packed),
        in_specs=scalars(1) + whole(len(blocks)),
        out_specs=tuple(whole(2)),
        compiler_params=pltpu.CompilerParams(vmem_limit_bytes=VMEM_LIMIT),
        name="edges",
    )(ids, *blocks)
    side_a = lax.ppermute(edge_a, "grp", pairs("grp", 0))
    side_b = lax.ppermute(edge_b, "grp", pairs("grp", 1))

    local = basis.reshape(-1, modes)
    gram = lax.dot_general(
        local, local, (((0,), (0,)), ((), ())), preferred_element_type=jnp.float32
    )

    wide = cells_z + LANES
    part = jax.ShapeDtypeStruct((cells_x, cells_y, snaps, cells_z), jnp.float32)
    final, *kept = pl.pallas_call(
        functools.partial(steps_kernel, count_x),
        out_shape=[jax.ShapeDtypeStruct(terminal.shape, jnp.float32)] + [part] * count_grp,
        in_specs=scalars(3) + whole(3 + len(blocks)),
        out_specs=whole(1 + count_grp),
        scratch_shapes=[
            pltpu.VMEM((spec, 3 * cells_y, all_x, wide), jnp.float32),
            pltpu.VMEM((spec * spec, 3 * cells_y, all_x, wide), jnp.float32),
            pltpu.VMEM((3 * cells_y, all_x, wide), jnp.float32),
        ],
        compiler_params=pltpu.CompilerParams(vmem_limit_bytes=VMEM_LIMIT),
        name="steps",
    )(ids, plan, diffusion, table, *blocks, side_a, side_b)

    order = sorted(range(1, count_grp), key=lambda flips: -flips)
    moved = {flips: exchange(kept[flips], "grp", flips) for flips in order}
    moved[0] = kept[0]
    total = jnp.zeros((2 * snaps, modes), jnp.float32)
    for flips in range(count_grp):
        total = product((grp ^ flips).reshape(1).astype(jnp.int32), moved[flips], basis, total)

    first = sum_all(total[:snaps])
    taken = jnp.dot(
        first.astype(jnp.bfloat16).astype(jnp.float32), gram, precision=lax.Precision.HIGHEST
    )
    second = sum_all(total[:snaps] + total[snaps:] - taken)
    return (first + second, final)


def solution(mesh):
    in_specs = (
        P(None, "gx", "gy", "grp"),
        P(),
        P("gx", "gy", "grp"),
        P("gx", "gy", "grp"),
        P(),
        P(),
        P(),
        P("grp", "gx", "gy", None, None),
    )
    out_specs = (P(), P(None, "gx", "gy", "grp"))
    return jax.shard_map(body, mesh=mesh, in_specs=in_specs, out_specs=out_specs, check_vma=False)
```

```python
import functools

import jax
import jax.numpy as jnp
from jax import lax
from jax.experimental import pallas as pl
from jax.experimental.pallas import tpu as pltpu
from jax.sharding import PartitionSpec as P

STEPS = 16
LANES = 128
GROUPS = LANES // STEPS
BLOCK = 8
VMEM_LIMIT = 60 * 1024 * 1024


def pairs(axis, first):
    count = lax.axis_size(axis)
    lower = range(first, count - 1, 2)
    return [(i, i + 1) for i in lower] + [(i + 1, i) for i in lower]


def exchange(value, axis, flips):
    count = lax.axis_size(axis)
    return lax.ppermute(value, axis, [(i, i ^ flips) for i in range(count)])


def sum_over(value, axis):
    count = lax.axis_size(axis)
    if count == 4:
        near, far, other = (exchange(value, axis, flips) for flips in (1, 2, 3))
        return (value + near) + (far + other)
    flips = 1
    while flips < count:
        value = value + exchange(value, axis, flips)
        flips *= 2
    return value


def sum_all(value):
    for axis in ("grp", "gx", "gy"):
        value = sum_over(value, axis)
    return value


def reaction_table(rates, stoich):
    react_count, spec = stoich.shape
    owner = jnp.arange(react_count) % spec
    pick = (owner[:, None] == jnp.arange(spec)[None, :]).astype(jnp.float32)
    return jnp.einsum(
        "mr,ra,rs->asm", rates, pick, stoich.astype(jnp.float32), precision=lax.Precision.HIGHEST
    )


def whole(count):
    return [pl.BlockSpec(memory_space=pltpu.VMEM)] * count


def scalars(count):
    return [pl.BlockSpec(memory_space=pltpu.SMEM)] * count


def edges_kernel(blocks_x, ids, *refs):
    blocks, (out_a, out_b) = refs[:-2], refs[-2:]
    fields, cells_y, cells_x, cells_z = blocks[0].shape
    per_block = cells_y // GROUPS
    even = ids[0] % 2 == 0
    place = lax.broadcasted_iota(jnp.int32, (blocks_x * cells_x, LANES), 1) // STEPS

    def field_body(field, _):
        for slot in range(len(blocks) // blocks_x):
            mine = blocks[slot * blocks_x : (slot + 1) * blocks_x]
            for part in range(per_block):
                top = bottom = None
                for group in range(GROUPS):
                    row = part * GROUPS + group
                    last = jnp.concatenate(
                        [b[field, row, :, cells_z - LANES :] for b in mine], axis=0
                    )
                    start = jnp.concatenate([b[field, row, :, :LANES] for b in mine], axis=0)
                    high = pltpu.roll(last, (STEPS * (group + 1)) % LANES, 1)
                    low = pltpu.roll(start, STEPS * group, 1) if group else start
                    top = high if top is None else jnp.where(place == group, high, top)
                    bottom = low if bottom is None else jnp.where(place == group, low, bottom)
                out_a[field, slot * per_block + part] = jnp.where(even, top, bottom)
                out_b[field, slot * per_block + part] = jnp.where(even, bottom, top)
        return 0

    lax.fori_loop(0, fields, field_body, 0)


def steps_kernel(blocks_x, ids, plan, diffusion, table, *refs):
    count_blocks = 3 * blocks_x
    blocks = refs[:count_blocks]
    side_a, side_b = refs[count_blocks : count_blocks + 2]
    adjoint = refs[count_blocks + 2]
    kept = refs[count_blocks + 3 : -4]
    state, other, matrix, speed = refs[-4:]
    spec, rows, all_x, wide = state.shape
    _, cells_y, cells_x, cells_z = blocks[0].shape
    grp, at_x, at_y, count_grp, count_y = (ids[i] for i in range(5))
    snaps = kept[0].shape[2]
    per_block = cells_y // GROUPS
    even_z = grp % 2 == 0
    even_y = at_y % 2 == 0
    starts = (
        BLOCK + cells_y,
        BLOCK + jnp.where(even_y, 2 * cells_y, 0),
        BLOCK + jnp.where(even_y, 0, 2 * cells_y),
    )
    lane = lax.broadcasted_iota(jnp.int32, (all_x, LANES), 1)
    is_right = lane < LANES // 2
    has_right = grp < count_grp - 1
    has_left = grp > 0
    beyond = jnp.where(
        is_right, jnp.where(has_right, 1.0, 0.0), jnp.where(has_left, 1.0, 0.0)
    ).astype(jnp.float32)
    inside = jnp.concatenate(
        [jnp.ones((all_x, LANES), jnp.float32)] * (cells_z // LANES) + [beyond], axis=1
    )
    row_x = lax.broadcasted_iota(jnp.int32, (all_x, wide), 0)
    place_x = (row_x + at_x * cells_x) % all_x
    is_first = place_x == 0
    is_last = place_x == all_x - 1

    for slot in range(3):
        mine = blocks[slot * blocks_x : (slot + 1) * blocks_x]
        for part in range(per_block):

            def load(field, part=part, slot=slot, mine=mine):
                packed_a = side_a[field, slot * per_block + part]
                packed_b = side_b[field, slot * per_block + part]
                right = jnp.where(even_z, packed_a, packed_b)
                left = jnp.where(even_z, packed_b, packed_a)
                out = []
                for group in range(GROUPS):
                    row = part * GROUPS + group
                    own = jnp.concatenate([b[field, row] for b in mine], axis=0)
                    after = pltpu.roll(right, (LANES - STEPS * group) % LANES, 1) if group else right
                    before = pltpu.roll(left, LANES - STEPS * (group + 1), 1) if group < GROUPS - 1 else left
                    out.append(jnp.concatenate([own, jnp.where(is_right, after, before)], axis=1))
                return out

            first_row = starts[slot] + part * GROUPS

            def species_body(s, _, load=load, first_row=first_row):
                for group, tile in enumerate(load(s)):
                    state[s, first_row + group] = tile
                return 0

            lax.fori_loop(0, spec, species_body, 0)
            winds = load(spec)
            kinds = load(spec + 1)
            for group in range(GROUPS):
                speed[first_row + group] = winds[group] * inside
                matrix[0, first_row + group] = kinds[group]

    def coefficients(row, _):
        kind = matrix[0, row].astype(jnp.int32)
        wind = speed[row]
        for a in range(spec):
            stay = inside * (1.0 - 6.0 * diffusion[a]) - wind
            for s in range(spec):
                tab = table[a * spec + s]
                tiles = [
                    jnp.concatenate(
                        [
                            jnp.take_along_axis(tab, kind[x : x + 8, z : z + LANES], axis=0)
                            for z in range(0, wide, LANES)
                        ],
                        axis=1,
                    )
                    for x in range(0, all_x, 8)
                ]
                value = jnp.concatenate(tiles, axis=0) * inside
                matrix[a * spec + s, row] = value + stay if a == s else value
        return 0

    zero = jnp.zeros((all_x, wide), jnp.float32)

    def clear(row, _):
        for s in range(spec):
            other[s, row] = zero
        return 0

    lax.fori_loop(0, rows, clear, 0)
    for row in (*range(BLOCK), *range(rows - BLOCK, rows)):
        speed[row] = zero
        for s in range(spec):
            state[s, row] = zero
        for k in range(spec * spec):
            matrix[k, row] = zero

    lowest = jnp.where(at_y > 0, BLOCK, BLOCK + cells_y)
    highest = jnp.where(at_y < count_y - 1, rows - BLOCK, rows - BLOCK - cells_y)
    lax.fori_loop(lowest, highest, coefficients, 0)

    def step(index, source, target):
        low = jnp.maximum(BLOCK + index + 1, lowest)
        high = jnp.minimum(rows - BLOCK - 1 - index, highest)
        turns = (high - low + BLOCK - 1) // BLOCK
        start = jnp.where(high == highest, high - turns * BLOCK, low)

        def block_body(turn, _):
            base = start + turn * BLOCK
            tiles = [[source[s, base + i] for s in range(spec)] for i in range(-1, BLOCK + 1)]
            for i in range(BLOCK):
                row = base + i
                before, here, after = tiles[i : i + 3]
                wind = speed[row]
                for a in range(spec):
                    ahead = jnp.where(is_last, 0.0, pltpu.roll(here[a], all_x - 1, 0))
                    behind = jnp.where(is_first, 0.0, pltpu.roll(here[a], 1, 0))
                    beside = (before[a] + after[a]) + (ahead + behind)
                    beside = beside + (pltpu.roll(here[a], 1, 1) + pltpu.roll(here[a], wide - 1, 1))
                    mix = matrix[a * spec, row] * here[0]
                    for s in range(1, spec):
                        mix = mix + matrix[a * spec + s, row] * here[s]
                    target[a, row] = mix + wind * ahead + spread[a] * beside
            return 0

        lax.fori_loop(0, turns, block_body, 0)
        slot = jnp.int32(0)
        hit = jnp.int32(0)
        for j in range(snaps):
            slot = slot + jnp.where(plan[j] < index, 1, 0)
            hit = hit + jnp.where(plan[j] == index, 1, 0)

        @pl.when(hit > 0)
        def _():
            def keep(y, _):
                for flips in range(len(kept)):
                    tile = target[grp ^ flips, BLOCK + cells_y + y, :cells_x, :cells_z]
                    for x in range(cells_x):
                        kept[flips][x, y, pl.ds(slot, 1), :] = tile[x : x + 1]
                return 0

            lax.fori_loop(0, cells_y, keep, 0, unroll=4)

    spread = [inside * diffusion[a] for a in range(spec)]

    def two_steps(pair, _):
        step(2 * pair, state, other)
        step(2 * pair + 1, other, state)
        return 0

    lax.fori_loop(0, STEPS // 2, two_steps, 0)

    def leave(s, _):
        for y in range(cells_y):
            tile = state[s, BLOCK + cells_y + y, :cells_x, :cells_z]
            for x in range(cells_x):
                adjoint[s, x, y : y + 1, :] = tile[x : x + 1]
        return 0

    lax.fori_loop(0, spec, leave, 0)


def product_kernel(_, part, basis, total, out):
    @pl.when(pl.program_id(0) == 0)
    def _():
        out[...] = total[...]

    _, cells_y, snaps, cells_z = part.shape
    values = part[0]
    high = values.astype(jnp.bfloat16)
    low = values - high.astype(jnp.float32)
    left = jnp.concatenate([high.astype(jnp.float32), low], axis=1).astype(jnp.bfloat16)
    acc = out[...]
    for y in range(0, cells_y, 2):
        acc = acc + jnp.dot(
            jnp.concatenate([left[y], left[y + 1]], axis=1),
            basis[0, 0, y : y + 2].reshape(2 * cells_z, basis.shape[-1]),
            preferred_element_type=jnp.float32,
        )
    out[...] = acc


def product(zone, part, basis, total):
    cells_x, cells_y, snaps, cells_z = part.shape
    modes = basis.shape[-1]
    return pl.pallas_call(
        product_kernel,
        out_shape=jax.ShapeDtypeStruct((2 * snaps, modes), jnp.float32),
        grid_spec=pltpu.PrefetchScalarGridSpec(
            num_scalar_prefetch=1,
            grid=(cells_x,),
            in_specs=[
                pl.BlockSpec((1, cells_y, snaps, cells_z), lambda x, z: (x, 0, 0, 0)),
                pl.BlockSpec((1, 1, cells_y, cells_z, modes), lambda x, z: (0, x, 0, z[0], 0)),
                pl.BlockSpec((2 * snaps, modes), lambda x, z: (0, 0)),
            ],
            out_specs=pl.BlockSpec((2 * snaps, modes), lambda x, z: (0, 0)),
        ),
        cost_estimate=pl.CostEstimate(
            flops=4 * snaps * cells_x * cells_y * cells_z * modes,
            bytes_accessed=2 * cells_x * cells_y * cells_z * modes,
            transcendentals=0,
        ),
        name="product",
    )(zone, part, basis, total)


def body(terminal, diffusion, velocity, material, rates, stoich, plan, basis):
    spec, cells_x, cells_y, cells_z = terminal.shape
    snaps, modes = plan.shape[0], basis.shape[-1]
    count_grp, count_x, count_y = (lax.axis_size(axis) for axis in ("grp", "gx", "gy"))
    grp = lax.axis_index("grp")
    ids = jnp.stack(
        [grp, lax.axis_index("gx"), lax.axis_index("gy"), jnp.int32(count_grp), jnp.int32(count_y)]
    ).astype(jnp.int32)
    table = reaction_table(rates, stoich).reshape(spec * spec, rates.shape[0], 1)
    table = jnp.broadcast_to(table, table.shape[:2] + (LANES,))

    own = jnp.concatenate(
        [terminal, velocity[None], material.astype(jnp.float32)[None]], axis=0
    ).transpose(0, 2, 1, 3)
    blocks = [own]
    for shift in range(1, count_x):
        blocks.append(
            lax.ppermute(own, "gx", [(i, (i - shift) % count_x) for i in range(count_x)])
        )
    blocks_a = [lax.ppermute(b, "gy", pairs("gy", 0)) for b in blocks]
    blocks_b = [lax.ppermute(b, "gy", pairs("gy", 1)) for b in blocks]
    blocks = blocks + blocks_a + blocks_b
    fields, all_x = spec + 2, cells_x * count_x
    packed = jax.ShapeDtypeStruct((fields, 3 * cells_y // GROUPS, all_x, LANES), jnp.float32)
    edge_a, edge_b = pl.pallas_call(
        functools.partial(edges_kernel, count_x),
        out_shape=(packed, packed),
        in_specs=scalars(1) + whole(len(blocks)),
        out_specs=tuple(whole(2)),
        compiler_params=pltpu.CompilerParams(vmem_limit_bytes=VMEM_LIMIT),
        name="edges",
    )(ids, *blocks)
    side_a = lax.ppermute(edge_a, "grp", pairs("grp", 0))
    side_b = lax.ppermute(edge_b, "grp", pairs("grp", 1))

    local = basis.reshape(-1, modes)
    gram = lax.dot_general(
        local, local, (((0,), (0,)), ((), ())), preferred_element_type=jnp.float32
    )

    side_a, side_b, gram = lax.optimization_barrier((side_a, side_b, gram))
    wide, rows = cells_z + LANES, 3 * cells_y + 2 * BLOCK
    part = jax.ShapeDtypeStruct((cells_x, cells_y, snaps, cells_z), jnp.float32)
    final, *kept = pl.pallas_call(
        functools.partial(steps_kernel, count_x),
        out_shape=[jax.ShapeDtypeStruct(terminal.shape, jnp.float32)] + [part] * count_grp,
        in_specs=scalars(3) + whole(3 + len(blocks)),
        out_specs=whole(1 + count_grp),
        scratch_shapes=[
            pltpu.VMEM((spec, rows, all_x, wide), jnp.float32),
            pltpu.VMEM((spec, rows, all_x, wide), jnp.float32),
            pltpu.VMEM((spec * spec, rows, all_x, wide), jnp.float32),
            pltpu.VMEM((rows, all_x, wide), jnp.float32),
        ],
        compiler_params=pltpu.CompilerParams(vmem_limit_bytes=VMEM_LIMIT),
        name="steps",
    )(ids, plan, diffusion, table, *blocks, side_a, side_b)

    order = sorted(range(1, count_grp), key=lambda flips: -flips)
    moved = {flips: exchange(kept[flips], "grp", flips) for flips in order}
    moved[0] = kept[0]
    total = jnp.zeros((2 * snaps, modes), jnp.float32)
    for flips in range(count_grp):
        total = product((grp ^ flips).reshape(1).astype(jnp.int32), moved[flips], basis, total)

    first = sum_all(total[:snaps])
    taken = jnp.dot(
        first.astype(jnp.bfloat16).astype(jnp.float32), gram, precision=lax.Precision.HIGHEST
    )
    second = sum_all(total[:snaps] + total[snaps:] - taken)
    return (first + second, final)


def solution(mesh):
    in_specs = (
        P(None, "gx", "gy", "grp"),
        P(),
        P("gx", "gy", "grp"),
        P("gx", "gy", "grp"),
        P(),
        P(),
        P(),
        P("grp", "gx", "gy", None, None),
    )
    out_specs = (P(), P(None, "gx", "gy", "grp"))
    return jax.shard_map(body, mesh=mesh, in_specs=in_specs, out_specs=out_specs, check_vma=False)
```

```python
import functools
import math

import jax
import jax.numpy as jnp
from jax import lax
from jax.experimental import pallas as pl
from jax.experimental.pallas import tpu as pltpu
from jax.sharding import PartitionSpec as P

STEPS = 16
LANES = 128
GROUPS = LANES // STEPS
BLOCK = 8
MIB = 1024 * 1024


def pairs(axis, first):
    count = lax.axis_size(axis)
    lower = range(first, count - 1, 2)
    return [(i, i + 1) for i in lower] + [(i + 1, i) for i in lower]


def exchange(value, axis, flips):
    count = lax.axis_size(axis)
    return lax.ppermute(value, axis, [(i, i ^ flips) for i in range(count)])


def sum_over(value, axis):
    count = lax.axis_size(axis)
    if count == 4:
        near, far, other = (exchange(value, axis, flips) for flips in (1, 2, 3))
        return (value + near) + (far + other)
    flips = 1
    while flips < count:
        value = value + exchange(value, axis, flips)
        flips *= 2
    return value


def sum_all(value):
    for axis in ("grp", "gx", "gy"):
        value = sum_over(value, axis)
    return value


def whole(count):
    return [pl.BlockSpec(memory_space=pltpu.VMEM)] * count


def scalars(count):
    return [pl.BlockSpec(memory_space=pltpu.SMEM)] * count


def anywhere(count):
    return [pl.BlockSpec(memory_space=pl.ANY)] * count


def vmem(*shapes):
    return pltpu.CompilerParams(vmem_limit_bytes=4 * sum(map(math.prod, shapes)) + 6 * MIB)


def fetch(sources, targets, sems):
    copies = [
        pltpu.make_async_copy(source, target, sems.at[i])
        for i, (source, target) in enumerate(zip(sources, targets))
    ]
    for copy in copies:
        copy.start()
    return copies


def pack_kernel(terminal, velocity, material, out):
    spec, cells_x, cells_y, cells_z = terminal.shape
    for x in range(cells_x):
        for s in range(spec):
            out[s, :, x, :] = terminal[s, x]
        out[spec, :, x, :] = velocity[x]
        out[spec + 1, :, x, :] = material[x].astype(jnp.float32)


def edges_kernel(blocks_x, *refs):
    given, (out_a, out_b, blocks, sems) = refs[:-4], refs[-4:]
    blocks = [blocks.at[i] for i in range(len(given))]
    copies = fetch(given, blocks, sems)
    fields, cells_y, cells_x, cells_z = blocks[0].shape
    per_block = cells_y // GROUPS
    even = lax.axis_index("grp") % 2 == 0
    for copy in copies:
        copy.wait()
    place = lax.broadcasted_iota(jnp.int32, (blocks_x * cells_x, LANES), 1) // STEPS

    def field_body(field, _):
        for slot in range(len(blocks) // blocks_x):
            mine = blocks[slot * blocks_x : (slot + 1) * blocks_x]
            for part in range(per_block):
                top = bottom = None
                for group in range(GROUPS):
                    row = part * GROUPS + group
                    last = jnp.concatenate(
                        [b[field, row, :, cells_z - LANES :] for b in mine], axis=0
                    )
                    start = jnp.concatenate([b[field, row, :, :LANES] for b in mine], axis=0)
                    high = pltpu.roll(last, (STEPS * (group + 1)) % LANES, 1)
                    low = pltpu.roll(start, STEPS * group, 1) if group else start
                    top = high if top is None else jnp.where(place == group, high, top)
                    bottom = low if bottom is None else jnp.where(place == group, low, bottom)
                out_a[field, slot * per_block + part] = jnp.where(even, top, bottom)
                out_b[field, slot * per_block + part] = jnp.where(even, bottom, top)
        return 0

    lax.fori_loop(0, fields, field_body, 0)


def steps_kernel(blocks_x, plan, diffusion, stoich, rates, *refs):
    count_blocks = 3 * blocks_x
    given = refs[: count_blocks + 2]
    adjoint = refs[count_blocks + 2]
    kept = refs[count_blocks + 3 : -7]
    state, other, matrix, speed, blocks, sides, sems = refs[-7:]
    blocks = [blocks.at[i] for i in range(count_blocks)]
    side_a, side_b = sides.at[0], sides.at[1]
    copies = fetch(given, blocks + [side_a, side_b], sems)
    spec, rows, all_x, wide = state.shape
    _, cells_y, cells_x, cells_z = blocks[0].shape
    grp, at_x, at_y = (lax.axis_index(axis) for axis in ("grp", "gx", "gy"))
    count_grp, count_y = lax.axis_size("grp"), lax.axis_size("gy")
    snaps = kept[0].shape[2]
    per_block = cells_y // GROUPS
    even_z = grp % 2 == 0
    even_y = at_y % 2 == 0
    starts = (
        BLOCK + cells_y,
        BLOCK + jnp.where(even_y, 2 * cells_y, 0),
        BLOCK + jnp.where(even_y, 0, 2 * cells_y),
    )
    lane = lax.broadcasted_iota(jnp.int32, (all_x, LANES), 1)
    is_right = lane < LANES // 2
    has_right = grp < count_grp - 1
    has_left = grp > 0
    beyond = jnp.where(
        is_right, jnp.where(has_right, 1.0, 0.0), jnp.where(has_left, 1.0, 0.0)
    ).astype(jnp.float32)
    inside = jnp.concatenate(
        [jnp.ones((all_x, LANES), jnp.float32)] * (cells_z // LANES) + [beyond], axis=1
    )
    row_x = lax.broadcasted_iota(jnp.int32, (all_x, wide), 0)
    place_x = (row_x + at_x * cells_x) % all_x
    is_first = place_x == 0
    is_last = place_x == all_x - 1

    columns = [
        jnp.broadcast_to(rates[:, r : r + 1], (rates.shape[0], LANES)) for r in range(rates.shape[1])
    ]
    table = [
        sum(
            columns[r] * stoich[r, s].astype(jnp.float32) for r in range(a, rates.shape[1], spec)
        )
        for a in range(spec)
        for s in range(spec)
    ]
    for copy in copies:
        copy.wait()
    for slot in range(3):
        mine = blocks[slot * blocks_x : (slot + 1) * blocks_x]
        for part in range(per_block):

            def load(field, part=part, slot=slot, mine=mine):
                packed_a = side_a[field, slot * per_block + part]
                packed_b = side_b[field, slot * per_block + part]
                right = jnp.where(even_z, packed_a, packed_b)
                left = jnp.where(even_z, packed_b, packed_a)
                out = []
                for group in range(GROUPS):
                    row = part * GROUPS + group
                    own = jnp.concatenate([b[field, row] for b in mine], axis=0)
                    after = pltpu.roll(right, (LANES - STEPS * group) % LANES, 1) if group else right
                    before = pltpu.roll(left, LANES - STEPS * (group + 1), 1) if group < GROUPS - 1 else left
                    out.append(jnp.concatenate([own, jnp.where(is_right, after, before)], axis=1))
                return out

            first_row = starts[slot] + part * GROUPS

            def species_body(s, _, load=load, first_row=first_row):
                for group, tile in enumerate(load(s)):
                    state[s, first_row + group] = tile
                return 0

            lax.fori_loop(0, spec, species_body, 0)
            winds = load(spec)
            kinds = load(spec + 1)
            for group in range(GROUPS):
                speed[first_row + group] = winds[group] * inside
                matrix[0, first_row + group] = kinds[group]

    def coefficients(row, _):
        kind = matrix[0, row].astype(jnp.int32)
        wind = speed[row]
        for a in range(spec):
            stay = inside * (1.0 - 6.0 * diffusion[a]) - wind
            for s in range(spec):
                tab = table[a * spec + s]
                tiles = [
                    jnp.concatenate(
                        [
                            jnp.take_along_axis(tab, kind[x : x + 8, z : z + LANES], axis=0)
                            for z in range(0, wide, LANES)
                        ],
                        axis=1,
                    )
                    for x in range(0, all_x, 8)
                ]
                value = jnp.concatenate(tiles, axis=0) * inside
                matrix[a * spec + s, row] = value + stay if a == s else value
        return 0

    zero = jnp.zeros((all_x, wide), jnp.float32)

    def clear(row, _):
        for s in range(spec):
            other[s, row] = zero
        return 0

    lax.fori_loop(0, rows, clear, 0)
    for row in (*range(BLOCK), *range(rows - BLOCK, rows)):
        speed[row] = zero
        for s in range(spec):
            state[s, row] = zero
        for k in range(spec * spec):
            matrix[k, row] = zero

    lowest = jnp.where(at_y > 0, BLOCK, BLOCK + cells_y)
    highest = jnp.where(at_y < count_y - 1, rows - BLOCK, rows - BLOCK - cells_y)
    lax.fori_loop(lowest, highest, coefficients, 0)

    def step(index, source, target):
        low = jnp.maximum(BLOCK + index + 1, lowest)
        high = jnp.minimum(rows - BLOCK - 1 - index, highest)
        turns = (high - low + BLOCK - 1) // BLOCK
        start = jnp.where(high == highest, high - turns * BLOCK, low)

        def block_body(turn, _):
            base = start + turn * BLOCK
            tiles = [[source[s, base + i] for s in range(spec)] for i in range(-1, BLOCK + 1)]
            for i in range(BLOCK):
                row = base + i
                before, here, after = tiles[i : i + 3]
                wind = speed[row]
                for a in range(spec):
                    ahead = jnp.where(is_last, 0.0, pltpu.roll(here[a], all_x - 1, 0))
                    behind = jnp.where(is_first, 0.0, pltpu.roll(here[a], 1, 0))
                    beside = (before[a] + after[a]) + (ahead + behind)
                    beside = beside + (pltpu.roll(here[a], 1, 1) + pltpu.roll(here[a], wide - 1, 1))
                    mix = matrix[a * spec, row] * here[0]
                    for s in range(1, spec):
                        mix = mix + matrix[a * spec + s, row] * here[s]
                    target[a, row] = mix + wind * ahead + spread[a] * beside
            return 0

        lax.fori_loop(0, turns, block_body, 0)
        slot = jnp.int32(0)
        hit = jnp.int32(0)
        for j in range(snaps):
            slot = slot + jnp.where(plan[j] < index, 1, 0)
            hit = hit + jnp.where(plan[j] == index, 1, 0)

        @pl.when(hit > 0)
        def _():
            def keep(y, _):
                for flips in range(len(kept)):
                    tile = target[grp ^ flips, BLOCK + cells_y + y, :cells_x, :cells_z]
                    for x in range(cells_x):
                        kept[flips][x, y, pl.ds(slot, 1), :] = tile[x : x + 1]
                return 0

            lax.fori_loop(0, cells_y, keep, 0, unroll=4)

    spread = [inside * diffusion[a] for a in range(spec)]

    def two_steps(pair, _):
        step(2 * pair, state, other)
        step(2 * pair + 1, other, state)
        return 0

    lax.fori_loop(0, STEPS // 2, two_steps, 0)

    def leave(s, _):
        for y in range(cells_y):
            tile = state[s, BLOCK + cells_y + y, :cells_x, :cells_z]
            for x in range(cells_x):
                adjoint[s, x, y : y + 1, :] = tile[x : x + 1]
        return 0

    lax.fori_loop(0, spec, leave, 0)


def gram_kernel(x, basis, *refs):
    (out, chunks, sems), total = refs[-3:], refs[:-3]
    count, rows, cells_z, modes = chunks.shape
    copies = fetch(
        [basis.at[0, x, pl.ds(i * rows, rows)] for i in range(count)],
        [chunks.at[i] for i in range(count)],
        sems,
    )
    acc = total[0][...] if total else None
    for i, copy in enumerate(copies):
        copy.wait()
        chunk = chunks[i].reshape(rows * cells_z, modes)
        part = lax.dot_general(
            chunk, chunk, (((0,), (0,)), ((), ())), preferred_element_type=jnp.float32
        )
        acc = part if acc is None else acc + part
    out[...] = acc


def gram_part(x, basis, *total):
    _, _, cells_y, cells_z, modes = basis.shape
    chunks = 2
    size = 2 * cells_y * cells_z * modes
    return pl.pallas_call(
        functools.partial(gram_kernel, x),
        out_shape=jax.ShapeDtypeStruct((modes, modes), jnp.float32),
        in_specs=anywhere(1) + whole(len(total)),
        out_specs=whole(1)[0],
        scratch_shapes=[
            pltpu.VMEM((chunks, cells_y // chunks, cells_z, modes), jnp.bfloat16),
            pltpu.SemaphoreType.DMA((chunks,)),
        ],
        compiler_params=pltpu.CompilerParams(vmem_limit_bytes=2 * size + 8 * MIB),
        cost_estimate=pl.CostEstimate(
            flops=2 * cells_y * cells_z * modes * modes, bytes_accessed=3 * size, transcendentals=0
        ),
        name="gram",
    )(basis, *total)


def product_kernel(flips, part, basis, *refs):
    (out_high, out_low, held, rows, sems), total = refs[-5:], refs[:-5]
    cells_x, cells_y, snaps, cells_z = held.shape
    zone = (lax.axis_index("grp") ^ flips) * cells_z
    copies = fetch(
        [part] + [basis.at[0, x, :, pl.ds(pl.multiple_of(zone, LANES), cells_z)] for x in range(cells_x)],
        [held] + [rows.at[x] for x in range(cells_x)],
        sems,
    )
    copies[0].wait()
    acc = jnp.concatenate([total[0][...], total[1][...]], axis=0) if total else None
    for x in range(cells_x):
        values = held[x]
        high = values.astype(jnp.bfloat16).astype(jnp.float32)
        left = jnp.concatenate([high, values - high], axis=1).astype(jnp.bfloat16)
        copies[1 + x].wait()
        for y in range(0, cells_y, 2):
            more = jnp.dot(
                jnp.concatenate([left[y], left[y + 1]], axis=1),
                rows[x, y : y + 2].reshape(2 * cells_z, basis.shape[-1]),
                preferred_element_type=jnp.float32,
            )
            acc = more if acc is None else acc + more
    out_high[...] = acc[:snaps]
    out_low[...] = acc[snaps:]


def product(flips, part, basis, *total):
    cells_x, cells_y, snaps, cells_z = part.shape
    modes = basis.shape[-1]
    size = 2 * cells_x * cells_y * cells_z * modes
    out = jax.ShapeDtypeStruct((snaps, modes), jnp.float32)
    return pl.pallas_call(
        functools.partial(product_kernel, flips),
        out_shape=(out, out),
        in_specs=anywhere(2) + whole(len(total)),
        out_specs=tuple(whole(2)),
        scratch_shapes=[
            pltpu.VMEM(part.shape, jnp.float32),
            pltpu.VMEM((cells_x, cells_y, cells_z, modes), jnp.bfloat16),
            pltpu.SemaphoreType.DMA((cells_x + 1,)),
        ],
        compiler_params=pltpu.CompilerParams(vmem_limit_bytes=size + 8 * MIB),
        cost_estimate=pl.CostEstimate(
            flops=2 * snaps * size, bytes_accessed=2 * size, transcendentals=0
        ),
        name="product",
    )(part, basis, *total)


def body(terminal, diffusion, velocity, material, rates, stoich, plan, basis):
    spec, cells_x, cells_y, cells_z = terminal.shape
    snaps, modes = plan.shape[0], basis.shape[-1]
    count_grp, count_x = lax.axis_size("grp"), lax.axis_size("gx")
    fields, all_x = spec + 2, cells_x * count_x
    wide, rows = cells_z + LANES, 3 * cells_y + 2 * BLOCK

    own = pl.pallas_call(
        pack_kernel,
        out_shape=jax.ShapeDtypeStruct((fields, cells_y, cells_x, cells_z), jnp.float32),
        in_specs=whole(3),
        out_specs=whole(1)[0],
        name="pack",
    )(terminal, velocity, material)
    blocks = [own]
    for shift in range(1, count_x):
        blocks.append(
            lax.ppermute(own, "gx", [(i, (i - shift) % count_x) for i in range(count_x)])
        )
    from_a = [lax.ppermute(own, "gy", pairs("gy", 0))]
    from_b = [lax.ppermute(own, "gy", pairs("gy", 1))]
    gram = gram_part(0, basis)
    *blocks, gram = lax.optimization_barrier((*blocks, gram))
    from_a += [lax.ppermute(b, "gy", pairs("gy", 0)) for b in blocks[1:]]
    from_b += [lax.ppermute(b, "gy", pairs("gy", 1)) for b in blocks[1:]]
    gram = gram_part(1, basis, gram)
    blocks = blocks + from_a + from_b
    *blocks, gram = lax.optimization_barrier((*blocks, gram))
    packed = jax.ShapeDtypeStruct((fields, 3 * cells_y // GROUPS, all_x, LANES), jnp.float32)
    held = (len(blocks), fields, cells_y, cells_x, cells_z)
    edge_a, edge_b = pl.pallas_call(
        functools.partial(edges_kernel, count_x),
        out_shape=(packed, packed),
        in_specs=anywhere(len(blocks)),
        out_specs=tuple(whole(2)),
        scratch_shapes=[pltpu.VMEM(held, jnp.float32), pltpu.SemaphoreType.DMA((len(blocks),))],
        compiler_params=vmem(held, packed.shape, packed.shape),
        name="edges",
    )(*blocks)
    side_a = lax.ppermute(edge_a, "grp", pairs("grp", 0))
    side_b = lax.ppermute(edge_b, "grp", pairs("grp", 1))
    gram = gram_part(2, basis, gram)
    side_a, side_b, gram = lax.optimization_barrier((side_a, side_b, gram))

    part = jax.ShapeDtypeStruct((cells_x, cells_y, snaps, cells_z), jnp.float32)
    room = (rows, all_x, wide)
    shapes = [(spec, *room), (spec, *room), (spec * spec, *room), room, held, (2, *packed.shape)]
    final, *kept = pl.pallas_call(
        functools.partial(steps_kernel, count_x),
        out_shape=[jax.ShapeDtypeStruct(terminal.shape, jnp.float32)] + [part] * count_grp,
        in_specs=scalars(3) + whole(1) + anywhere(len(blocks) + 2),
        out_specs=whole(1 + count_grp),
        scratch_shapes=[pltpu.VMEM(shape, jnp.float32) for shape in shapes]
        + [pltpu.SemaphoreType.DMA((len(blocks) + 2,))],
        compiler_params=vmem(*shapes, terminal.shape, (count_grp, *part.shape)),
        name="steps",
    )(plan, diffusion, stoich, rates, *blocks, side_a, side_b)

    order = sorted(range(1, count_grp), key=lambda flips: -flips)
    moved = {flips: exchange(kept[flips], "grp", flips) for flips in order}
    moved[0] = kept[0]
    total = ()
    for flips in range(count_grp):
        total = product(flips, moved[flips], basis, *total)
        if flips == min(1, count_grp - 1):
            for x in range(3, cells_x):
                gram = gram_part(x, basis, gram)
            *total, gram = lax.optimization_barrier((*total, gram))
    high, low = total

    first = sum_all(high)
    taken = jnp.dot(
        first.astype(jnp.bfloat16).astype(jnp.float32), gram, precision=lax.Precision.HIGHEST
    )
    second = sum_all(high + low - taken)
    return (first + second, final)


def solution(mesh):
    in_specs = (
        P(None, "gx", "gy", "grp"),
        P(),
        P("gx", "gy", "grp"),
        P("gx", "gy", "grp"),
        P(),
        P(),
        P(),
        P("grp", "gx", "gy", None, None),
    )
    out_specs = (P(), P(None, "gx", "gy", "grp"))
    return jax.shard_map(body, mesh=mesh, in_specs=in_specs, out_specs=out_specs, check_vma=False)
```

```python
import functools
import math

import jax
import jax.numpy as jnp
from jax import lax
from jax.experimental import pallas as pl
from jax.experimental.pallas import tpu as pltpu
from jax.sharding import PartitionSpec as P

STEPS = 16
LANES = 128
GROUPS = LANES // STEPS
BLOCK = 8
MIB = 1024 * 1024
BASIS_VMEM = 50 * MIB


def pairs(axis, first):
    count = lax.axis_size(axis)
    lower = range(first, count - 1, 2)
    return [(i, i + 1) for i in lower] + [(i + 1, i) for i in lower]


def exchange(value, axis, flips):
    count = lax.axis_size(axis)
    return lax.ppermute(value, axis, [(i, i ^ flips) for i in range(count)])


def sum_over(value, axis):
    count = lax.axis_size(axis)
    if count == 4:
        near, far, other = (exchange(value, axis, flips) for flips in (1, 2, 3))
        return (value + near) + (far + other)
    flips = 1
    while flips < count:
        value = value + exchange(value, axis, flips)
        flips *= 2
    return value


def sum_all(value):
    for axis in ("grp", "gx", "gy"):
        value = sum_over(value, axis)
    return value


def whole(count):
    return [pl.BlockSpec(memory_space=pltpu.VMEM)] * count


def scalars(count):
    return [pl.BlockSpec(memory_space=pltpu.SMEM)] * count


def anywhere(count):
    return [pl.BlockSpec(memory_space=pl.ANY)] * count


def vmem(*shapes):
    return pltpu.CompilerParams(vmem_limit_bytes=4 * sum(map(math.prod, shapes)) + 6 * MIB)


def fetch(sources, targets, sems):
    copies = [
        pltpu.make_async_copy(source, target, sems.at[i])
        for i, (source, target) in enumerate(zip(sources, targets))
    ]
    for copy in copies:
        copy.start()
    return copies


def pack_kernel(terminal, velocity, material, out):
    spec, cells_x, cells_y, cells_z = terminal.shape
    for x in range(cells_x):
        for s in range(spec):
            out[s, :, x, :] = terminal[s, x]
        out[spec, :, x, :] = velocity[x]
        out[spec + 1, :, x, :] = material[x].astype(jnp.float32)


def edges_kernel(blocks_x, *refs):
    given, (out_a, out_b, blocks, sems) = refs[:-4], refs[-4:]
    blocks = [blocks.at[i] for i in range(len(given))]
    copies = fetch(given, blocks, sems)
    fields, cells_y, cells_x, cells_z = blocks[0].shape
    per_block = cells_y // GROUPS
    even = lax.axis_index("grp") % 2 == 0
    for copy in copies:
        copy.wait()
    place = lax.broadcasted_iota(jnp.int32, (blocks_x * cells_x, LANES), 1) // STEPS

    def field_body(field, _):
        for slot in range(len(blocks) // blocks_x):
            mine = blocks[slot * blocks_x : (slot + 1) * blocks_x]
            for part in range(per_block):
                top = bottom = None
                for group in range(GROUPS):
                    row = part * GROUPS + group
                    last = jnp.concatenate(
                        [b[field, row, :, cells_z - LANES :] for b in mine], axis=0
                    )
                    start = jnp.concatenate([b[field, row, :, :LANES] for b in mine], axis=0)
                    high = pltpu.roll(last, (STEPS * (group + 1)) % LANES, 1)
                    low = pltpu.roll(start, STEPS * group, 1) if group else start
                    top = high if top is None else jnp.where(place == group, high, top)
                    bottom = low if bottom is None else jnp.where(place == group, low, bottom)
                out_a[field, slot * per_block + part] = jnp.where(even, top, bottom)
                out_b[field, slot * per_block + part] = jnp.where(even, bottom, top)
        return 0

    lax.fori_loop(0, fields, field_body, 0)


def steps_kernel(blocks_x, plan, diffusion, stoich, rates, *refs):
    count_blocks = 3 * blocks_x
    given = refs[: count_blocks + 2]
    adjoint = refs[count_blocks + 2]
    kept = refs[count_blocks + 3 : -7]
    state, other, matrix, speed, blocks, sides, sems = refs[-7:]
    blocks = [blocks.at[i] for i in range(count_blocks)]
    side_a, side_b = sides.at[0], sides.at[1]
    copies = fetch(given, blocks + [side_a, side_b], sems)
    spec, rows, all_x, wide = state.shape
    _, cells_y, cells_x, cells_z = blocks[0].shape
    grp, at_x, at_y = (lax.axis_index(axis) for axis in ("grp", "gx", "gy"))
    count_grp, count_y = lax.axis_size("grp"), lax.axis_size("gy")
    snaps = kept[0].shape[2]
    per_block = cells_y // GROUPS
    even_z = grp % 2 == 0
    even_y = at_y % 2 == 0
    starts = (
        BLOCK + cells_y,
        BLOCK + jnp.where(even_y, 2 * cells_y, 0),
        BLOCK + jnp.where(even_y, 0, 2 * cells_y),
    )
    lane = lax.broadcasted_iota(jnp.int32, (all_x, LANES), 1)
    is_right = lane < LANES // 2
    has_right = grp < count_grp - 1
    has_left = grp > 0
    beyond = jnp.where(
        is_right, jnp.where(has_right, 1.0, 0.0), jnp.where(has_left, 1.0, 0.0)
    ).astype(jnp.float32)
    inside = jnp.concatenate(
        [jnp.ones((all_x, LANES), jnp.float32)] * (cells_z // LANES) + [beyond], axis=1
    )
    row_x = lax.broadcasted_iota(jnp.int32, (all_x, wide), 0)
    place_x = (row_x + at_x * cells_x) % all_x
    is_first = place_x == 0
    is_last = place_x == all_x - 1

    columns = [
        jnp.broadcast_to(rates[:, r : r + 1], (rates.shape[0], LANES)) for r in range(rates.shape[1])
    ]
    table = [
        sum(
            columns[r] * stoich[r, s].astype(jnp.float32) for r in range(a, rates.shape[1], spec)
        )
        for a in range(spec)
        for s in range(spec)
    ]
    for copy in copies:
        copy.wait()
    for slot in range(3):
        mine = blocks[slot * blocks_x : (slot + 1) * blocks_x]
        for part in range(per_block):

            def load(field, part=part, slot=slot, mine=mine):
                packed_a = side_a[field, slot * per_block + part]
                packed_b = side_b[field, slot * per_block + part]
                right = jnp.where(even_z, packed_a, packed_b)
                left = jnp.where(even_z, packed_b, packed_a)
                out = []
                for group in range(GROUPS):
                    row = part * GROUPS + group
                    own = jnp.concatenate([b[field, row] for b in mine], axis=0)
                    after = pltpu.roll(right, (LANES - STEPS * group) % LANES, 1) if group else right
                    before = pltpu.roll(left, LANES - STEPS * (group + 1), 1) if group < GROUPS - 1 else left
                    out.append(jnp.concatenate([own, jnp.where(is_right, after, before)], axis=1))
                return out

            first_row = starts[slot] + part * GROUPS

            def species_body(s, _, load=load, first_row=first_row):
                for group, tile in enumerate(load(s)):
                    state[s, first_row + group] = tile
                return 0

            lax.fori_loop(0, spec, species_body, 0)
            winds = load(spec)
            kinds = load(spec + 1)
            for group in range(GROUPS):
                speed[first_row + group] = winds[group] * inside
                matrix[0, first_row + group] = kinds[group]

    def coefficients(row, _):
        kind = matrix[0, row].astype(jnp.int32)
        wind = speed[row]
        for a in range(spec):
            stay = inside * (1.0 - 6.0 * diffusion[a]) - wind
            for s in range(spec):
                tab = table[a * spec + s]
                tiles = [
                    jnp.concatenate(
                        [
                            jnp.take_along_axis(tab, kind[x : x + 8, z : z + LANES], axis=0)
                            for z in range(0, wide, LANES)
                        ],
                        axis=1,
                    )
                    for x in range(0, all_x, 8)
                ]
                value = jnp.concatenate(tiles, axis=0) * inside
                matrix[a * spec + s, row] = value + stay if a == s else value
        return 0

    zero = jnp.zeros((all_x, wide), jnp.float32)

    def clear(row, _):
        for s in range(spec):
            other[s, row] = zero
        return 0

    lax.fori_loop(0, rows, clear, 0)
    for row in (*range(BLOCK), *range(rows - BLOCK, rows)):
        speed[row] = zero
        for s in range(spec):
            state[s, row] = zero
        for k in range(spec * spec):
            matrix[k, row] = zero

    lowest = jnp.where(at_y > 0, BLOCK, BLOCK + cells_y)
    highest = jnp.where(at_y < count_y - 1, rows - BLOCK, rows - BLOCK - cells_y)
    lax.fori_loop(lowest, highest, coefficients, 0)

    def step(index, source, target):
        low = jnp.maximum(BLOCK + index + 1, lowest)
        high = jnp.minimum(rows - BLOCK - 1 - index, highest)
        turns = (high - low + BLOCK - 1) // BLOCK
        start = jnp.where(high == highest, high - turns * BLOCK, low)

        def block_body(turn, _):
            base = start + turn * BLOCK
            tiles = [[source[s, base + i] for s in range(spec)] for i in range(-1, BLOCK + 1)]
            for i in range(BLOCK):
                row = base + i
                before, here, after = tiles[i : i + 3]
                wind = speed[row]
                for a in range(spec):
                    ahead = jnp.where(is_last, 0.0, pltpu.roll(here[a], all_x - 1, 0))
                    behind = jnp.where(is_first, 0.0, pltpu.roll(here[a], 1, 0))
                    beside = (before[a] + after[a]) + (ahead + behind)
                    beside = beside + (pltpu.roll(here[a], 1, 1) + pltpu.roll(here[a], wide - 1, 1))
                    mix = matrix[a * spec, row] * here[0]
                    for s in range(1, spec):
                        mix = mix + matrix[a * spec + s, row] * here[s]
                    target[a, row] = mix + wind * ahead + spread[a] * beside
            return 0

        lax.fori_loop(0, turns, block_body, 0)
        slot = jnp.int32(0)
        hit = jnp.int32(0)
        for j in range(snaps):
            slot = slot + jnp.where(plan[j] < index, 1, 0)
            hit = hit + jnp.where(plan[j] == index, 1, 0)

        @pl.when(hit > 0)
        def _():
            def keep(y, _):
                for flips in range(len(kept)):
                    tile = target[grp ^ flips, BLOCK + cells_y + y, :cells_x, :cells_z]
                    for x in range(cells_x):
                        kept[flips][x, y, pl.ds(slot, 1), :] = tile[x : x + 1]
                return 0

            lax.fori_loop(0, cells_y, keep, 0, unroll=4)

    spread = [inside * diffusion[a] for a in range(spec)]

    def two_steps(pair, _):
        step(2 * pair, state, other)
        step(2 * pair + 1, other, state)
        return 0

    lax.fori_loop(0, STEPS // 2, two_steps, 0)

    def leave(s, _):
        for y in range(cells_y):
            tile = state[s, BLOCK + cells_y + y, :cells_x, :cells_z]
            for x in range(cells_x):
                adjoint[s, x, y : y + 1, :] = tile[x : x + 1]
        return 0

    lax.fori_loop(0, spec, leave, 0)


def gram_kernel(x, given, basis, *refs):
    total, (out, chunks, held, sems) = refs[:given], refs[given:]
    count, rows, cells_z, modes = chunks.shape
    copies = fetch(
        [basis.at[0, x, pl.ds(i * rows, rows)] for i in range(count)] + list(total),
        [chunks.at[i] for i in range(count)] + [held],
        sems,
    )
    acc = None
    for i in range(count):
        copies[i].wait()
        chunk = chunks[i].reshape(rows * cells_z, modes)
        part = lax.dot_general(
            chunk, chunk, (((0,), (0,)), ((), ())), preferred_element_type=jnp.float32
        )
        acc = part if acc is None else acc + part
    if total:
        copies[-1].wait()
        acc = acc + held[...]
    out[...] = acc


def gram_part(x, basis, *total):
    _, _, cells_y, cells_z, modes = basis.shape
    chunks = 2
    size = 2 * cells_y * cells_z * modes
    return pl.pallas_call(
        functools.partial(gram_kernel, x, len(total)),
        out_shape=jax.ShapeDtypeStruct((modes, modes), jnp.float32),
        in_specs=anywhere(1 + len(total)),
        out_specs=whole(1)[0],
        scratch_shapes=[
            pltpu.VMEM((chunks, cells_y // chunks, cells_z, modes), jnp.bfloat16),
            pltpu.VMEM((modes, modes), jnp.float32),
            pltpu.SemaphoreType.DMA((chunks + 1,)),
        ],
        compiler_params=pltpu.CompilerParams(vmem_limit_bytes=BASIS_VMEM),
        cost_estimate=pl.CostEstimate(
            flops=2 * cells_y * cells_z * modes * modes, bytes_accessed=3 * size, transcendentals=0
        ),
        name="gram",
    )(basis, *total)


def rows_of(basis, flips, cells_z):
    zone = (lax.axis_index("grp") ^ flips) * cells_z
    return [
        basis.at[0, x, :, pl.ds(pl.multiple_of(zone, LANES), cells_z)]
        for x in range(basis.shape[1])
    ]


def multiply(held, rows, waits, acc):
    cells_x, cells_y, snaps, cells_z = held.shape
    for x in range(cells_x):
        values = held[x]
        high = values.astype(jnp.bfloat16).astype(jnp.float32)
        left = jnp.concatenate([high, values - high], axis=1).astype(jnp.bfloat16)
        waits[x].wait()
        for y in range(0, cells_y, 2):
            more = jnp.dot(
                jnp.concatenate([left[y], left[y + 1]], axis=1),
                rows[x, y : y + 2].reshape(2 * cells_z, rows.shape[-1]),
                preferred_element_type=jnp.float32,
            )
            acc = more if acc is None else acc + more
    return acc


def first_kernel(later, gram_x, part, basis, gram, *refs):
    out_high, out_low, out_gram, *ahead = refs[: 3 + len(later)]
    held, rows, chunks, total, sems = refs[3 + len(later) :]
    cells_x, cells_y, snaps, cells_z = held.shape
    modes = rows.shape[-1]
    sources = [part, *rows_of(basis, 0, cells_z)]
    targets = [held, *(rows.at[x] for x in range(cells_x))]
    sources += [basis.at[0, x] for x in gram_x] + [gram]
    targets += [chunks.at[i] for i in range(len(gram_x))] + [total]
    start_gram = 1 + cells_x
    for i, flips in enumerate(later):
        sources += rows_of(basis, flips, cells_z)
        targets += [ahead[i].at[x] for x in range(cells_x)]
    copies = fetch(sources, targets, sems)
    copies[0].wait()
    acc = multiply(held, rows, copies[1:], None)
    out_high[...] = acc[:snaps]
    out_low[...] = acc[snaps:]
    acc = None
    for i in range(len(gram_x)):
        copies[start_gram + i].wait()
        chunk = chunks[i].reshape(-1, modes)
        more = lax.dot_general(
            chunk, chunk, (((0,), (0,)), ((), ())), preferred_element_type=jnp.float32
        )
        acc = more if acc is None else acc + more
    for copy in copies[start_gram + len(gram_x) :]:
        copy.wait()
    out_gram[...] = total[...] if acc is None else acc + total[...]


def product_kernel(flips, part, basis, high, low, out_high, out_low, held, rows, sums, sems):
    cells_x, cells_y, snaps, cells_z = held.shape
    if flips is None:
        sources = [basis.at[x] for x in range(cells_x)]
    else:
        sources = rows_of(basis, flips, cells_z)
    copies = fetch(
        [part, *sources, high, low],
        [held, *(rows.at[x] for x in range(cells_x)), sums.at[0], sums.at[1]],
        sems,
    )
    copies[0].wait()
    acc = multiply(held, rows, copies[1:], None)
    copies[-2].wait()
    copies[-1].wait()
    out_high[...] = acc[:snaps] + sums[0]
    out_low[...] = acc[snaps:] + sums[1]


def first_product(part, basis, gram, later, gram_x):
    cells_x, cells_y, snaps, cells_z = part.shape
    modes = basis.shape[-1]
    size = 2 * cells_x * cells_y * cells_z * modes
    out = jax.ShapeDtypeStruct((snaps, modes), jnp.float32)
    rows = (cells_x, cells_y, cells_z, modes)
    return pl.pallas_call(
        functools.partial(first_kernel, later, gram_x),
        out_shape=[out, out, jax.ShapeDtypeStruct(gram.shape, jnp.float32)]
        + [jax.ShapeDtypeStruct(rows, jnp.bfloat16)] * len(later),
        in_specs=anywhere(3),
        out_specs=whole(3) + anywhere(len(later)),
        scratch_shapes=[
            pltpu.VMEM(part.shape, jnp.float32),
            pltpu.VMEM(rows, jnp.bfloat16),
            pltpu.VMEM((max(len(gram_x), 1), *basis.shape[2:]), jnp.bfloat16),
            pltpu.VMEM(gram.shape, jnp.float32),
            pltpu.SemaphoreType.DMA((2 + cells_x * (1 + len(later)) + len(gram_x),)),
        ],
        compiler_params=pltpu.CompilerParams(vmem_limit_bytes=BASIS_VMEM),
        cost_estimate=pl.CostEstimate(
            flops=2 * snaps * size, bytes_accessed=4 * size, transcendentals=0
        ),
        name="first_product",
    )(part, basis, gram)


def product(flips, part, basis, high, low):
    cells_x, cells_y, snaps, cells_z = part.shape
    modes = basis.shape[-1]
    size = 2 * cells_x * cells_y * cells_z * modes
    out = jax.ShapeDtypeStruct((snaps, modes), jnp.float32)
    return pl.pallas_call(
        functools.partial(product_kernel, flips),
        out_shape=(out, out),
        in_specs=anywhere(4),
        out_specs=tuple(whole(2)),
        scratch_shapes=[
            pltpu.VMEM(part.shape, jnp.float32),
            pltpu.VMEM((cells_x, cells_y, cells_z, modes), jnp.bfloat16),
            pltpu.VMEM((2, snaps, modes), jnp.float32),
            pltpu.SemaphoreType.DMA((cells_x + 3,)),
        ],
        compiler_params=pltpu.CompilerParams(vmem_limit_bytes=BASIS_VMEM),
        cost_estimate=pl.CostEstimate(
            flops=2 * snaps * size, bytes_accessed=2 * size, transcendentals=0
        ),
        name="product",
    )(part, basis, high, low)


def body(terminal, diffusion, velocity, material, rates, stoich, plan, basis):
    spec, cells_x, cells_y, cells_z = terminal.shape
    snaps, modes = plan.shape[0], basis.shape[-1]
    count_grp, count_x = lax.axis_size("grp"), lax.axis_size("gx")
    fields, all_x = spec + 2, cells_x * count_x
    wide, depth = cells_z + LANES, 3 * cells_y + 2 * BLOCK

    own = pl.pallas_call(
        pack_kernel,
        out_shape=jax.ShapeDtypeStruct((fields, cells_y, cells_x, cells_z), jnp.float32),
        in_specs=whole(3),
        out_specs=whole(1)[0],
        name="pack",
    )(terminal, velocity, material)
    blocks = [own]
    for shift in range(1, count_x):
        blocks.append(
            lax.ppermute(own, "gx", [(i, (i - shift) % count_x) for i in range(count_x)])
        )
    from_a = [lax.ppermute(own, "gy", pairs("gy", 0))]
    from_b = [lax.ppermute(own, "gy", pairs("gy", 1))]
    gram = gram_part(0, basis)
    *blocks, gram = lax.optimization_barrier((*blocks, gram))
    from_a += [lax.ppermute(b, "gy", pairs("gy", 0)) for b in blocks[1:]]
    from_b += [lax.ppermute(b, "gy", pairs("gy", 1)) for b in blocks[1:]]
    gram = gram_part(1, basis, gram)
    blocks = blocks + from_a + from_b
    *blocks, gram = lax.optimization_barrier((*blocks, gram))
    packed = jax.ShapeDtypeStruct((fields, 3 * cells_y // GROUPS, all_x, LANES), jnp.float32)
    held = (len(blocks), fields, cells_y, cells_x, cells_z)
    edge_a, edge_b = pl.pallas_call(
        functools.partial(edges_kernel, count_x),
        out_shape=(packed, packed),
        in_specs=anywhere(len(blocks)),
        out_specs=tuple(whole(2)),
        scratch_shapes=[pltpu.VMEM(held, jnp.float32), pltpu.SemaphoreType.DMA((len(blocks),))],
        compiler_params=vmem(held, packed.shape, packed.shape),
        name="edges",
    )(*blocks)
    side_a = lax.ppermute(edge_a, "grp", pairs("grp", 0))
    side_b = lax.ppermute(edge_b, "grp", pairs("grp", 1))
    gram = gram_part(2, basis, gram)
    side_a, side_b, gram = lax.optimization_barrier((side_a, side_b, gram))

    part = jax.ShapeDtypeStruct((cells_x, cells_y, snaps, cells_z), jnp.float32)
    room = (depth, all_x, wide)
    shapes = [(spec, *room), (spec, *room), (spec * spec, *room), room, held, (2, *packed.shape)]
    final, *kept = pl.pallas_call(
        functools.partial(steps_kernel, count_x),
        out_shape=[jax.ShapeDtypeStruct(terminal.shape, jnp.float32)] + [part] * count_grp,
        in_specs=scalars(3) + whole(1) + anywhere(len(blocks) + 2),
        out_specs=whole(1 + count_grp),
        scratch_shapes=[pltpu.VMEM(shape, jnp.float32) for shape in shapes]
        + [pltpu.SemaphoreType.DMA((len(blocks) + 2,))],
        compiler_params=vmem(*shapes, terminal.shape, (count_grp, *part.shape)),
        name="steps",
    )(plan, diffusion, stoich, rates, *blocks, side_a, side_b)

    order = sorted(range(1, count_grp), key=lambda flips: -flips)
    moved = {flips: exchange(kept[flips], "grp", flips) for flips in order}
    later = tuple(range(2, count_grp))
    high, low, gram, *ahead = first_product(
        kept[0], basis, gram, later, tuple(range(3, cells_x))
    )
    if count_grp > 1:
        high, low = product(1, moved[1], basis, high, low)
    for flips, rows in zip(later, ahead):
        high, low = product(None, moved[flips], rows, high, low)

    first = sum_all(high)
    taken = jnp.dot(
        first.astype(jnp.bfloat16).astype(jnp.float32), gram, precision=lax.Precision.HIGHEST
    )
    second = sum_all(high + low - taken)
    return (first + second, final)


def solution(mesh):
    in_specs = (
        P(None, "gx", "gy", "grp"),
        P(),
        P("gx", "gy", "grp"),
        P("gx", "gy", "grp"),
        P(),
        P(),
        P(),
        P("grp", "gx", "gy", None, None),
    )
    out_specs = (P(), P(None, "gx", "gy", "grp"))
    return jax.shard_map(body, mesh=mesh, in_specs=in_specs, out_specs=out_specs, check_vma=False)
```

```python
import functools
import math

import jax
import jax.numpy as jnp
from jax import lax
from jax.experimental import pallas as pl
from jax.experimental.pallas import tpu as pltpu
from jax.sharding import PartitionSpec as P

STEPS = 16
LANES = 128
GROUPS = LANES // STEPS
BLOCK = 8
MIB = 1024 * 1024
BASIS_VMEM = 50 * MIB


def pairs(axis, first):
    count = lax.axis_size(axis)
    lower = range(first, count - 1, 2)
    return [(i, i + 1) for i in lower] + [(i + 1, i) for i in lower]


def exchange(value, axis, flips):
    count = lax.axis_size(axis)
    return lax.ppermute(value, axis, [(i, i ^ flips) for i in range(count)])


def sum_over(value, axis):
    count = lax.axis_size(axis)
    if count == 4:
        near, far, other = (exchange(value, axis, flips) for flips in (1, 2, 3))
        return (value + near) + (far + other)
    flips = 1
    while flips < count:
        value = value + exchange(value, axis, flips)
        flips *= 2
    return value


def sum_all(value):
    for axis in ("grp", "gx", "gy"):
        value = sum_over(value, axis)
    return value


def whole(count):
    return [pl.BlockSpec(memory_space=pltpu.VMEM)] * count


def scalars(count):
    return [pl.BlockSpec(memory_space=pltpu.SMEM)] * count


def anywhere(count):
    return [pl.BlockSpec(memory_space=pl.ANY)] * count


def vmem(*shapes):
    return pltpu.CompilerParams(vmem_limit_bytes=4 * sum(map(math.prod, shapes)) + 6 * MIB)


def fetch(sources, targets, sems):
    copies = [
        pltpu.make_async_copy(source, target, sems.at[i])
        for i, (source, target) in enumerate(zip(sources, targets))
    ]
    for copy in copies:
        copy.start()
    return copies


def pack_kernel(terminal, velocity, material, out):
    spec, cells_x, cells_y, cells_z = terminal.shape
    for x in range(cells_x):
        for s in range(spec):
            out[s, :, x, :] = terminal[s, x]
        out[spec, :, x, :] = velocity[x]
        out[spec + 1, :, x, :] = material[x].astype(jnp.float32)


def edges_kernel(blocks_x, *refs):
    given, (out_a, out_b, blocks, sems) = refs[:-4], refs[-4:]
    blocks = [blocks.at[i] for i in range(len(given))]
    copies = fetch(given, blocks, sems)
    fields, cells_y, cells_x, cells_z = blocks[0].shape
    per_block = cells_y // GROUPS
    even = lax.axis_index("grp") % 2 == 0
    for copy in copies:
        copy.wait()
    place = lax.broadcasted_iota(jnp.int32, (blocks_x * cells_x, LANES), 1) // STEPS

    def field_body(field, _):
        for slot in range(len(blocks) // blocks_x):
            mine = blocks[slot * blocks_x : (slot + 1) * blocks_x]
            for part in range(per_block):
                top = bottom = None
                for group in range(GROUPS):
                    row = part * GROUPS + group
                    last = jnp.concatenate(
                        [b[field, row, :, cells_z - LANES :] for b in mine], axis=0
                    )
                    start = jnp.concatenate([b[field, row, :, :LANES] for b in mine], axis=0)
                    high = pltpu.roll(last, (STEPS * (group + 1)) % LANES, 1)
                    low = pltpu.roll(start, STEPS * group, 1) if group else start
                    top = high if top is None else jnp.where(place == group, high, top)
                    bottom = low if bottom is None else jnp.where(place == group, low, bottom)
                out_a[field, slot * per_block + part] = jnp.where(even, top, bottom)
                out_b[field, slot * per_block + part] = jnp.where(even, bottom, top)
        return 0

    lax.fori_loop(0, fields, field_body, 0)


def steps_kernel(blocks_x, plan, diffusion, stoich, rates, *refs):
    count_blocks = 3 * blocks_x
    given = refs[: count_blocks + 2]
    adjoint = refs[count_blocks + 2]
    kept = refs[count_blocks + 3 : -7]
    state, other, matrix, speed, blocks, sides, sems = refs[-7:]
    blocks = [blocks.at[i] for i in range(count_blocks)]
    side_a, side_b = sides.at[0], sides.at[1]
    copies = fetch(given, blocks + [side_a, side_b], sems)
    spec, rows, all_x, wide = state.shape
    _, cells_y, cells_x, cells_z = blocks[0].shape
    grp, at_x, at_y = (lax.axis_index(axis) for axis in ("grp", "gx", "gy"))
    count_grp, count_y = lax.axis_size("grp"), lax.axis_size("gy")
    snaps = kept[0].shape[2]
    per_block = cells_y // GROUPS
    even_z = grp % 2 == 0
    even_y = at_y % 2 == 0
    starts = (
        BLOCK + cells_y,
        BLOCK + jnp.where(even_y, 2 * cells_y, 0),
        BLOCK + jnp.where(even_y, 0, 2 * cells_y),
    )
    lane = lax.broadcasted_iota(jnp.int32, (all_x, LANES), 1)
    is_right = lane < LANES // 2
    has_right = grp < count_grp - 1
    has_left = grp > 0
    beyond = jnp.where(
        is_right, jnp.where(has_right, 1.0, 0.0), jnp.where(has_left, 1.0, 0.0)
    ).astype(jnp.float32)
    inside = jnp.concatenate(
        [jnp.ones((all_x, LANES), jnp.float32)] * (cells_z // LANES) + [beyond], axis=1
    )
    row_x = lax.broadcasted_iota(jnp.int32, (all_x, wide), 0)
    place_x = (row_x + at_x * cells_x) % all_x
    is_first = place_x == 0
    is_last = place_x == all_x - 1

    columns = [
        jnp.broadcast_to(rates[:, r : r + 1], (rates.shape[0], LANES)) for r in range(rates.shape[1])
    ]
    table = [
        sum(
            columns[r] * stoich[r, s].astype(jnp.float32) for r in range(a, rates.shape[1], spec)
        )
        for a in range(spec)
        for s in range(spec)
    ]
    for copy in copies:
        copy.wait()
    for slot in range(3):
        mine = blocks[slot * blocks_x : (slot + 1) * blocks_x]
        for part in range(per_block):

            def load(field, part=part, slot=slot, mine=mine):
                packed_a = side_a[field, slot * per_block + part]
                packed_b = side_b[field, slot * per_block + part]
                right = jnp.where(even_z, packed_a, packed_b)
                left = jnp.where(even_z, packed_b, packed_a)
                out = []
                for group in range(GROUPS):
                    row = part * GROUPS + group
                    own = jnp.concatenate([b[field, row] for b in mine], axis=0)
                    after = pltpu.roll(right, (LANES - STEPS * group) % LANES, 1) if group else right
                    before = pltpu.roll(left, LANES - STEPS * (group + 1), 1) if group < GROUPS - 1 else left
                    out.append(jnp.concatenate([own, jnp.where(is_right, after, before)], axis=1))
                return out

            first_row = starts[slot] + part * GROUPS

            def species_body(s, _, load=load, first_row=first_row):
                for group, tile in enumerate(load(s)):
                    state[s, first_row + group] = tile
                return 0

            lax.fori_loop(0, spec, species_body, 0)
            winds = load(spec)
            kinds = load(spec + 1)
            for group in range(GROUPS):
                speed[first_row + group] = winds[group] * inside
                matrix[0, first_row + group] = kinds[group]

    def coefficients(row, _):
        kind = matrix[0, row].astype(jnp.int32)
        wind = speed[row]
        for a in range(spec):
            stay = inside * (1.0 - 6.0 * diffusion[a]) - wind
            for s in range(spec):
                tab = table[a * spec + s]
                tiles = [
                    jnp.concatenate(
                        [
                            jnp.take_along_axis(tab, kind[x : x + 8, z : z + LANES], axis=0)
                            for z in range(0, wide, LANES)
                        ],
                        axis=1,
                    )
                    for x in range(0, all_x, 8)
                ]
                value = jnp.concatenate(tiles, axis=0) * inside
                matrix[a * spec + s, row] = value + stay if a == s else value
        return 0

    zero = jnp.zeros((all_x, wide), jnp.float32)

    def clear(row, _):
        for s in range(spec):
            other[s, row] = zero
        return 0

    lax.fori_loop(0, rows, clear, 0)
    for row in (*range(BLOCK), *range(rows - BLOCK, rows)):
        speed[row] = zero
        for s in range(spec):
            state[s, row] = zero
        for k in range(spec * spec):
            matrix[k, row] = zero

    lowest = jnp.where(at_y > 0, BLOCK, BLOCK + cells_y)
    highest = jnp.where(at_y < count_y - 1, rows - BLOCK, rows - BLOCK - cells_y)
    lax.fori_loop(lowest, highest, coefficients, 0)

    def step(index, source, target):
        low = jnp.maximum(BLOCK + index + 1, lowest)
        high = jnp.minimum(rows - BLOCK - 1 - index, highest)
        turns = (high - low + BLOCK - 1) // BLOCK
        start = jnp.where(high == highest, high - turns * BLOCK, low)

        def block_body(turn, _):
            base = start + turn * BLOCK
            tiles = [[source[s, base + i] for s in range(spec)] for i in range(-1, BLOCK + 1)]
            for i in range(BLOCK):
                row = base + i
                before, here, after = tiles[i : i + 3]
                wind = speed[row]
                for a in range(spec):
                    ahead = jnp.where(is_last, 0.0, pltpu.roll(here[a], all_x - 1, 0))
                    behind = jnp.where(is_first, 0.0, pltpu.roll(here[a], 1, 0))
                    beside = (before[a] + after[a]) + (ahead + behind)
                    beside = beside + (pltpu.roll(here[a], 1, 1) + pltpu.roll(here[a], wide - 1, 1))
                    mix = matrix[a * spec, row] * here[0]
                    for s in range(1, spec):
                        mix = mix + matrix[a * spec + s, row] * here[s]
                    target[a, row] = mix + wind * ahead + spread[a] * beside
            return 0

        lax.fori_loop(0, turns, block_body, 0)
        slot = jnp.int32(0)
        hit = jnp.int32(0)
        for j in range(snaps):
            slot = slot + jnp.where(plan[j] < index, 1, 0)
            hit = hit + jnp.where(plan[j] == index, 1, 0)

        @pl.when(hit > 0)
        def _():
            def keep(y, _):
                for flips in range(len(kept)):
                    tile = target[grp ^ flips, BLOCK + cells_y + y, :cells_x, :cells_z]
                    for x in range(cells_x):
                        kept[flips][x, y, pl.ds(slot, 1), :] = tile[x : x + 1]
                return 0

            lax.fori_loop(0, cells_y, keep, 0, unroll=4)

    spread = [inside * diffusion[a] for a in range(spec)]

    def two_steps(pair, _):
        step(2 * pair, state, other)
        step(2 * pair + 1, other, state)
        return 0

    lax.fori_loop(0, STEPS // 2, two_steps, 0)

    def leave(s, _):
        for y in range(cells_y):
            tile = state[s, BLOCK + cells_y + y, :cells_x, :cells_z]
            for x in range(cells_x):
                adjoint[s, x, y : y + 1, :] = tile[x : x + 1]
        return 0

    lax.fori_loop(0, spec, leave, 0)


def gram_kernel(x, given, basis, *refs):
    total, (out, chunks, held, sems) = refs[:given], refs[given:]
    count, rows, cells_z, modes = chunks.shape
    copies = fetch(
        [basis.at[0, x, pl.ds(i * rows, rows)] for i in range(count)] + list(total),
        [chunks.at[i] for i in range(count)] + [held],
        sems,
    )
    acc = None
    for i in range(count):
        copies[i].wait()
        chunk = chunks[i].reshape(rows * cells_z, modes)
        part = lax.dot_general(
            chunk, chunk, (((0,), (0,)), ((), ())), preferred_element_type=jnp.float32
        )
        acc = part if acc is None else acc + part
    if total:
        copies[-1].wait()
        acc = acc + held[...]
    out[...] = acc


def gram_part(x, basis, *total):
    _, _, cells_y, cells_z, modes = basis.shape
    chunks = 2
    size = 2 * cells_y * cells_z * modes
    return pl.pallas_call(
        functools.partial(gram_kernel, x, len(total)),
        out_shape=jax.ShapeDtypeStruct((modes, modes), jnp.float32),
        in_specs=anywhere(1 + len(total)),
        out_specs=whole(1)[0],
        scratch_shapes=[
            pltpu.VMEM((chunks, cells_y // chunks, cells_z, modes), jnp.bfloat16),
            pltpu.VMEM((modes, modes), jnp.float32),
            pltpu.SemaphoreType.DMA((chunks + 1,)),
        ],
        compiler_params=pltpu.CompilerParams(vmem_limit_bytes=BASIS_VMEM),
        cost_estimate=pl.CostEstimate(
            flops=2 * cells_y * cells_z * modes * modes, bytes_accessed=3 * size, transcendentals=0
        ),
        name="gram",
    )(basis, *total)


def rows_of(basis, flips, cells_z):
    zone = (lax.axis_index("grp") ^ flips) * cells_z
    return [
        basis.at[0, x, :, pl.ds(pl.multiple_of(zone, LANES), cells_z)]
        for x in range(basis.shape[1])
    ]


def multiply(held, rows, waits, acc):
    cells_x, cells_y, snaps, cells_z = held.shape
    for x in range(cells_x):
        values = held[x]
        high = values.astype(jnp.bfloat16).astype(jnp.float32)
        left = jnp.concatenate([high, values - high], axis=1).astype(jnp.bfloat16)
        waits[x].wait()
        for y in range(0, cells_y, 2):
            more = jnp.dot(
                jnp.concatenate([left[y], left[y + 1]], axis=1),
                rows[x, y : y + 2].reshape(2 * cells_z, rows.shape[-1]),
                preferred_element_type=jnp.float32,
            )
            acc = more if acc is None else acc + more
    return acc


def first_kernel(
    gram_x, part, basis, gram, out_high, out_low, out_gram, held, rows, chunks, total, sems
):
    cells_x, cells_y, snaps, cells_z = held.shape
    modes = rows.shape[-1]
    sources = [part, *rows_of(basis, 0, cells_z)]
    targets = [held, *(rows.at[x] for x in range(cells_x))]
    sources += [basis.at[0, x] for x in gram_x] + [gram]
    targets += [chunks.at[i] for i in range(len(gram_x))] + [total]
    start_gram = 1 + cells_x
    copies = fetch(sources, targets, sems)
    copies[0].wait()
    acc = multiply(held, rows, copies[1:], None)
    out_high[...] = acc[:snaps]
    out_low[...] = acc[snaps:]
    acc = None
    for i in range(len(gram_x)):
        copies[start_gram + i].wait()
        chunk = chunks[i].reshape(-1, modes)
        more = lax.dot_general(
            chunk, chunk, (((0,), (0,)), ((), ())), preferred_element_type=jnp.float32
        )
        acc = more if acc is None else acc + more
    for copy in copies[start_gram + len(gram_x) :]:
        copy.wait()
    out_gram[...] = total[...] if acc is None else acc + total[...]


def product_kernel(flips, *refs):
    count = len(flips)
    parts, refs = refs[:count], refs[count:]
    basis, high, low, out_high, out_low, held, rows, sums, sems = refs
    _, cells_x, cells_y, snaps, cells_z = held.shape
    sources, targets = [], []
    for i in range(count):
        sources += [parts[i], *rows_of(basis, flips[i], cells_z)]
        targets += [held.at[i], *(rows.at[i, x] for x in range(cells_x))]
    copies = fetch([*sources, high, low], [*targets, sums.at[0], sums.at[1]], sems)
    acc = None
    for i in range(count):
        start = i * (cells_x + 1)
        copies[start].wait()
        acc = multiply(held.at[i], rows.at[i], copies[start + 1 :], acc)
    copies[-2].wait()
    copies[-1].wait()
    out_high[...] = acc[:snaps] + sums[0]
    out_low[...] = acc[snaps:] + sums[1]


def first_product(part, basis, gram, gram_x):
    cells_x, cells_y, snaps, cells_z = part.shape
    modes = basis.shape[-1]
    size = 2 * cells_x * cells_y * cells_z * modes
    out = jax.ShapeDtypeStruct((snaps, modes), jnp.float32)
    rows = (cells_x, cells_y, cells_z, modes)
    return pl.pallas_call(
        functools.partial(first_kernel, gram_x),
        out_shape=[out, out, jax.ShapeDtypeStruct(gram.shape, jnp.float32)],
        in_specs=anywhere(3),
        out_specs=whole(3),
        scratch_shapes=[
            pltpu.VMEM(part.shape, jnp.float32),
            pltpu.VMEM(rows, jnp.bfloat16),
            pltpu.VMEM((max(len(gram_x), 1), *basis.shape[2:]), jnp.bfloat16),
            pltpu.VMEM(gram.shape, jnp.float32),
            pltpu.SemaphoreType.DMA((2 + cells_x + len(gram_x),)),
        ],
        compiler_params=pltpu.CompilerParams(vmem_limit_bytes=BASIS_VMEM),
        cost_estimate=pl.CostEstimate(
            flops=2 * snaps * size, bytes_accessed=4 * size, transcendentals=0
        ),
        name="first_product",
    )(part, basis, gram)


def product(flips, parts, basis, high, low):
    cells_x, cells_y, snaps, cells_z = parts[0].shape
    modes, count = basis.shape[-1], len(flips)
    size = 2 * count * cells_x * cells_y * cells_z * modes
    out = jax.ShapeDtypeStruct((snaps, modes), jnp.float32)
    return pl.pallas_call(
        functools.partial(product_kernel, flips),
        out_shape=(out, out),
        in_specs=anywhere(3 + count),
        out_specs=tuple(whole(2)),
        scratch_shapes=[
            pltpu.VMEM((count, *parts[0].shape), jnp.float32),
            pltpu.VMEM((count, cells_x, cells_y, cells_z, modes), jnp.bfloat16),
            pltpu.VMEM((2, snaps, modes), jnp.float32),
            pltpu.SemaphoreType.DMA((count * (cells_x + 1) + 2,)),
        ],
        compiler_params=pltpu.CompilerParams(vmem_limit_bytes=BASIS_VMEM),
        cost_estimate=pl.CostEstimate(
            flops=2 * snaps * size, bytes_accessed=2 * size, transcendentals=0
        ),
        name="product",
    )(*parts, basis, high, low)


def body(terminal, diffusion, velocity, material, rates, stoich, plan, basis):
    spec, cells_x, cells_y, cells_z = terminal.shape
    snaps, modes = plan.shape[0], basis.shape[-1]
    count_grp, count_x = lax.axis_size("grp"), lax.axis_size("gx")
    fields, all_x = spec + 2, cells_x * count_x
    wide, depth = cells_z + LANES, 3 * cells_y + 2 * BLOCK

    own = pl.pallas_call(
        pack_kernel,
        out_shape=jax.ShapeDtypeStruct((fields, cells_y, cells_x, cells_z), jnp.float32),
        in_specs=whole(3),
        out_specs=whole(1)[0],
        name="pack",
    )(terminal, velocity, material)
    blocks = [own]
    for shift in range(1, count_x):
        blocks.append(
            lax.ppermute(own, "gx", [(i, (i - shift) % count_x) for i in range(count_x)])
        )
    from_a = [lax.ppermute(own, "gy", pairs("gy", 0))]
    from_b = [lax.ppermute(own, "gy", pairs("gy", 1))]
    gram = gram_part(0, basis)
    *blocks, gram = lax.optimization_barrier((*blocks, gram))
    from_a += [lax.ppermute(b, "gy", pairs("gy", 0)) for b in blocks[1:]]
    from_b += [lax.ppermute(b, "gy", pairs("gy", 1)) for b in blocks[1:]]
    gram = gram_part(1, basis, gram)
    blocks = blocks + from_a + from_b
    *blocks, gram = lax.optimization_barrier((*blocks, gram))
    packed = jax.ShapeDtypeStruct((fields, 3 * cells_y // GROUPS, all_x, LANES), jnp.float32)
    held = (len(blocks), fields, cells_y, cells_x, cells_z)
    edge_a, edge_b = pl.pallas_call(
        functools.partial(edges_kernel, count_x),
        out_shape=(packed, packed),
        in_specs=anywhere(len(blocks)),
        out_specs=tuple(whole(2)),
        scratch_shapes=[pltpu.VMEM(held, jnp.float32), pltpu.SemaphoreType.DMA((len(blocks),))],
        compiler_params=vmem(held, packed.shape, packed.shape),
        name="edges",
    )(*blocks)
    side_a = lax.ppermute(edge_a, "grp", pairs("grp", 0))
    side_b = lax.ppermute(edge_b, "grp", pairs("grp", 1))
    gram = gram_part(2, basis, gram)
    side_a, side_b, gram = lax.optimization_barrier((side_a, side_b, gram))

    part = jax.ShapeDtypeStruct((cells_x, cells_y, snaps, cells_z), jnp.float32)
    room = (depth, all_x, wide)
    shapes = [(spec, *room), (spec, *room), (spec * spec, *room), room, held, (2, *packed.shape)]
    final, *kept = pl.pallas_call(
        functools.partial(steps_kernel, count_x),
        out_shape=[jax.ShapeDtypeStruct(terminal.shape, jnp.float32)] + [part] * count_grp,
        in_specs=scalars(3) + whole(1) + anywhere(len(blocks) + 2),
        out_specs=whole(1 + count_grp),
        scratch_shapes=[pltpu.VMEM(shape, jnp.float32) for shape in shapes]
        + [pltpu.SemaphoreType.DMA((len(blocks) + 2,))],
        compiler_params=vmem(*shapes, terminal.shape, (count_grp, *part.shape)),
        name="steps",
    )(plan, diffusion, stoich, rates, *blocks, side_a, side_b)

    order = sorted(range(1, count_grp), key=lambda flips: -flips)
    moved = {flips: exchange(kept[flips], "grp", flips) for flips in order}
    high, low, gram = first_product(kept[0], basis, gram, tuple(range(3, cells_x)))
    for flips in ((1,), tuple(range(2, count_grp))):
        high, low = product(flips, [moved[f] for f in flips], basis, high, low)

    first = sum_all(high)
    taken = jnp.dot(
        first.astype(jnp.bfloat16).astype(jnp.float32), gram, precision=lax.Precision.HIGHEST
    )
    second = sum_all(high + low - taken)
    return (first + second, final)


def solution(mesh):
    in_specs = (
        P(None, "gx", "gy", "grp"),
        P(),
        P("gx", "gy", "grp"),
        P("gx", "gy", "grp"),
        P(),
        P(),
        P(),
        P("grp", "gx", "gy", None, None),
    )
    out_specs = (P(), P(None, "gx", "gy", "grp"))
    return jax.shard_map(body, mesh=mesh, in_specs=in_specs, out_specs=out_specs, check_vma=False)
```

```python
import functools
import math

import jax
import jax.numpy as jnp
from jax import lax
from jax.experimental import pallas as pl
from jax.experimental.pallas import tpu as pltpu
from jax.sharding import PartitionSpec as P

STEPS = 16
LANES = 128
GROUPS = LANES // STEPS
BLOCK = 8
MIB = 1024 * 1024
BASIS_VMEM = 50 * MIB


def pairs(axis, first):
    count = lax.axis_size(axis)
    lower = range(first, count - 1, 2)
    return [(i, i + 1) for i in lower] + [(i + 1, i) for i in lower]


def exchange(value, axis, flips):
    count = lax.axis_size(axis)
    return lax.ppermute(value, axis, [(i, i ^ flips) for i in range(count)])


def copies_over(value, axis):
    count = lax.axis_size(axis)
    while count > 4:
        count //= 2
        value = value + exchange(value, axis, count)
    return [value] + [exchange(value, axis, flips) for flips in range(1, count)]


def add_up(values):
    while len(values) > 1:
        values = [a + b for a, b in zip(values[::2], values[1::2])]
    return values[0]


def sum_over(value, axis):
    return add_up(copies_over(value, axis))


def whole(count):
    return [pl.BlockSpec(memory_space=pltpu.VMEM)] * count


def scalars(count):
    return [pl.BlockSpec(memory_space=pltpu.SMEM)] * count


def anywhere(count):
    return [pl.BlockSpec(memory_space=pl.ANY)] * count


def vmem(*shapes):
    return pltpu.CompilerParams(vmem_limit_bytes=4 * sum(map(math.prod, shapes)) + 6 * MIB)


def fetch(sources, targets, sems):
    copies = [
        pltpu.make_async_copy(source, target, sems.at[i])
        for i, (source, target) in enumerate(zip(sources, targets))
    ]
    for copy in copies:
        copy.start()
    return copies


def pack_kernel(terminal, velocity, material, out):
    spec, cells_x, cells_y, cells_z = terminal.shape
    for x in range(cells_x):
        for s in range(spec):
            out[s, :, x, :] = terminal[s, x]
        out[spec, :, x, :] = velocity[x]
        out[spec + 1, :, x, :] = material[x].astype(jnp.float32)


def edges_kernel(blocks_x, *refs):
    given, (out_a, out_b, blocks, sems) = refs[:-4], refs[-4:]
    blocks = [blocks.at[i] for i in range(len(given))]
    copies = fetch(given, blocks, sems)
    fields, cells_y, cells_x, cells_z = blocks[0].shape
    per_block = cells_y // GROUPS
    even = lax.axis_index("grp") % 2 == 0
    for copy in copies:
        copy.wait()
    place = lax.broadcasted_iota(jnp.int32, (blocks_x * cells_x, LANES), 1) // STEPS

    def field_body(field, _):
        for slot in range(len(blocks) // blocks_x):
            mine = blocks[slot * blocks_x : (slot + 1) * blocks_x]
            for part in range(per_block):
                top = bottom = None
                for group in range(GROUPS):
                    row = part * GROUPS + group
                    last = jnp.concatenate(
                        [b[field, row, :, cells_z - LANES :] for b in mine], axis=0
                    )
                    start = jnp.concatenate([b[field, row, :, :LANES] for b in mine], axis=0)
                    high = pltpu.roll(last, (STEPS * (group + 1)) % LANES, 1)
                    low = pltpu.roll(start, STEPS * group, 1) if group else start
                    top = high if top is None else jnp.where(place == group, high, top)
                    bottom = low if bottom is None else jnp.where(place == group, low, bottom)
                out_a[field, slot * per_block + part] = jnp.where(even, top, bottom)
                out_b[field, slot * per_block + part] = jnp.where(even, bottom, top)
        return 0

    lax.fori_loop(0, fields, field_body, 0)


def steps_kernel(blocks_x, plan, diffusion, stoich, rates, *refs):
    count_blocks = 3 * blocks_x
    given = refs[: count_blocks + 2]
    adjoint = refs[count_blocks + 2]
    kept = refs[count_blocks + 3 : -7]
    state, other, matrix, speed, blocks, sides, sems = refs[-7:]
    blocks = [blocks.at[i] for i in range(count_blocks)]
    side_a, side_b = sides.at[0], sides.at[1]
    copies = fetch(given, blocks + [side_a, side_b], sems)
    spec, rows, all_x, wide = state.shape
    _, cells_y, cells_x, cells_z = blocks[0].shape
    grp, at_x, at_y = (lax.axis_index(axis) for axis in ("grp", "gx", "gy"))
    count_grp, count_y = lax.axis_size("grp"), lax.axis_size("gy")
    snaps = kept[0].shape[2]
    per_block = cells_y // GROUPS
    even_z = grp % 2 == 0
    even_y = at_y % 2 == 0
    starts = (
        BLOCK + cells_y,
        BLOCK + jnp.where(even_y, 2 * cells_y, 0),
        BLOCK + jnp.where(even_y, 0, 2 * cells_y),
    )
    lane = lax.broadcasted_iota(jnp.int32, (all_x, LANES), 1)
    is_right = lane < LANES // 2
    has_right = grp < count_grp - 1
    has_left = grp > 0
    beyond = jnp.where(
        is_right, jnp.where(has_right, 1.0, 0.0), jnp.where(has_left, 1.0, 0.0)
    ).astype(jnp.float32)
    inside = jnp.concatenate(
        [jnp.ones((all_x, LANES), jnp.float32)] * (cells_z // LANES) + [beyond], axis=1
    )
    row_x = lax.broadcasted_iota(jnp.int32, (all_x, wide), 0)
    place_x = (row_x + at_x * cells_x) % all_x
    is_first = place_x == 0
    is_last = place_x == all_x - 1

    columns = [
        jnp.broadcast_to(rates[:, r : r + 1], (rates.shape[0], LANES)) for r in range(rates.shape[1])
    ]
    table = [
        sum(
            columns[r] * stoich[r, s].astype(jnp.float32) for r in range(a, rates.shape[1], spec)
        )
        for a in range(spec)
        for s in range(spec)
    ]
    for copy in copies:
        copy.wait()
    for slot in range(3):
        mine = blocks[slot * blocks_x : (slot + 1) * blocks_x]
        for part in range(per_block):

            def load(field, part=part, slot=slot, mine=mine):
                packed_a = side_a[field, slot * per_block + part]
                packed_b = side_b[field, slot * per_block + part]
                right = jnp.where(even_z, packed_a, packed_b)
                left = jnp.where(even_z, packed_b, packed_a)
                out = []
                for group in range(GROUPS):
                    row = part * GROUPS + group
                    own = jnp.concatenate([b[field, row] for b in mine], axis=0)
                    after = pltpu.roll(right, (LANES - STEPS * group) % LANES, 1) if group else right
                    before = pltpu.roll(left, LANES - STEPS * (group + 1), 1) if group < GROUPS - 1 else left
                    out.append(jnp.concatenate([own, jnp.where(is_right, after, before)], axis=1))
                return out

            first_row = starts[slot] + part * GROUPS

            def species_body(s, _, load=load, first_row=first_row):
                for group, tile in enumerate(load(s)):
                    state[s, first_row + group] = tile
                return 0

            lax.fori_loop(0, spec, species_body, 0)
            winds = load(spec)
            kinds = load(spec + 1)
            for group in range(GROUPS):
                speed[first_row + group] = winds[group] * inside
                matrix[0, first_row + group] = kinds[group]

    def coefficients(row, _):
        kind = matrix[0, row].astype(jnp.int32)
        wind = speed[row]
        for a in range(spec):
            stay = inside * (1.0 - 6.0 * diffusion[a]) - wind
            for s in range(spec):
                tab = table[a * spec + s]
                tiles = [
                    jnp.concatenate(
                        [
                            jnp.take_along_axis(tab, kind[x : x + 8, z : z + LANES], axis=0)
                            for z in range(0, wide, LANES)
                        ],
                        axis=1,
                    )
                    for x in range(0, all_x, 8)
                ]
                value = jnp.concatenate(tiles, axis=0) * inside
                matrix[a * spec + s, row] = value + stay if a == s else value
        return 0

    zero = jnp.zeros((all_x, wide), jnp.float32)

    def clear(row, _):
        for s in range(spec):
            other[s, row] = zero
        return 0

    lax.fori_loop(0, rows, clear, 0)
    for row in (*range(BLOCK), *range(rows - BLOCK, rows)):
        speed[row] = zero
        for s in range(spec):
            state[s, row] = zero
        for k in range(spec * spec):
            matrix[k, row] = zero

    lowest = jnp.where(at_y > 0, BLOCK, BLOCK + cells_y)
    highest = jnp.where(at_y < count_y - 1, rows - BLOCK, rows - BLOCK - cells_y)
    lax.fori_loop(lowest, highest, coefficients, 0)

    def step(index, source, target):
        low = jnp.maximum(BLOCK + index + 1, lowest)
        high = jnp.minimum(rows - BLOCK - 1 - index, highest)
        turns = (high - low + BLOCK - 1) // BLOCK
        start = jnp.where(high == highest, high - turns * BLOCK, low)

        def block_body(turn, _):
            base = start + turn * BLOCK
            tiles = [[source[s, base + i] for s in range(spec)] for i in range(-1, BLOCK + 1)]
            for i in range(BLOCK):
                row = base + i
                before, here, after = tiles[i : i + 3]
                wind = speed[row]
                for a in range(spec):
                    ahead = jnp.where(is_last, 0.0, pltpu.roll(here[a], all_x - 1, 0))
                    behind = jnp.where(is_first, 0.0, pltpu.roll(here[a], 1, 0))
                    beside = (before[a] + after[a]) + (ahead + behind)
                    beside = beside + (pltpu.roll(here[a], 1, 1) + pltpu.roll(here[a], wide - 1, 1))
                    mix = matrix[a * spec, row] * here[0]
                    for s in range(1, spec):
                        mix = mix + matrix[a * spec + s, row] * here[s]
                    target[a, row] = mix + wind * ahead + spread[a] * beside
            return 0

        lax.fori_loop(0, turns, block_body, 0)
        slot = jnp.int32(0)
        hit = jnp.int32(0)
        for j in range(snaps):
            slot = slot + jnp.where(plan[j] < index, 1, 0)
            hit = hit + jnp.where(plan[j] == index, 1, 0)

        @pl.when(hit > 0)
        def _():
            def keep(y, _):
                for flips in range(len(kept)):
                    tile = target[grp ^ flips, BLOCK + cells_y + y, :cells_x, :cells_z]
                    for x in range(cells_x):
                        kept[flips][x, y, pl.ds(slot, 1), :] = tile[x : x + 1]
                return 0

            lax.fori_loop(0, cells_y, keep, 0, unroll=4)

    spread = [inside * diffusion[a] for a in range(spec)]

    def two_steps(pair, _):
        step(2 * pair, state, other)
        step(2 * pair + 1, other, state)
        return 0

    lax.fori_loop(0, STEPS // 2, two_steps, 0)

    def leave(s, _):
        for y in range(cells_y):
            tile = state[s, BLOCK + cells_y + y, :cells_x, :cells_z]
            for x in range(cells_x):
                adjoint[s, x, y : y + 1, :] = tile[x : x + 1]
        return 0

    lax.fori_loop(0, spec, leave, 0)


def gram_kernel(places, given, basis, *refs):
    total, (out, chunks, held, sems) = refs[:given], refs[given:]
    count, rows, cells_z, modes = chunks.shape
    halves = count // len(places)
    copies = fetch(
        [basis.at[0, x, pl.ds(i * rows, rows)] for x in places for i in range(halves)]
        + list(total),
        [chunks.at[i] for i in range(count)] + [held],
        sems,
    )
    acc = None
    for i in range(count):
        copies[i].wait()
        chunk = chunks[i].reshape(rows * cells_z, modes)
        part = lax.dot_general(
            chunk, chunk, (((0,), (0,)), ((), ())), preferred_element_type=jnp.float32
        )
        acc = part if acc is None else acc + part
    if total:
        copies[-1].wait()
        acc = acc + held[...]
    out[...] = acc


def gram_part(places, basis, *total):
    _, _, cells_y, cells_z, modes = basis.shape
    chunks = 2 * len(places)
    size = 2 * len(places) * cells_y * cells_z * modes
    return pl.pallas_call(
        functools.partial(gram_kernel, places, len(total)),
        out_shape=jax.ShapeDtypeStruct((modes, modes), jnp.float32),
        in_specs=anywhere(1 + len(total)),
        out_specs=whole(1)[0],
        scratch_shapes=[
            pltpu.VMEM((chunks, cells_y // 2, cells_z, modes), jnp.bfloat16),
            pltpu.VMEM((modes, modes), jnp.float32),
            pltpu.SemaphoreType.DMA((chunks + 1,)),
        ],
        compiler_params=pltpu.CompilerParams(vmem_limit_bytes=BASIS_VMEM),
        cost_estimate=pl.CostEstimate(
            flops=size * modes, bytes_accessed=3 * size, transcendentals=0
        ),
        name="gram",
    )(basis, *total)


def rows_of(basis, flips, cells_z):
    zone = (lax.axis_index("grp") ^ flips) * cells_z
    return [
        basis.at[0, x, :, pl.ds(pl.multiple_of(zone, LANES), cells_z)]
        for x in range(basis.shape[1])
    ]


def multiply(held, rows, waits, acc):
    cells_x, cells_y, snaps, cells_z = held.shape
    for x in range(cells_x):
        values = held[x]
        high = values.astype(jnp.bfloat16).astype(jnp.float32)
        left = jnp.concatenate([high, values - high], axis=1).astype(jnp.bfloat16)
        waits[x].wait()
        for y in range(0, cells_y, 2):
            more = jnp.dot(
                jnp.concatenate([left[y], left[y + 1]], axis=1),
                rows[x, y : y + 2].reshape(2 * cells_z, rows.shape[-1]),
                preferred_element_type=jnp.float32,
            )
            acc = more if acc is None else acc + more
    return acc


def product_kernel(flips, given, *refs):
    count = len(flips)
    parts, basis, total = refs[:count], refs[count], refs[count + 1 : count + 1 + given]
    out, held, rows, sums, sems = refs[count + 1 + given :]
    cells_x, cells_z = held.shape[1], held.shape[-1]
    sources, targets = [], []
    for i in range(count):
        sources += [parts[i], *rows_of(basis, flips[i], cells_z)]
        targets += [held.at[i], *(rows.at[i, x] for x in range(cells_x))]
    copies = fetch([*sources, *total], [*targets, sums], sems)
    acc = None
    for i in range(count):
        start = i * (cells_x + 1)
        copies[start].wait()
        acc = multiply(held.at[i], rows.at[i], copies[start + 1 :], acc)
    if total:
        copies[-1].wait()
        acc = acc + sums[...]
    out[...] = acc


def product(flips, parts, basis, *total):
    cells_x, cells_y, snaps, cells_z = parts[0].shape
    modes, count = basis.shape[-1], len(flips)
    size = 2 * count * cells_x * cells_y * cells_z * modes
    return pl.pallas_call(
        functools.partial(product_kernel, flips, len(total)),
        out_shape=jax.ShapeDtypeStruct((2 * snaps, modes), jnp.float32),
        in_specs=anywhere(1 + count + len(total)),
        out_specs=whole(1)[0],
        scratch_shapes=[
            pltpu.VMEM((count, *parts[0].shape), jnp.float32),
            pltpu.VMEM((count, cells_x, cells_y, cells_z, modes), jnp.bfloat16),
            pltpu.VMEM((2 * snaps, modes), jnp.float32),
            pltpu.SemaphoreType.DMA((count * (cells_x + 1) + 1,)),
        ],
        compiler_params=pltpu.CompilerParams(vmem_limit_bytes=BASIS_VMEM),
        cost_estimate=pl.CostEstimate(
            flops=2 * snaps * size, bytes_accessed=2 * size, transcendentals=0
        ),
        name="product",
    )(*parts, basis, *total)


def body(terminal, diffusion, velocity, material, rates, stoich, plan, basis):
    spec, cells_x, cells_y, cells_z = terminal.shape
    snaps, modes = plan.shape[0], basis.shape[-1]
    count_grp, count_x = lax.axis_size("grp"), lax.axis_size("gx")
    fields, all_x = spec + 2, cells_x * count_x
    wide, depth = cells_z + LANES, 3 * cells_y + 2 * BLOCK

    own = pl.pallas_call(
        pack_kernel,
        out_shape=jax.ShapeDtypeStruct((fields, cells_y, cells_x, cells_z), jnp.float32),
        in_specs=whole(3),
        out_specs=whole(1)[0],
        name="pack",
    )(terminal, velocity, material)
    blocks = [own]
    for shift in range(1, count_x):
        blocks.append(
            lax.ppermute(own, "gx", [(i, (i - shift) % count_x) for i in range(count_x)])
        )
    from_a = [lax.ppermute(own, "gy", pairs("gy", 0))]
    from_b = [lax.ppermute(own, "gy", pairs("gy", 1))]
    gram = gram_part((0,), basis)
    *blocks, gram = lax.optimization_barrier((*blocks, gram))
    from_a += [lax.ppermute(b, "gy", pairs("gy", 0)) for b in blocks[1:]]
    from_b += [lax.ppermute(b, "gy", pairs("gy", 1)) for b in blocks[1:]]
    gram = gram_part(tuple(range(1, cells_x - 1)), basis, gram)
    blocks = blocks + from_a + from_b
    *blocks, gram = lax.optimization_barrier((*blocks, gram))
    packed = jax.ShapeDtypeStruct((fields, 3 * cells_y // GROUPS, all_x, LANES), jnp.float32)
    held = (len(blocks), fields, cells_y, cells_x, cells_z)
    edge_a, edge_b = pl.pallas_call(
        functools.partial(edges_kernel, count_x),
        out_shape=(packed, packed),
        in_specs=anywhere(len(blocks)),
        out_specs=tuple(whole(2)),
        scratch_shapes=[pltpu.VMEM(held, jnp.float32), pltpu.SemaphoreType.DMA((len(blocks),))],
        compiler_params=vmem(held, packed.shape, packed.shape),
        name="edges",
    )(*blocks)
    side_a = lax.ppermute(edge_a, "grp", pairs("grp", 0))
    side_b = lax.ppermute(edge_b, "grp", pairs("grp", 1))
    gram = gram_part((cells_x - 1,), basis, gram)
    side_a, side_b, gram = lax.optimization_barrier((side_a, side_b, gram))
    grams = copies_over(gram, "grp")

    part = jax.ShapeDtypeStruct((cells_x, cells_y, snaps, cells_z), jnp.float32)
    room = (depth, all_x, wide)
    shapes = [(spec, *room), (spec, *room), (spec * spec, *room), room, held, (2, *packed.shape)]
    final, *kept = pl.pallas_call(
        functools.partial(steps_kernel, count_x),
        out_shape=[jax.ShapeDtypeStruct(terminal.shape, jnp.float32)] + [part] * count_grp,
        in_specs=scalars(3) + whole(1) + anywhere(len(blocks) + 2),
        out_specs=whole(1 + count_grp),
        scratch_shapes=[pltpu.VMEM(shape, jnp.float32) for shape in shapes]
        + [pltpu.SemaphoreType.DMA((len(blocks) + 2,))],
        compiler_params=vmem(*shapes, terminal.shape, (count_grp, *part.shape)),
        cost_estimate=pl.CostEstimate(
            flops=0,
            bytes_accessed=2 * STEPS * spec * (spec + 2) * math.prod(room),
            transcendentals=0,
        ),
        name="steps",
    )(plan, diffusion, stoich, rates, *blocks, side_a, side_b)

    order = sorted(range(1, count_grp), key=lambda flips: -flips)
    moved = {flips: exchange(kept[flips], "grp", flips) for flips in order}
    mine, *grams = lax.optimization_barrier((kept[0], *grams))
    mine, gram = lax.optimization_barrier((mine, add_up(grams)))
    grams = copies_over(gram, "gy")
    total = product((0,), [mine], basis)
    for flips in ((1,), tuple(range(2, count_grp))):
        total = product(flips, [moved[f] for f in flips], basis, total)

    total = sum_over(total, "grp")
    total, *grams = lax.optimization_barrier((total, *grams))
    total = copies_over(total, "gy")
    high = add_up([part[:snaps] for part in total])
    low = add_up([part[snaps:] for part in total])
    first = sum_over(high, "gx")
    taken = jnp.dot(
        first.astype(jnp.bfloat16).astype(jnp.float32),
        add_up(grams),
        precision=lax.Precision.HIGHEST,
    )
    second = sum_over(high + low - taken, "gx")
    return (first + second, final)


def solution(mesh):
    in_specs = (
        P(None, "gx", "gy", "grp"),
        P(),
        P("gx", "gy", "grp"),
        P("gx", "gy", "grp"),
        P(),
        P(),
        P(),
        P("grp", "gx", "gy", None, None),
    )
    out_specs = (P(), P(None, "gx", "gy", "grp"))
    return jax.shard_map(body, mesh=mesh, in_specs=in_specs, out_specs=out_specs, check_vma=False)
```

```python
import functools
import math

import jax
import jax.numpy as jnp
from jax import lax
from jax.experimental import pallas as pl
from jax.experimental.pallas import tpu as pltpu
from jax.sharding import PartitionSpec as P

STEPS = 16
LANES = 128
GROUPS = LANES // STEPS
BLOCK = 8
ROWS = 4
MIB = 1024 * 1024
BASIS_VMEM = 50 * MIB


def pairs(axis, first):
    count = lax.axis_size(axis)
    lower = range(first, count - 1, 2)
    return [(i, i + 1) for i in lower] + [(i + 1, i) for i in lower]


def exchange(value, axis, flips):
    count = lax.axis_size(axis)
    return lax.ppermute(value, axis, [(i, i ^ flips) for i in range(count)])


def copies_over(value, axis):
    count = lax.axis_size(axis)
    while count > 4:
        count //= 2
        value = value + exchange(value, axis, count)
    return [value] + [exchange(value, axis, flips) for flips in range(1, count)]


def add_up(values):
    while len(values) > 1:
        values = [a + b for a, b in zip(values[::2], values[1::2])]
    return values[0]


def sum_over(value, axis):
    return add_up(copies_over(value, axis))


def whole(count):
    return [pl.BlockSpec(memory_space=pltpu.VMEM)] * count


def scalars(count):
    return [pl.BlockSpec(memory_space=pltpu.SMEM)] * count


def anywhere(count):
    return [pl.BlockSpec(memory_space=pl.ANY)] * count


def vmem(*shapes):
    return pltpu.CompilerParams(vmem_limit_bytes=4 * sum(map(math.prod, shapes)) + 6 * MIB)


def fetch(sources, targets, sems):
    copies = [
        pltpu.make_async_copy(source, target, sems.at[i])
        for i, (source, target) in enumerate(zip(sources, targets))
    ]
    for copy in copies:
        copy.start()
    return copies


def pack_kernel(terminal, velocity, material, out):
    spec, cells_x, cells_y, cells_z = terminal.shape
    for x in range(cells_x):
        for s in range(spec):
            out[s, :, x, :] = terminal[s, x]
        out[spec, :, x, :] = velocity[x]
        out[spec + 1, :, x, :] = material[x].astype(jnp.float32)


def edges_kernel(blocks_x, *refs):
    given, (out_a, out_b, blocks, sems) = refs[:-4], refs[-4:]
    blocks = [blocks.at[i] for i in range(len(given))]
    copies = fetch(given, blocks, sems)
    fields, cells_y, cells_x, cells_z = blocks[0].shape
    per_block = cells_y // GROUPS
    even = lax.axis_index("grp") % 2 == 0
    for copy in copies:
        copy.wait()
    place = lax.broadcasted_iota(jnp.int32, (blocks_x * cells_x, LANES), 1) // STEPS

    def field_body(field, _):
        for slot in range(len(blocks) // blocks_x):
            mine = blocks[slot * blocks_x : (slot + 1) * blocks_x]
            for part in range(per_block):
                top = bottom = None
                for group in range(GROUPS):
                    row = part * GROUPS + group
                    last = jnp.concatenate(
                        [b[field, row, :, cells_z - LANES :] for b in mine], axis=0
                    )
                    start = jnp.concatenate([b[field, row, :, :LANES] for b in mine], axis=0)
                    high = pltpu.roll(last, (STEPS * (group + 1)) % LANES, 1)
                    low = pltpu.roll(start, STEPS * group, 1) if group else start
                    top = high if top is None else jnp.where(place == group, high, top)
                    bottom = low if bottom is None else jnp.where(place == group, low, bottom)
                out_a[field, slot * per_block + part] = jnp.where(even, top, bottom)
                out_b[field, slot * per_block + part] = jnp.where(even, bottom, top)
        return 0

    lax.fori_loop(0, fields, field_body, 0)


def steps_kernel(blocks_x, plan, diffusion, stoich, rates, *refs):
    count_blocks = 3 * blocks_x
    given = refs[: count_blocks + 2]
    adjoint = refs[count_blocks + 2]
    kept = refs[count_blocks + 3 : -7]
    state, other, matrix, speed, blocks, sides, sems = refs[-7:]
    blocks = [blocks.at[i] for i in range(count_blocks)]
    side_a, side_b = sides.at[0], sides.at[1]
    copies = fetch(given, blocks + [side_a, side_b], sems)
    spec, rows, all_x, wide = state.shape
    _, cells_y, cells_x, cells_z = blocks[0].shape
    grp, at_x, at_y = (lax.axis_index(axis) for axis in ("grp", "gx", "gy"))
    count_grp, count_y = lax.axis_size("grp"), lax.axis_size("gy")
    snaps = kept[0].shape[2]
    per_block = cells_y // GROUPS
    even_z = grp % 2 == 0
    even_y = at_y % 2 == 0
    starts = (
        BLOCK + cells_y,
        BLOCK + jnp.where(even_y, 2 * cells_y, 0),
        BLOCK + jnp.where(even_y, 0, 2 * cells_y),
    )
    lane = lax.broadcasted_iota(jnp.int32, (all_x, LANES), 1)
    is_right = lane < LANES // 2
    has_right = grp < count_grp - 1
    has_left = grp > 0
    beyond = jnp.where(
        is_right, jnp.where(has_right, 1.0, 0.0), jnp.where(has_left, 1.0, 0.0)
    ).astype(jnp.float32)
    inside = jnp.concatenate(
        [jnp.ones((all_x, LANES), jnp.float32)] * (cells_z // LANES) + [beyond], axis=1
    )
    row_x = lax.broadcasted_iota(jnp.int32, (all_x, wide), 0)
    place_x = (row_x + at_x * cells_x) % all_x
    is_first = place_x == 0
    is_last = place_x == all_x - 1

    columns = [
        jnp.broadcast_to(rates[:, r : r + 1], (rates.shape[0], LANES)) for r in range(rates.shape[1])
    ]
    table = [
        sum(
            columns[r] * stoich[r, s].astype(jnp.float32) for r in range(a, rates.shape[1], spec)
        )
        for a in range(spec)
        for s in range(spec)
    ]
    for copy in copies:
        copy.wait()
    for slot in range(3):
        mine = blocks[slot * blocks_x : (slot + 1) * blocks_x]
        for part in range(per_block):

            def load(field, part=part, slot=slot, mine=mine):
                packed_a = side_a[field, slot * per_block + part]
                packed_b = side_b[field, slot * per_block + part]
                right = jnp.where(even_z, packed_a, packed_b)
                left = jnp.where(even_z, packed_b, packed_a)
                out = []
                for group in range(GROUPS):
                    row = part * GROUPS + group
                    own = jnp.concatenate([b[field, row] for b in mine], axis=0)
                    after = pltpu.roll(right, (LANES - STEPS * group) % LANES, 1) if group else right
                    before = pltpu.roll(left, LANES - STEPS * (group + 1), 1) if group < GROUPS - 1 else left
                    out.append(jnp.concatenate([own, jnp.where(is_right, after, before)], axis=1))
                return out

            first_row = starts[slot] + part * GROUPS

            def species_body(s, _, load=load, first_row=first_row):
                for group, tile in enumerate(load(s)):
                    state[s, first_row + group] = tile
                return 0

            lax.fori_loop(0, spec, species_body, 0)
            winds = load(spec)
            kinds = load(spec + 1)
            for group in range(GROUPS):
                speed[first_row + group] = winds[group] * inside
                matrix[0, first_row + group] = kinds[group]

    def coefficients(turn, _):
        for i in range(ROWS):
            row_coefficients(lowest + turn * ROWS + i)
        return 0

    def row_coefficients(row):
        kind = matrix[0, row].astype(jnp.int32)
        wind = speed[row]
        for a in range(spec):
            stay = inside * (1.0 - 6.0 * diffusion[a]) - wind
            for s in range(spec):
                tab = table[a * spec + s]
                tiles = [
                    jnp.concatenate(
                        [
                            jnp.take_along_axis(tab, kind[x : x + 8, z : z + LANES], axis=0)
                            for z in range(0, wide, LANES)
                        ],
                        axis=1,
                    )
                    for x in range(0, all_x, 8)
                ]
                value = jnp.concatenate(tiles, axis=0) * inside
                matrix[a * spec + s, row] = value + stay if a == s else value

    zero = jnp.zeros((all_x, wide), jnp.float32)

    def clear(row, _):
        for s in range(spec):
            other[s, row] = zero
        return 0

    lax.fori_loop(0, rows, clear, 0)
    for row in (*range(BLOCK), *range(rows - BLOCK, rows)):
        speed[row] = zero
        for s in range(spec):
            state[s, row] = zero
        for k in range(spec * spec):
            matrix[k, row] = zero

    lowest = jnp.where(at_y > 0, BLOCK, BLOCK + cells_y)
    highest = jnp.where(at_y < count_y - 1, rows - BLOCK, rows - BLOCK - cells_y)
    lax.fori_loop(0, (highest - lowest) // ROWS, coefficients, 0)

    def step(index, source, target):
        low = jnp.maximum(BLOCK + index + 1, lowest)
        high = jnp.minimum(rows - BLOCK - 1 - index, highest)
        turns = (high - low + BLOCK - 1) // BLOCK
        start = jnp.where(high == highest, high - turns * BLOCK, low)

        def block_body(turn, _):
            base = start + turn * BLOCK
            tiles = [[source[s, base + i] for s in range(spec)] for i in range(-1, BLOCK + 1)]
            for i in range(BLOCK):
                row = base + i
                before, here, after = tiles[i : i + 3]
                wind = speed[row]
                for a in range(spec):
                    ahead = jnp.where(is_last, 0.0, pltpu.roll(here[a], all_x - 1, 0))
                    behind = jnp.where(is_first, 0.0, pltpu.roll(here[a], 1, 0))
                    beside = (before[a] + after[a]) + (ahead + behind)
                    beside = beside + (pltpu.roll(here[a], 1, 1) + pltpu.roll(here[a], wide - 1, 1))
                    mix = matrix[a * spec, row] * here[0]
                    for s in range(1, spec):
                        mix = mix + matrix[a * spec + s, row] * here[s]
                    target[a, row] = mix + wind * ahead + spread[a] * beside
            return 0

        lax.fori_loop(0, turns, block_body, 0)
        slot = jnp.int32(0)
        hit = jnp.int32(0)
        for j in range(snaps):
            slot = slot + jnp.where(plan[j] < index, 1, 0)
            hit = hit + jnp.where(plan[j] == index, 1, 0)

        @pl.when(hit > 0)
        def _():
            def keep(y, _):
                for flips in range(len(kept)):
                    tile = target[grp ^ flips, BLOCK + cells_y + y, :cells_x, :cells_z]
                    for x in range(cells_x):
                        kept[flips][x, y, pl.ds(slot, 1), :] = tile[x : x + 1]
                return 0

            lax.fori_loop(0, cells_y, keep, 0, unroll=4)

    spread = [inside * diffusion[a] for a in range(spec)]

    def two_steps(pair, _):
        step(2 * pair, state, other)
        step(2 * pair + 1, other, state)
        return 0

    lax.fori_loop(0, STEPS // 2, two_steps, 0)

    def leave(s, _):
        for y in range(cells_y):
            tile = state[s, BLOCK + cells_y + y, :cells_x, :cells_z]
            for x in range(cells_x):
                adjoint[s, x, y : y + 1, :] = tile[x : x + 1]
        return 0

    lax.fori_loop(0, spec, leave, 0)


def gram_kernel(places, given, basis, *refs):
    total, (out, chunks, held, sems) = refs[:given], refs[given:]
    count, rows, cells_z, modes = chunks.shape
    halves = count // len(places)
    copies = fetch(
        [basis.at[0, x, pl.ds(i * rows, rows)] for x in places for i in range(halves)]
        + list(total),
        [chunks.at[i] for i in range(count)] + [held],
        sems,
    )
    acc = None
    for i in range(count):
        copies[i].wait()
        chunk = chunks[i].reshape(rows * cells_z, modes)
        part = lax.dot_general(
            chunk, chunk, (((0,), (0,)), ((), ())), preferred_element_type=jnp.float32
        )
        acc = part if acc is None else acc + part
    if total:
        copies[-1].wait()
        acc = acc + held[...]
    out[...] = acc


def gram_part(places, basis, *total):
    _, _, cells_y, cells_z, modes = basis.shape
    chunks = 2 * len(places)
    size = 2 * len(places) * cells_y * cells_z * modes
    return pl.pallas_call(
        functools.partial(gram_kernel, places, len(total)),
        out_shape=jax.ShapeDtypeStruct((modes, modes), jnp.float32),
        in_specs=anywhere(1 + len(total)),
        out_specs=whole(1)[0],
        scratch_shapes=[
            pltpu.VMEM((chunks, cells_y // 2, cells_z, modes), jnp.bfloat16),
            pltpu.VMEM((modes, modes), jnp.float32),
            pltpu.SemaphoreType.DMA((chunks + 1,)),
        ],
        compiler_params=pltpu.CompilerParams(vmem_limit_bytes=BASIS_VMEM),
        cost_estimate=pl.CostEstimate(
            flops=size * modes, bytes_accessed=3 * size, transcendentals=0
        ),
        name="gram",
    )(basis, *total)


def rows_of(basis, flips, cells_z):
    zone = (lax.axis_index("grp") ^ flips) * cells_z
    return [
        basis.at[0, x, :, pl.ds(pl.multiple_of(zone, LANES), cells_z)]
        for x in range(basis.shape[1])
    ]


def multiply(held, rows, waits, acc):
    cells_x, cells_y, snaps, cells_z = held.shape
    for x in range(cells_x):
        values = held[x]
        high = values.astype(jnp.bfloat16).astype(jnp.float32)
        left = jnp.concatenate([high, values - high], axis=1).astype(jnp.bfloat16)
        waits[x].wait()
        for y in range(0, cells_y, 2):
            more = jnp.dot(
                jnp.concatenate([left[y], left[y + 1]], axis=1),
                rows[x, y : y + 2].reshape(2 * cells_z, rows.shape[-1]),
                preferred_element_type=jnp.float32,
            )
            acc = more if acc is None else acc + more
    return acc


def product_kernel(flips, given, *refs):
    count = len(flips)
    parts, basis, total = refs[:count], refs[count], refs[count + 1 : count + 1 + given]
    out, held, rows, sums, sems = refs[count + 1 + given :]
    cells_x, cells_z = held.shape[1], held.shape[-1]
    sources, targets = [], []
    for i in range(count):
        sources += [parts[i], *rows_of(basis, flips[i], cells_z)]
        targets += [held.at[i], *(rows.at[i, x] for x in range(cells_x))]
    copies = fetch([*sources, *total], [*targets, sums], sems)
    acc = None
    for i in range(count):
        start = i * (cells_x + 1)
        copies[start].wait()
        acc = multiply(held.at[i], rows.at[i], copies[start + 1 :], acc)
    if total:
        copies[-1].wait()
        acc = acc + sums[...]
    out[...] = acc


def product(flips, parts, basis, *total):
    cells_x, cells_y, snaps, cells_z = parts[0].shape
    modes, count = basis.shape[-1], len(flips)
    size = 2 * count * cells_x * cells_y * cells_z * modes
    return pl.pallas_call(
        functools.partial(product_kernel, flips, len(total)),
        out_shape=jax.ShapeDtypeStruct((2 * snaps, modes), jnp.float32),
        in_specs=anywhere(1 + count + len(total)),
        out_specs=whole(1)[0],
        scratch_shapes=[
            pltpu.VMEM((count, *parts[0].shape), jnp.float32),
            pltpu.VMEM((count, cells_x, cells_y, cells_z, modes), jnp.bfloat16),
            pltpu.VMEM((2 * snaps, modes), jnp.float32),
            pltpu.SemaphoreType.DMA((count * (cells_x + 1) + 1,)),
        ],
        compiler_params=pltpu.CompilerParams(vmem_limit_bytes=BASIS_VMEM),
        cost_estimate=pl.CostEstimate(
            flops=2 * snaps * size, bytes_accessed=2 * size, transcendentals=0
        ),
        name="product",
    )(*parts, basis, *total)


def body(terminal, diffusion, velocity, material, rates, stoich, plan, basis):
    spec, cells_x, cells_y, cells_z = terminal.shape
    snaps, modes = plan.shape[0], basis.shape[-1]
    count_grp, count_x = lax.axis_size("grp"), lax.axis_size("gx")
    fields, all_x = spec + 2, cells_x * count_x
    wide, depth = cells_z + LANES, 3 * cells_y + 2 * BLOCK

    own = pl.pallas_call(
        pack_kernel,
        out_shape=jax.ShapeDtypeStruct((fields, cells_y, cells_x, cells_z), jnp.float32),
        in_specs=whole(3),
        out_specs=whole(1)[0],
        name="pack",
    )(terminal, velocity, material)
    blocks = [own]
    for shift in range(1, count_x):
        blocks.append(
            lax.ppermute(own, "gx", [(i, (i - shift) % count_x) for i in range(count_x)])
        )
    from_a = [lax.ppermute(own, "gy", pairs("gy", 0))]
    from_b = [lax.ppermute(own, "gy", pairs("gy", 1))]
    gram = gram_part((0,), basis)
    *blocks, gram = lax.optimization_barrier((*blocks, gram))
    from_a += [lax.ppermute(b, "gy", pairs("gy", 0)) for b in blocks[1:]]
    from_b += [lax.ppermute(b, "gy", pairs("gy", 1)) for b in blocks[1:]]
    gram = gram_part(tuple(range(1, cells_x - 1)), basis, gram)
    blocks = blocks + from_a + from_b
    *blocks, gram = lax.optimization_barrier((*blocks, gram))
    packed = jax.ShapeDtypeStruct((fields, 3 * cells_y // GROUPS, all_x, LANES), jnp.float32)
    held = (len(blocks), fields, cells_y, cells_x, cells_z)
    edge_a, edge_b = pl.pallas_call(
        functools.partial(edges_kernel, count_x),
        out_shape=(packed, packed),
        in_specs=anywhere(len(blocks)),
        out_specs=tuple(whole(2)),
        scratch_shapes=[pltpu.VMEM(held, jnp.float32), pltpu.SemaphoreType.DMA((len(blocks),))],
        compiler_params=vmem(held, packed.shape, packed.shape),
        name="edges",
    )(*blocks)
    side_a = lax.ppermute(edge_a, "grp", pairs("grp", 0))
    side_b = lax.ppermute(edge_b, "grp", pairs("grp", 1))
    gram = gram_part((cells_x - 1,), basis, gram)
    side_a, side_b, gram = lax.optimization_barrier((side_a, side_b, gram))
    grams = copies_over(gram, "grp")

    part = jax.ShapeDtypeStruct((cells_x, cells_y, snaps, cells_z), jnp.float32)
    room = (depth, all_x, wide)
    shapes = [(spec, *room), (spec, *room), (spec * spec, *room), room, held, (2, *packed.shape)]
    final, *kept = pl.pallas_call(
        functools.partial(steps_kernel, count_x),
        out_shape=[jax.ShapeDtypeStruct(terminal.shape, jnp.float32)] + [part] * count_grp,
        in_specs=scalars(3) + whole(1) + anywhere(len(blocks) + 2),
        out_specs=whole(1 + count_grp),
        scratch_shapes=[pltpu.VMEM(shape, jnp.float32) for shape in shapes]
        + [pltpu.SemaphoreType.DMA((len(blocks) + 2,))],
        compiler_params=vmem(*shapes, terminal.shape, (count_grp, *part.shape)),
        cost_estimate=pl.CostEstimate(
            flops=0,
            bytes_accessed=2 * STEPS * spec * (spec + 2) * math.prod(room),
            transcendentals=0,
        ),
        name="steps",
    )(plan, diffusion, stoich, rates, *blocks, side_a, side_b)

    order = sorted(range(1, count_grp), key=lambda flips: -flips)
    moved = {flips: exchange(kept[flips], "grp", flips) for flips in order}
    mine, *grams = lax.optimization_barrier((kept[0], *grams))
    mine, gram = lax.optimization_barrier((mine, add_up(grams)))
    grams = copies_over(gram, "gx")
    total = product((0,), [mine], basis)
    for flips in ((1,), tuple(range(2, count_grp))):
        total = product(flips, [moved[f] for f in flips], basis, total)

    total = sum_over(total, "grp")
    total, *grams = lax.optimization_barrier((total, *grams))
    total = copies_over(total, "gx")
    high = add_up([part[:snaps] for part in total])
    low = add_up([part[snaps:] for part in total])
    first = sum_over(high, "gy")
    taken = jnp.dot(
        first.astype(jnp.bfloat16).astype(jnp.float32),
        add_up(grams),
        precision=lax.Precision.HIGHEST,
    )
    second = sum_over(high + low - taken, "gy")
    return (first + second, final)


def solution(mesh):
    in_specs = (
        P(None, "gx", "gy", "grp"),
        P(),
        P("gx", "gy", "grp"),
        P("gx", "gy", "grp"),
        P(),
        P(),
        P(),
        P("grp", "gx", "gy", None, None),
    )
    out_specs = (P(), P(None, "gx", "gy", "grp"))
    return jax.shard_map(body, mesh=mesh, in_specs=in_specs, out_specs=out_specs, check_vma=False)
```

```python
import functools
import math

import jax
import jax.numpy as jnp
from jax import lax
from jax.experimental import pallas as pl
from jax.experimental.pallas import tpu as pltpu
from jax.sharding import PartitionSpec as P

STEPS = 16
LANES = 128
GROUPS = LANES // STEPS
BLOCK = 8
ROWS = 4
MIB = 1024 * 1024


def pairs(axis, first):
    count = lax.axis_size(axis)
    lower = range(first, count - 1, 2)
    return [(i, i + 1) for i in lower] + [(i + 1, i) for i in lower]


def exchange(value, axis, flips):
    count = lax.axis_size(axis)
    return lax.ppermute(value, axis, [(i, i ^ flips) for i in range(count)])


def copies_over(value, axis):
    count = lax.axis_size(axis)
    while count > 4:
        count //= 2
        value = value + exchange(value, axis, count)
    return [value] + [exchange(value, axis, flips) for flips in range(1, count)]


def add_up(values):
    while len(values) > 1:
        values = [a + b for a, b in zip(values[::2], values[1::2])]
    return values[0]


def sum_over(value, axis):
    return add_up(copies_over(value, axis))


def whole(count):
    return [pl.BlockSpec(memory_space=pltpu.VMEM)] * count


def scalars(count):
    return [pl.BlockSpec(memory_space=pltpu.SMEM)] * count


def anywhere(count):
    return [pl.BlockSpec(memory_space=pl.ANY)] * count


def vmem(*shapes):
    return pltpu.CompilerParams(vmem_limit_bytes=4 * sum(map(math.prod, shapes)) + 6 * MIB)


def fetch(sources, targets, sems):
    copies = [
        pltpu.make_async_copy(source, target, sems.at[i])
        for i, (source, target) in enumerate(zip(sources, targets))
    ]
    for copy in copies:
        copy.start()
    return copies


def pack_kernel(terminal, velocity, material, out):
    spec, cells_x, cells_y, cells_z = terminal.shape
    for x in range(cells_x):
        for s in range(spec):
            out[s, :, x, :] = terminal[s, x]
        out[spec, :, x, :] = velocity[x]
        out[spec + 1, :, x, :] = material[x].astype(jnp.float32)


def edges_kernel(blocks_x, *refs):
    given, (out_a, out_b, blocks, sems) = refs[:-4], refs[-4:]
    blocks = [blocks.at[i] for i in range(len(given))]
    copies = fetch(given, blocks, sems)
    fields, cells_y, cells_x, cells_z = blocks[0].shape
    per_block = cells_y // GROUPS
    even = lax.axis_index("grp") % 2 == 0
    for copy in copies:
        copy.wait()
    place = lax.broadcasted_iota(jnp.int32, (blocks_x * cells_x, LANES), 1) // STEPS

    def field_body(field, _):
        for slot in range(len(blocks) // blocks_x):
            mine = blocks[slot * blocks_x : (slot + 1) * blocks_x]
            for part in range(per_block):
                top = bottom = None
                for group in range(GROUPS):
                    row = part * GROUPS + group
                    last = jnp.concatenate(
                        [b[field, row, :, cells_z - LANES :] for b in mine], axis=0
                    )
                    start = jnp.concatenate([b[field, row, :, :LANES] for b in mine], axis=0)
                    high = pltpu.roll(last, (STEPS * (group + 1)) % LANES, 1)
                    low = pltpu.roll(start, STEPS * group, 1) if group else start
                    top = high if top is None else jnp.where(place == group, high, top)
                    bottom = low if bottom is None else jnp.where(place == group, low, bottom)
                out_a[field, slot * per_block + part] = jnp.where(even, top, bottom)
                out_b[field, slot * per_block + part] = jnp.where(even, bottom, top)
        return 0

    lax.fori_loop(0, fields, field_body, 0)


def steps_kernel(blocks_x, plan, diffusion, stoich, rates, *refs):
    count_blocks = 3 * blocks_x
    given = refs[: count_blocks + 2]
    adjoint = refs[count_blocks + 2]
    kept = refs[count_blocks + 3 : -7]
    state, other, matrix, speed, blocks, sides, sems = refs[-7:]
    blocks = [blocks.at[i] for i in range(count_blocks)]
    side_a, side_b = sides.at[0], sides.at[1]
    copies = fetch(given, blocks + [side_a, side_b], sems)
    spec, rows, all_x, wide = state.shape
    _, cells_y, cells_x, cells_z = blocks[0].shape
    grp, at_x, at_y = (lax.axis_index(axis) for axis in ("grp", "gx", "gy"))
    count_grp, count_y = lax.axis_size("grp"), lax.axis_size("gy")
    snaps = kept[0].shape[2]
    per_block = cells_y // GROUPS
    even_z = grp % 2 == 0
    even_y = at_y % 2 == 0
    starts = (
        BLOCK + cells_y,
        BLOCK + jnp.where(even_y, 2 * cells_y, 0),
        BLOCK + jnp.where(even_y, 0, 2 * cells_y),
    )
    lane = lax.broadcasted_iota(jnp.int32, (all_x, LANES), 1)
    is_right = lane < LANES // 2
    has_right = grp < count_grp - 1
    has_left = grp > 0
    beyond = jnp.where(
        is_right, jnp.where(has_right, 1.0, 0.0), jnp.where(has_left, 1.0, 0.0)
    ).astype(jnp.float32)
    inside = jnp.concatenate(
        [jnp.ones((all_x, LANES), jnp.float32)] * (cells_z // LANES) + [beyond], axis=1
    )
    row_x = lax.broadcasted_iota(jnp.int32, (all_x, wide), 0)
    place_x = (row_x + at_x * cells_x) % all_x
    is_first = place_x == 0
    is_last = place_x == all_x - 1

    columns = [
        jnp.broadcast_to(rates[:, r : r + 1], (rates.shape[0], LANES)) for r in range(rates.shape[1])
    ]
    table = [
        sum(
            columns[r] * stoich[r, s].astype(jnp.float32) for r in range(a, rates.shape[1], spec)
        )
        for a in range(spec)
        for s in range(spec)
    ]
    for copy in copies:
        copy.wait()
    for slot in range(3):
        mine = blocks[slot * blocks_x : (slot + 1) * blocks_x]
        for part in range(per_block):

            def load(field, part=part, slot=slot, mine=mine):
                packed_a = side_a[field, slot * per_block + part]
                packed_b = side_b[field, slot * per_block + part]
                right = jnp.where(even_z, packed_a, packed_b)
                left = jnp.where(even_z, packed_b, packed_a)
                out = []
                for group in range(GROUPS):
                    row = part * GROUPS + group
                    own = jnp.concatenate([b[field, row] for b in mine], axis=0)
                    after = pltpu.roll(right, (LANES - STEPS * group) % LANES, 1) if group else right
                    before = pltpu.roll(left, LANES - STEPS * (group + 1), 1) if group < GROUPS - 1 else left
                    out.append(jnp.concatenate([own, jnp.where(is_right, after, before)], axis=1))
                return out

            first_row = starts[slot] + part * GROUPS

            def species_body(s, _, load=load, first_row=first_row):
                for group, tile in enumerate(load(s)):
                    state[s, first_row + group] = tile
                return 0

            lax.fori_loop(0, spec, species_body, 0, unroll=True)
            winds = load(spec)
            kinds = load(spec + 1)
            for group in range(GROUPS):
                speed[first_row + group] = winds[group] * inside
                matrix[0, first_row + group] = kinds[group]

    def coefficients(turn, _):
        for i in range(ROWS):
            row_coefficients(lowest + turn * ROWS + i)
        return 0

    def row_coefficients(row):
        kind = matrix[0, row].astype(jnp.int32)
        wind = speed[row]
        for a in range(spec):
            stay = inside * (1.0 - 6.0 * diffusion[a]) - wind
            for s in range(spec):
                tab = table[a * spec + s]
                tiles = [
                    jnp.concatenate(
                        [
                            jnp.take_along_axis(tab, kind[x : x + 8, z : z + LANES], axis=0)
                            for z in range(0, wide, LANES)
                        ],
                        axis=1,
                    )
                    for x in range(0, all_x, 8)
                ]
                value = jnp.concatenate(tiles, axis=0) * inside
                matrix[a * spec + s, row] = value + stay if a == s else value

    zero = jnp.zeros((all_x, wide), jnp.float32)

    def clear(row, _):
        for s in range(spec):
            other[s, row] = zero
        return 0

    lax.fori_loop(0, rows, clear, 0)
    for row in (*range(BLOCK), *range(rows - BLOCK, rows)):
        speed[row] = zero
        for s in range(spec):
            state[s, row] = zero
        for k in range(spec * spec):
            matrix[k, row] = zero

    lowest = jnp.where(at_y > 0, BLOCK, BLOCK + cells_y)
    highest = jnp.where(at_y < count_y - 1, rows - BLOCK, rows - BLOCK - cells_y)
    lax.fori_loop(0, (highest - lowest) // ROWS, coefficients, 0)

    def step(index, source, target):
        low = jnp.maximum(BLOCK + index + 1, lowest)
        high = jnp.minimum(rows - BLOCK - 1 - index, highest)
        turns = (high - low + BLOCK - 1) // BLOCK
        start = jnp.where(high == highest, high - turns * BLOCK, low)

        def block_body(turn, _):
            base = start + turn * BLOCK
            tiles = [[source[s, base + i] for s in range(spec)] for i in range(-1, BLOCK + 1)]
            for i in range(BLOCK):
                row = base + i
                before, here, after = tiles[i : i + 3]
                wind = speed[row]
                for a in range(spec):
                    ahead = jnp.where(is_last, 0.0, pltpu.roll(here[a], all_x - 1, 0))
                    behind = jnp.where(is_first, 0.0, pltpu.roll(here[a], 1, 0))
                    beside = (before[a] + after[a]) + (ahead + behind)
                    beside = beside + (pltpu.roll(here[a], 1, 1) + pltpu.roll(here[a], wide - 1, 1))
                    mix = matrix[a * spec, row] * here[0]
                    for s in range(1, spec):
                        mix = mix + matrix[a * spec + s, row] * here[s]
                    target[a, row] = mix + wind * ahead + spread[a] * beside
            return 0

        lax.fori_loop(0, turns, block_body, 0)
        slot = jnp.int32(0)
        hit = jnp.int32(0)
        for j in range(snaps):
            slot = slot + jnp.where(plan[j] < index, 1, 0)
            hit = hit + jnp.where(plan[j] == index, 1, 0)

        @pl.when(hit > 0)
        def _():
            def keep(y, _):
                for flips in range(len(kept)):
                    tile = target[grp ^ flips, BLOCK + cells_y + y, :cells_x, :cells_z]
                    for x in range(cells_x):
                        kept[flips][x, y, pl.ds(slot, 1), :] = tile[x : x + 1]
                return 0

            lax.fori_loop(0, cells_y, keep, 0, unroll=4)

    spread = [inside * diffusion[a] for a in range(spec)]

    def two_steps(pair, _):
        step(2 * pair, state, other)
        step(2 * pair + 1, other, state)
        return 0

    lax.fori_loop(0, STEPS // 2, two_steps, 0)

    def leave(s, _):
        for y in range(cells_y):
            tile = state[s, BLOCK + cells_y + y, :cells_x, :cells_z]
            for x in range(cells_x):
                adjoint[s, x, y : y + 1, :] = tile[x : x + 1]
        return 0

    lax.fori_loop(0, spec, leave, 0)


def gram_kernel(places, later, fetched, given, *refs):
    tables, refs = refs[: len(places) if fetched else 1], refs[len(places) if fetched else 1 :]
    total, refs = refs[:given], refs[given:]
    out, ahead, (chunks, held, sems) = refs[0], refs[1 : 1 + len(later)], refs[1 + len(later) :]
    count, rows, cells_z, modes = chunks.shape
    halves = count // len(places)
    wholes = list(tables) if fetched else [tables[0].at[0, x] for x in places]
    sources = [part.at[pl.ds(i * rows, rows)] for part in wholes for i in range(halves)]
    sources += [*total, *(tables[0].at[0, x] for x in later)]
    targets = [chunks.at[i] for i in range(count)] + [held][:given] + list(ahead)
    copies = fetch(sources, targets, sems)
    acc = None
    for i in range(count):
        copies[i].wait()
        chunk = chunks[i].reshape(rows * cells_z, modes)
        part = lax.dot_general(
            chunk, chunk, (((0,), (0,)), ((), ())), preferred_element_type=jnp.float32
        )
        acc = part if acc is None else acc + part
    for copy in copies[count:]:
        copy.wait()
    if total:
        acc = acc + held[...]
    out[...] = acc


def gram_part(places, basis, *total, later=(), parts=()):
    _, _, cells_y, cells_z, modes = basis.shape
    chunks, given = 2 * len(places), len(total)
    size = 2 * len(places) * cells_y * cells_z * modes
    tables = parts or (basis,)
    return pl.pallas_call(
        functools.partial(gram_kernel, places, later, bool(parts), given),
        out_shape=[jax.ShapeDtypeStruct((modes, modes), jnp.float32)]
        + [jax.ShapeDtypeStruct((cells_y, cells_z, modes), jnp.bfloat16)] * len(later),
        in_specs=anywhere(len(tables) + given),
        out_specs=whole(1) + anywhere(len(later)),
        scratch_shapes=[
            pltpu.VMEM((chunks, cells_y // 2, cells_z, modes), jnp.bfloat16),
            pltpu.VMEM((modes, modes), jnp.float32),
            pltpu.SemaphoreType.DMA((chunks + given + len(later),)),
        ],
        compiler_params=pltpu.CompilerParams(vmem_limit_bytes=size + 8 * MIB),
        cost_estimate=pl.CostEstimate(
            flops=size * modes, bytes_accessed=3 * size, transcendentals=0
        ),
        name="gram",
    )(*tables, *total)


def rows_of(basis, flips, cells_z):
    zone = (lax.axis_index("grp") ^ flips) * cells_z
    return [
        basis.at[0, x, :, pl.ds(pl.multiple_of(zone, LANES), cells_z)]
        for x in range(basis.shape[1])
    ]


def multiply(held, rows, waits, acc):
    cells_x, cells_y, snaps, cells_z = held.shape
    for x in range(cells_x):
        values = held[x]
        high = values.astype(jnp.bfloat16).astype(jnp.float32)
        left = jnp.concatenate([high, values - high], axis=1).astype(jnp.bfloat16)
        waits[x].wait()
        for y in range(0, cells_y, 2):
            more = jnp.dot(
                jnp.concatenate([left[y], left[y + 1]], axis=1),
                rows[x, y : y + 2].reshape(2 * cells_z, rows.shape[-1]),
                preferred_element_type=jnp.float32,
            )
            acc = more if acc is None else acc + more
    return acc


def product_kernel(flips, later, fetched, given, *refs):
    count = len(flips)
    parts, refs = refs[:count], refs[count:]
    tables, refs = refs[: count if fetched else 1], refs[count if fetched else 1 :]
    total, refs = refs[:given], refs[given:]
    out, ahead, (held, rows, sums, sems) = refs[0], refs[1 : 1 + len(later)], refs[1 + len(later) :]
    cells_x, cells_z = held.shape[1], held.shape[-1]
    places = range(cells_x)
    sources, targets = [], []
    for i in range(count):
        if fetched:
            table = [tables[i].at[x] for x in places]
        else:
            table = rows_of(tables[0], flips[i], cells_z)
        sources += [parts[i], *table]
        targets += [held.at[i], *(rows.at[i, x] for x in places)]
    sources += total
    targets += [sums][:given]
    for i in range(len(later)):
        sources += rows_of(tables[0], later[i], cells_z)
        targets += [ahead[i].at[x] for x in places]
    copies = fetch(sources, targets, sems)
    acc = None
    for i in range(count):
        start = i * (cells_x + 1)
        copies[start].wait()
        acc = multiply(held.at[i], rows.at[i], copies[start + 1 :], acc)
    for copy in copies[count * (cells_x + 1) :]:
        copy.wait()
    if total:
        acc = acc + sums[...]
    out[...] = acc


def product(flips, parts, basis, *total, later=(), rows=()):
    cells_x, cells_y, snaps, cells_z = parts[0].shape
    modes, count = basis.shape[-1], len(flips)
    room = (cells_x, cells_y, cells_z, modes)
    size = 2 * count * math.prod(room)
    tables = rows or (basis,)
    given = len(total)
    return pl.pallas_call(
        functools.partial(product_kernel, flips, later, bool(rows), given),
        out_shape=[jax.ShapeDtypeStruct((2 * snaps, modes), jnp.float32)]
        + [jax.ShapeDtypeStruct(room, jnp.bfloat16)] * len(later),
        in_specs=anywhere(count + len(tables) + given),
        out_specs=whole(1) + anywhere(len(later)),
        scratch_shapes=[
            pltpu.VMEM((count, *parts[0].shape), jnp.float32),
            pltpu.VMEM((count, *room), jnp.bfloat16),
            pltpu.VMEM((2 * snaps, modes), jnp.float32),
            pltpu.SemaphoreType.DMA((count * (cells_x + 1) + cells_x * len(later) + given,)),
        ],
        compiler_params=pltpu.CompilerParams(vmem_limit_bytes=size + 8 * MIB),
        cost_estimate=pl.CostEstimate(
            flops=2 * snaps * size, bytes_accessed=2 * size, transcendentals=0
        ),
        name="product",
    )(*parts, *tables, *total)


def body(terminal, diffusion, velocity, material, rates, stoich, plan, basis):
    spec, cells_x, cells_y, cells_z = terminal.shape
    snaps, modes = plan.shape[0], basis.shape[-1]
    count_grp, count_x = lax.axis_size("grp"), lax.axis_size("gx")
    basis = pltpu.with_memory_space_constraint(basis, pltpu.HBM)
    fields, all_x = spec + 2, cells_x * count_x
    wide, depth = cells_z + LANES, 3 * cells_y + 2 * BLOCK

    own = pl.pallas_call(
        pack_kernel,
        out_shape=jax.ShapeDtypeStruct((fields, cells_y, cells_x, cells_z), jnp.float32),
        in_specs=whole(3),
        out_specs=whole(1)[0],
        name="pack",
    )(terminal, velocity, material)
    blocks = [own]
    for shift in range(1, count_x):
        blocks.append(
            lax.ppermute(own, "gx", [(i, (i - shift) % count_x) for i in range(count_x)])
        )
    from_a = [lax.ppermute(own, "gy", pairs("gy", 0))]
    from_b = [lax.ppermute(own, "gy", pairs("gy", 1))]
    (gram,) = gram_part((0,), basis)
    *blocks, gram = lax.optimization_barrier((*blocks, gram))
    from_a += [lax.ppermute(b, "gy", pairs("gy", 0)) for b in blocks[1:]]
    from_b += [lax.ppermute(b, "gy", pairs("gy", 1)) for b in blocks[1:]]
    later = tuple(range(2, cells_x))
    gram, *parts = gram_part((1,), basis, gram, later=later)
    blocks = blocks + from_a + from_b
    *blocks, gram = lax.optimization_barrier((*blocks, gram))
    packed = jax.ShapeDtypeStruct((fields, 3 * cells_y // GROUPS, all_x, LANES), jnp.float32)
    held = (len(blocks), fields, cells_y, cells_x, cells_z)
    edge_a, edge_b = pl.pallas_call(
        functools.partial(edges_kernel, count_x),
        out_shape=(packed, packed),
        in_specs=anywhere(len(blocks)),
        out_specs=tuple(whole(2)),
        scratch_shapes=[pltpu.VMEM(held, jnp.float32), pltpu.SemaphoreType.DMA((len(blocks),))],
        compiler_params=vmem(held, packed.shape, packed.shape),
        name="edges",
    )(*blocks)
    side_a = lax.ppermute(edge_a, "grp", pairs("grp", 0))
    side_b = lax.ppermute(edge_b, "grp", pairs("grp", 1))
    (gram,) = gram_part(later, basis, gram, parts=tuple(parts))
    side_a, side_b, gram = lax.optimization_barrier((side_a, side_b, gram))
    grams = copies_over(gram, "grp")

    part = jax.ShapeDtypeStruct((cells_x, cells_y, snaps, cells_z), jnp.float32)
    room = (depth, all_x, wide)
    shapes = [(spec, *room), (spec, *room), (spec * spec, *room), room, held, (2, *packed.shape)]
    final, *kept = pl.pallas_call(
        functools.partial(steps_kernel, count_x),
        out_shape=[jax.ShapeDtypeStruct(terminal.shape, jnp.float32)] + [part] * count_grp,
        in_specs=scalars(3) + whole(1) + anywhere(len(blocks) + 2),
        out_specs=whole(1 + count_grp),
        scratch_shapes=[pltpu.VMEM(shape, jnp.float32) for shape in shapes]
        + [pltpu.SemaphoreType.DMA((len(blocks) + 2,))],
        compiler_params=vmem(*shapes, terminal.shape, (count_grp, *part.shape)),
        cost_estimate=pl.CostEstimate(
            flops=0,
            bytes_accessed=2 * STEPS * spec * (spec + 2) * math.prod(room),
            transcendentals=0,
        ),
        name="steps",
    )(plan, diffusion, stoich, rates, *blocks, side_a, side_b)

    order = sorted(range(1, count_grp), key=lambda flips: -flips)
    moved = {flips: exchange(kept[flips], "grp", flips) for flips in order}
    mine, *grams = lax.optimization_barrier((kept[0], *grams))
    mine, gram = lax.optimization_barrier((mine, add_up(grams)))
    grams = copies_over(gram, "gx")
    later = tuple(range(2, count_grp))
    total, *rows = product((0,), [mine], basis, later=later)
    (total,) = product((1,), [moved[1]], basis, total)
    (total,) = product(later, [moved[f] for f in later], basis, total, rows=tuple(rows))

    total = sum_over(total, "grp")
    total, *grams = lax.optimization_barrier((total, *grams))
    total = copies_over(total, "gx")
    high = add_up([part[:snaps] for part in total])
    low = add_up([part[snaps:] for part in total])
    first = sum_over(high, "gy")
    taken = jnp.dot(
        first.astype(jnp.bfloat16).astype(jnp.float32),
        add_up(grams),
        precision=lax.Precision.HIGHEST,
    )
    second = sum_over(high + low - taken, "gy")
    return (first + second, final)


def solution(mesh):
    in_specs = (
        P(None, "gx", "gy", "grp"),
        P(),
        P("gx", "gy", "grp"),
        P("gx", "gy", "grp"),
        P(),
        P(),
        P(),
        P("grp", "gx", "gy", None, None),
    )
    out_specs = (P(), P(None, "gx", "gy", "grp"))
    return jax.shard_map(body, mesh=mesh, in_specs=in_specs, out_specs=out_specs, check_vma=False)
```

```python
import functools
import math

import jax
import jax.numpy as jnp
from jax import lax
from jax.experimental import pallas as pl
from jax.experimental.pallas import tpu as pltpu
from jax.sharding import PartitionSpec as P

STEPS = 16
LANES = 128
GROUPS = LANES // STEPS
BLOCK = 8
ROWS = 4
MIB = 1024 * 1024


def pairs(axis, first):
    count = lax.axis_size(axis)
    lower = range(first, count - 1, 2)
    return [(i, i + 1) for i in lower] + [(i + 1, i) for i in lower]


def exchange(value, axis, flips):
    count = lax.axis_size(axis)
    return lax.ppermute(value, axis, [(i, i ^ flips) for i in range(count)])


def copies_over(value, axis):
    count = lax.axis_size(axis)
    while count > 4:
        count //= 2
        value = value + exchange(value, axis, count)
    return [value] + [exchange(value, axis, flips) for flips in range(1, count)]


def add_up(values):
    while len(values) > 1:
        values = [a + b for a, b in zip(values[::2], values[1::2])]
    return values[0]


def sum_over(value, axis):
    return add_up(copies_over(value, axis))


def whole(count):
    return [pl.BlockSpec(memory_space=pltpu.VMEM)] * count


def scalars(count):
    return [pl.BlockSpec(memory_space=pltpu.SMEM)] * count


def anywhere(count):
    return [pl.BlockSpec(memory_space=pl.ANY)] * count


def vmem(*shapes):
    return pltpu.CompilerParams(vmem_limit_bytes=4 * sum(map(math.prod, shapes)) + 6 * MIB)


def fetch(sources, targets, sems):
    copies = [
        pltpu.make_async_copy(source, target, sems.at[i])
        for i, (source, target) in enumerate(zip(sources, targets))
    ]
    for copy in copies:
        copy.start()
    return copies


def pack_kernel(terminal, velocity, material, out):
    spec, cells_x, cells_y, cells_z = terminal.shape
    for x in range(cells_x):
        for s in range(spec):
            out[s, :, x, :] = terminal[s, x]
        out[spec, :, x, :] = velocity[x]
        out[spec + 1, :, x, :] = material[x].astype(jnp.float32)


def edges_kernel(blocks_x, *refs):
    given, (out_a, out_b, blocks, sems) = refs[:-4], refs[-4:]
    blocks = [blocks.at[i] for i in range(len(given))]
    copies = fetch(given, blocks, sems)
    fields, cells_y, cells_x, cells_z = blocks[0].shape
    per_block = cells_y // GROUPS
    even = lax.axis_index("grp") % 2 == 0
    for copy in copies:
        copy.wait()
    place = lax.broadcasted_iota(jnp.int32, (blocks_x * cells_x, LANES), 1) // STEPS

    def field_body(field, _):
        for slot in range(len(blocks) // blocks_x):
            mine = blocks[slot * blocks_x : (slot + 1) * blocks_x]
            for part in range(per_block):
                top = bottom = None
                for group in range(GROUPS):
                    row = part * GROUPS + group
                    low = jnp.concatenate([b[field, row, :, :LANES] for b in mine], axis=0)
                    low = pltpu.roll(low, STEPS * group, 1) if group else low
                    high = low
                    if cells_z > LANES:
                        high = jnp.concatenate(
                            [b[field, row, :, cells_z - LANES :] for b in mine], axis=0
                        )
                        high = pltpu.roll(high, STEPS * group, 1) if group else high
                    is_high = place == (group - 1) % GROUPS
                    top = high if top is None else jnp.where(is_high, high, top)
                    bottom = low if bottom is None else jnp.where(place == group, low, bottom)
                out_a[field, slot * per_block + part] = jnp.where(even, top, bottom)
                out_b[field, slot * per_block + part] = jnp.where(even, bottom, top)
        return 0

    lax.fori_loop(0, fields, field_body, 0)


def steps_kernel(blocks_x, plan, diffusion, stoich, rates, *refs):
    count_blocks = 3 * blocks_x
    given = refs[: count_blocks + 2]
    adjoint = refs[count_blocks + 2]
    kept = refs[count_blocks + 3 : -7]
    state, other, matrix, speed, blocks, sides, sems = refs[-7:]
    blocks = [blocks.at[i] for i in range(count_blocks)]
    side_a, side_b = sides.at[0], sides.at[1]
    copies = fetch(given, blocks + [side_a, side_b], sems)
    spec, rows, all_x, wide = state.shape
    _, cells_y, cells_x, cells_z = blocks[0].shape
    grp, at_x, at_y = (lax.axis_index(axis) for axis in ("grp", "gx", "gy"))
    count_grp, count_y = lax.axis_size("grp"), lax.axis_size("gy")
    snaps = kept[0].shape[2]
    per_block = cells_y // GROUPS
    even_z = grp % 2 == 0
    even_y = at_y % 2 == 0
    starts = (
        BLOCK + cells_y,
        BLOCK + jnp.where(even_y, 2 * cells_y, 0),
        BLOCK + jnp.where(even_y, 0, 2 * cells_y),
    )
    lane = lax.broadcasted_iota(jnp.int32, (all_x, LANES), 1)
    place = lane // STEPS
    is_right = lane < LANES // 2
    has_right = grp < count_grp - 1
    has_left = grp > 0
    beyond = jnp.where(
        is_right, jnp.where(has_right, 1.0, 0.0), jnp.where(has_left, 1.0, 0.0)
    ).astype(jnp.float32)
    inside = jnp.concatenate(
        [jnp.ones((all_x, LANES), jnp.float32)] * (cells_z // LANES) + [beyond], axis=1
    )
    row_x = lax.broadcasted_iota(jnp.int32, (all_x, wide), 0)
    place_x = (row_x + at_x * cells_x) % all_x
    is_first = place_x == 0
    is_last = place_x == all_x - 1

    columns = [
        jnp.broadcast_to(rates[:, r : r + 1], (rates.shape[0], LANES)) for r in range(rates.shape[1])
    ]
    table = [
        sum(
            columns[r] * stoich[r, s].astype(jnp.float32) for r in range(a, rates.shape[1], spec)
        )
        for a in range(spec)
        for s in range(spec)
    ]
    for copy in copies:
        copy.wait()
    for slot in range(3):
        mine = blocks[slot * blocks_x : (slot + 1) * blocks_x]
        for part in range(per_block):

            def load(field, part=part, slot=slot, mine=mine):
                packed_a = side_a[field, slot * per_block + part]
                packed_b = side_b[field, slot * per_block + part]
                right = jnp.where(even_z, packed_a, packed_b)
                left = jnp.where(even_z, packed_b, packed_a)
                out = []
                for group in range(GROUPS):
                    row = part * GROUPS + group
                    own = jnp.concatenate([b[field, row] for b in mine], axis=0)
                    beyond = jnp.where(place == group, right, left)
                    if group:
                        beyond = pltpu.roll(beyond, LANES - STEPS * group, 1)
                    out.append(jnp.concatenate([own, beyond], axis=1))
                return out

            first_row = starts[slot] + part * GROUPS

            def species_body(s, _, load=load, first_row=first_row):
                for group, tile in enumerate(load(s)):
                    state[s, first_row + group] = tile
                return 0

            lax.fori_loop(0, spec, species_body, 0, unroll=True)
            winds = load(spec)
            kinds = load(spec + 1)
            for group in range(GROUPS):
                speed[first_row + group] = winds[group] * inside
                matrix[0, first_row + group] = kinds[group]

    def coefficients(turn, _):
        for i in range(ROWS):
            row_coefficients(lowest + turn * ROWS + i)
        return 0

    def row_coefficients(row):
        kind = matrix[0, row].astype(jnp.int32)
        wind = speed[row]
        for a in range(spec):
            stay = inside * (1.0 - 6.0 * diffusion[a]) - wind
            for s in range(spec):
                tab = table[a * spec + s]
                tiles = [
                    jnp.concatenate(
                        [
                            jnp.take_along_axis(tab, kind[x : x + 8, z : z + LANES], axis=0)
                            for z in range(0, wide, LANES)
                        ],
                        axis=1,
                    )
                    for x in range(0, all_x, 8)
                ]
                value = jnp.concatenate(tiles, axis=0) * inside
                matrix[a * spec + s, row] = value + stay if a == s else value

    zero = jnp.zeros((all_x, wide), jnp.float32)

    def clear(row, _):
        for s in range(spec):
            other[s, row] = zero
        return 0

    lax.fori_loop(0, rows, clear, 0)
    for row in (*range(BLOCK), *range(rows - BLOCK, rows)):
        speed[row] = zero
        for s in range(spec):
            state[s, row] = zero
        for k in range(spec * spec):
            matrix[k, row] = zero

    lowest = jnp.where(at_y > 0, BLOCK, BLOCK + cells_y)
    highest = jnp.where(at_y < count_y - 1, rows - BLOCK, rows - BLOCK - cells_y)
    lax.fori_loop(0, (highest - lowest) // ROWS, coefficients, 0)

    def step(index, source, target):
        low = jnp.maximum(BLOCK + index + 1, lowest)
        high = jnp.minimum(rows - BLOCK - 1 - index, highest)
        turns = (high - low + BLOCK - 1) // BLOCK
        start = jnp.where(high == highest, high - turns * BLOCK, low)

        def block_body(turn, _):
            base = start + turn * BLOCK
            tiles = [[source[s, base + i] for s in range(spec)] for i in range(-1, BLOCK + 1)]
            for i in range(BLOCK):
                row = base + i
                before, here, after = tiles[i : i + 3]
                wind = speed[row]
                for a in range(spec):
                    ahead = jnp.where(is_last, 0.0, pltpu.roll(here[a], all_x - 1, 0))
                    behind = jnp.where(is_first, 0.0, pltpu.roll(here[a], 1, 0))
                    beside = (before[a] + after[a]) + (ahead + behind)
                    beside = beside + (pltpu.roll(here[a], 1, 1) + pltpu.roll(here[a], wide - 1, 1))
                    mix = matrix[a * spec, row] * here[0]
                    for s in range(1, spec):
                        mix = mix + matrix[a * spec + s, row] * here[s]
                    target[a, row] = mix + wind * ahead + spread[a] * beside
            return 0

        lax.fori_loop(0, turns, block_body, 0)
        slot = jnp.int32(0)
        hit = jnp.int32(0)
        for j in range(snaps):
            slot = slot + jnp.where(plan[j] < index, 1, 0)
            hit = hit + jnp.where(plan[j] == index, 1, 0)

        @pl.when(hit > 0)
        def _():
            def keep(y, _):
                for flips in range(len(kept)):
                    tile = target[grp ^ flips, BLOCK + cells_y + y, :cells_x, :cells_z]
                    for x in range(cells_x):
                        kept[flips][x, y, pl.ds(slot, 1), :] = tile[x : x + 1]
                return 0

            lax.fori_loop(0, cells_y, keep, 0, unroll=4)

    spread = [inside * diffusion[a] for a in range(spec)]

    def two_steps(pair, _):
        step(2 * pair, state, other)
        step(2 * pair + 1, other, state)
        return 0

    lax.fori_loop(0, STEPS // 2, two_steps, 0)

    def leave(s, _):
        for y in range(cells_y):
            tile = state[s, BLOCK + cells_y + y, :cells_x, :cells_z]
            for x in range(cells_x):
                adjoint[s, x, y : y + 1, :] = tile[x : x + 1]
        return 0

    lax.fori_loop(0, spec, leave, 0)


def gram_kernel(places, later, fetched, given, *refs):
    tables, refs = refs[: len(places) if fetched else 1], refs[len(places) if fetched else 1 :]
    total, refs = refs[:given], refs[given:]
    out, ahead, (chunks, held, sems) = refs[0], refs[1 : 1 + len(later)], refs[1 + len(later) :]
    count, rows, cells_z, modes = chunks.shape
    halves = count // len(places)
    wholes = list(tables) if fetched else [tables[0].at[0, x] for x in places]
    sources = [part.at[pl.ds(i * rows, rows)] for part in wholes for i in range(halves)]
    sources += [*total, *(tables[0].at[0, x] for x in later)]
    targets = [chunks.at[i] for i in range(count)] + [held][:given] + list(ahead)
    copies = fetch(sources, targets, sems)
    acc = None
    together = count if fetched else 1
    for i in range(0, count, together):
        for copy in copies[i : i + together]:
            copy.wait()
        chunk = chunks[i : i + together].reshape(together * rows * cells_z, modes)
        part = lax.dot_general(
            chunk, chunk, (((0,), (0,)), ((), ())), preferred_element_type=jnp.float32
        )
        acc = part if acc is None else acc + part
    for copy in copies[count:]:
        copy.wait()
    if total:
        acc = acc + held[...]
    out[...] = acc


def gram_part(places, basis, *total, later=(), parts=()):
    _, _, cells_y, cells_z, modes = basis.shape
    halves, given = 1 if parts else 2, len(total)
    chunks = halves * len(places)
    size = 2 * len(places) * cells_y * cells_z * modes
    tables = parts or (basis,)
    return pl.pallas_call(
        functools.partial(gram_kernel, places, later, bool(parts), given),
        out_shape=[jax.ShapeDtypeStruct((modes, modes), jnp.float32)]
        + [jax.ShapeDtypeStruct((cells_y, cells_z, modes), jnp.bfloat16)] * len(later),
        in_specs=anywhere(len(tables) + given),
        out_specs=whole(1) + anywhere(len(later)),
        scratch_shapes=[
            pltpu.VMEM((chunks, cells_y // halves, cells_z, modes), jnp.bfloat16),
            pltpu.VMEM((modes, modes), jnp.float32),
            pltpu.SemaphoreType.DMA((chunks + given + len(later),)),
        ],
        compiler_params=pltpu.CompilerParams(vmem_limit_bytes=3 * size + 8 * MIB),
        cost_estimate=pl.CostEstimate(
            flops=size * modes, bytes_accessed=3 * size, transcendentals=0
        ),
        name="gram",
    )(*tables, *total)


def rows_of(basis, flips, cells_z):
    zone = (lax.axis_index("grp") ^ flips) * cells_z
    return [
        basis.at[0, x, :, pl.ds(pl.multiple_of(zone, LANES), cells_z)]
        for x in range(basis.shape[1])
    ]


def multiply(held, rows, waits, acc):
    cells_x, cells_y, snaps, cells_z = held.shape
    for x in range(cells_x):
        values = held[x]
        high = values.astype(jnp.bfloat16).astype(jnp.float32)
        left = jnp.concatenate([high, values - high], axis=1).astype(jnp.bfloat16)
        waits[x].wait()
        for y in range(0, cells_y, 2):
            more = jnp.dot(
                jnp.concatenate([left[y], left[y + 1]], axis=1),
                rows[x, y : y + 2].reshape(2 * cells_z, rows.shape[-1]),
                preferred_element_type=jnp.float32,
            )
            acc = more if acc is None else acc + more
    return acc


def product_kernel(flips, later, fetched, given, *refs):
    count = len(flips)
    parts, refs = refs[:count], refs[count:]
    tables, refs = refs[: count if fetched else 1], refs[count if fetched else 1 :]
    total, refs = refs[:given], refs[given:]
    out, ahead, (held, rows, sums, sems) = refs[0], refs[1 : 1 + len(later)], refs[1 + len(later) :]
    cells_x, cells_z = held.shape[1], held.shape[-1]
    places = range(cells_x)
    sources, targets = [], []
    for i in range(count):
        if fetched:
            table = [tables[i].at[x] for x in places]
        else:
            table = rows_of(tables[0], flips[i], cells_z)
        sources += [parts[i], *table]
        targets += [held.at[i], *(rows.at[i, x] for x in places)]
    sources += total
    targets += [sums][:given]
    for i in range(len(later)):
        sources += rows_of(tables[0], later[i], cells_z)
        targets += [ahead[i].at[x] for x in places]
    copies = fetch(sources, targets, sems)
    acc = None
    for i in range(count):
        start = i * (cells_x + 1)
        copies[start].wait()
        acc = multiply(held.at[i], rows.at[i], copies[start + 1 :], acc)
    for copy in copies[count * (cells_x + 1) :]:
        copy.wait()
    if total:
        acc = acc + sums[...]
    out[...] = acc


def product(flips, parts, basis, *total, later=(), rows=()):
    cells_x, cells_y, snaps, cells_z = parts[0].shape
    modes, count = basis.shape[-1], len(flips)
    room = (cells_x, cells_y, cells_z, modes)
    size = 2 * count * math.prod(room)
    tables = rows or (basis,)
    given = len(total)
    return pl.pallas_call(
        functools.partial(product_kernel, flips, later, bool(rows), given),
        out_shape=[jax.ShapeDtypeStruct((2 * snaps, modes), jnp.float32)]
        + [jax.ShapeDtypeStruct(room, jnp.bfloat16)] * len(later),
        in_specs=anywhere(count + len(tables) + given),
        out_specs=whole(1) + anywhere(len(later)),
        scratch_shapes=[
            pltpu.VMEM((count, *parts[0].shape), jnp.float32),
            pltpu.VMEM((count, *room), jnp.bfloat16),
            pltpu.VMEM((2 * snaps, modes), jnp.float32),
            pltpu.SemaphoreType.DMA((count * (cells_x + 1) + cells_x * len(later) + given,)),
        ],
        compiler_params=pltpu.CompilerParams(vmem_limit_bytes=size + 8 * MIB),
        cost_estimate=pl.CostEstimate(
            flops=2 * snaps * size, bytes_accessed=2 * size, transcendentals=0
        ),
        name="product",
    )(*parts, *tables, *total)


def body(terminal, diffusion, velocity, material, rates, stoich, plan, basis):
    spec, cells_x, cells_y, cells_z = terminal.shape
    snaps, modes = plan.shape[0], basis.shape[-1]
    count_grp, count_x = lax.axis_size("grp"), lax.axis_size("gx")
    basis = pltpu.with_memory_space_constraint(basis, pltpu.HBM)
    fields, all_x = spec + 2, cells_x * count_x
    wide, depth = cells_z + LANES, 3 * cells_y + 2 * BLOCK

    own = pl.pallas_call(
        pack_kernel,
        out_shape=jax.ShapeDtypeStruct((fields, cells_y, cells_x, cells_z), jnp.float32),
        in_specs=whole(3),
        out_specs=whole(1)[0],
        name="pack",
    )(terminal, velocity, material)
    blocks = [own]
    for shift in range(1, count_x):
        blocks.append(
            lax.ppermute(own, "gx", [(i, (i - shift) % count_x) for i in range(count_x)])
        )
    from_a = [lax.ppermute(own, "gy", pairs("gy", 0))]
    from_b = [lax.ppermute(own, "gy", pairs("gy", 1))]
    (gram,) = gram_part((0,), basis)
    *blocks, gram = lax.optimization_barrier((*blocks, gram))
    from_a += [lax.ppermute(b, "gy", pairs("gy", 0)) for b in blocks[1:]]
    from_b += [lax.ppermute(b, "gy", pairs("gy", 1)) for b in blocks[1:]]
    later = tuple(range(2, cells_x))
    gram, *parts = gram_part((1,), basis, gram, later=later)
    blocks = blocks + from_a + from_b
    *blocks, gram = lax.optimization_barrier((*blocks, gram))
    packed = jax.ShapeDtypeStruct((fields, 3 * cells_y // GROUPS, all_x, LANES), jnp.float32)
    held = (len(blocks), fields, cells_y, cells_x, cells_z)
    edge_a, edge_b = pl.pallas_call(
        functools.partial(edges_kernel, count_x),
        out_shape=(packed, packed),
        in_specs=anywhere(len(blocks)),
        out_specs=tuple(whole(2)),
        scratch_shapes=[pltpu.VMEM(held, jnp.float32), pltpu.SemaphoreType.DMA((len(blocks),))],
        compiler_params=vmem(held, packed.shape, packed.shape),
        name="edges",
    )(*blocks)
    side_a = lax.ppermute(edge_a, "grp", pairs("grp", 0))
    side_b = lax.ppermute(edge_b, "grp", pairs("grp", 1))
    (gram,) = gram_part(later, basis, gram, parts=tuple(parts))
    side_a, side_b, gram = lax.optimization_barrier((side_a, side_b, gram))
    grams = copies_over(gram, "grp")

    part = jax.ShapeDtypeStruct((cells_x, cells_y, snaps, cells_z), jnp.float32)
    room = (depth, all_x, wide)
    shapes = [(spec, *room), (spec, *room), (spec * spec, *room), room, held, (2, *packed.shape)]
    final, *kept = pl.pallas_call(
        functools.partial(steps_kernel, count_x),
        out_shape=[jax.ShapeDtypeStruct(terminal.shape, jnp.float32)] + [part] * count_grp,
        in_specs=scalars(3) + whole(1) + anywhere(len(blocks) + 2),
        out_specs=whole(1 + count_grp),
        scratch_shapes=[pltpu.VMEM(shape, jnp.float32) for shape in shapes]
        + [pltpu.SemaphoreType.DMA((len(blocks) + 2,))],
        compiler_params=vmem(*shapes, terminal.shape, (count_grp, *part.shape)),
        cost_estimate=pl.CostEstimate(
            flops=0,
            bytes_accessed=2 * STEPS * spec * (spec + 2) * math.prod(room),
            transcendentals=0,
        ),
        name="steps",
    )(plan, diffusion, stoich, rates, *blocks, side_a, side_b)

    order = sorted(range(1, count_grp), key=lambda flips: -flips)
    moved = {flips: exchange(kept[flips], "grp", flips) for flips in order}
    mine, *grams = lax.optimization_barrier((kept[0], *grams))
    mine, gram = lax.optimization_barrier((mine, add_up(grams)))
    grams = copies_over(gram, "gx")
    later = tuple(range(2, count_grp))
    total, *rows = product((0,), [mine], basis, later=later)
    (total,) = product((1,), [moved[1]], basis, total)
    (total,) = product(later, [moved[f] for f in later], basis, total, rows=tuple(rows))

    total = sum_over(total, "grp")
    total, *grams = lax.optimization_barrier((total, *grams))
    total = copies_over(total, "gx")
    high = add_up([part[:snaps] for part in total])
    low = add_up([part[snaps:] for part in total])
    first = sum_over(high, "gy")
    taken = jnp.dot(
        first.astype(jnp.bfloat16).astype(jnp.float32),
        add_up(grams),
        precision=lax.Precision.HIGHEST,
    )
    second = sum_over(high + low - taken, "gy")
    return (first + second, final)


def solution(mesh):
    in_specs = (
        P(None, "gx", "gy", "grp"),
        P(),
        P("gx", "gy", "grp"),
        P("gx", "gy", "grp"),
        P(),
        P(),
        P(),
        P("grp", "gx", "gy", None, None),
    )
    out_specs = (P(), P(None, "gx", "gy", "grp"))
    return jax.shard_map(body, mesh=mesh, in_specs=in_specs, out_specs=out_specs, check_vma=False)
```

```python
import functools
import math

import jax
import jax.numpy as jnp
from jax import lax
from jax.experimental import pallas as pl
from jax.experimental.pallas import tpu as pltpu
from jax.sharding import PartitionSpec as P

STEPS = 16
LANES = 128
GROUPS = LANES // STEPS
BLOCK = 8
ROWS = 4
MIB = 1024 * 1024


def pairs(axis, first):
    count = lax.axis_size(axis)
    lower = range(first, count - 1, 2)
    return [(i, i + 1) for i in lower] + [(i + 1, i) for i in lower]


def exchange(value, axis, flips):
    count = lax.axis_size(axis)
    return lax.ppermute(value, axis, [(i, i ^ flips) for i in range(count)])


def copies_over(value, axis):
    count = lax.axis_size(axis)
    while count > 4:
        count //= 2
        value = value + exchange(value, axis, count)
    return [value] + [exchange(value, axis, flips) for flips in range(1, count)]


def add_up(values):
    while len(values) > 1:
        values = [a + b for a, b in zip(values[::2], values[1::2])]
    return values[0]


def sum_over(value, axis):
    return add_up(copies_over(value, axis))


def whole(count):
    return [pl.BlockSpec(memory_space=pltpu.VMEM)] * count


def scalars(count):
    return [pl.BlockSpec(memory_space=pltpu.SMEM)] * count


def anywhere(count):
    return [pl.BlockSpec(memory_space=pl.ANY)] * count


def vmem(*shapes):
    return pltpu.CompilerParams(vmem_limit_bytes=4 * sum(map(math.prod, shapes)) + 6 * MIB)


def fetch(sources, targets, sems):
    copies = [
        pltpu.make_async_copy(source, target, sems.at[i])
        for i, (source, target) in enumerate(zip(sources, targets))
    ]
    for copy in copies:
        copy.start()
    return copies


def pack_kernel(terminal, velocity, material, out):
    spec, cells_x, cells_y, cells_z = terminal.shape
    for x in range(cells_x):
        for s in range(spec):
            out[s, :, x, :] = terminal[s, x]
        out[spec, :, x, :] = velocity[x]
        out[spec + 1, :, x, :] = material[x].astype(jnp.float32)


def edges_kernel(blocks_x, *refs):
    given, (out_a, out_b, blocks, sems) = refs[:-4], refs[-4:]
    blocks = [blocks.at[i] for i in range(len(given))]
    copies = fetch(given, blocks, sems)
    fields, cells_y, cells_x, cells_z = blocks[0].shape
    per_block = cells_y // GROUPS
    even = lax.axis_index("grp") % 2 == 0
    for copy in copies:
        copy.wait()
    place = lax.broadcasted_iota(jnp.int32, (blocks_x * cells_x, LANES), 1) // STEPS

    def field_body(field, _):
        for slot in range(len(blocks) // blocks_x):
            mine = blocks[slot * blocks_x : (slot + 1) * blocks_x]
            for part in range(per_block):
                top = bottom = None
                for group in range(GROUPS):
                    row = part * GROUPS + group
                    low = jnp.concatenate([b[field, row, :, :LANES] for b in mine], axis=0)
                    low = pltpu.roll(low, STEPS * group, 1) if group else low
                    high = low
                    if cells_z > LANES:
                        high = jnp.concatenate(
                            [b[field, row, :, cells_z - LANES :] for b in mine], axis=0
                        )
                        high = pltpu.roll(high, STEPS * group, 1) if group else high
                    is_high = place == (group - 1) % GROUPS
                    top = high if top is None else jnp.where(is_high, high, top)
                    bottom = low if bottom is None else jnp.where(place == group, low, bottom)
                out_a[field, slot * per_block + part] = jnp.where(even, top, bottom)
                out_b[field, slot * per_block + part] = jnp.where(even, bottom, top)
        return 0

    lax.fori_loop(0, fields, field_body, 0)


def steps_kernel(blocks_x, plan, diffusion, stoich, rates, *refs):
    count_blocks = 3 * blocks_x
    given = refs[: count_blocks + 2]
    adjoint = refs[count_blocks + 2]
    kept = refs[count_blocks + 3 : -7]
    state, other, matrix, speed, blocks, sides, sems = refs[-7:]
    blocks = [blocks.at[i] for i in range(count_blocks)]
    side_a, side_b = sides.at[0], sides.at[1]
    copies = fetch(given, blocks + [side_a, side_b], sems)
    spec, rows, all_x, wide = state.shape
    _, cells_y, cells_x, cells_z = blocks[0].shape
    grp, at_x, at_y = (lax.axis_index(axis) for axis in ("grp", "gx", "gy"))
    count_grp, count_y = lax.axis_size("grp"), lax.axis_size("gy")
    snaps = kept[0].shape[2]
    per_block = cells_y // GROUPS
    even_z = grp % 2 == 0
    even_y = at_y % 2 == 0
    starts = (
        BLOCK + cells_y,
        BLOCK + jnp.where(even_y, 2 * cells_y, 0),
        BLOCK + jnp.where(even_y, 0, 2 * cells_y),
    )
    lane = lax.broadcasted_iota(jnp.int32, (all_x, LANES), 1)
    place = lane // STEPS
    is_right = lane < LANES // 2
    has_right = grp < count_grp - 1
    has_left = grp > 0
    beyond = jnp.where(
        is_right, jnp.where(has_right, 1.0, 0.0), jnp.where(has_left, 1.0, 0.0)
    ).astype(jnp.float32)
    inside = jnp.concatenate(
        [jnp.ones((all_x, LANES), jnp.float32)] * (cells_z // LANES) + [beyond], axis=1
    )
    row_x = lax.broadcasted_iota(jnp.int32, (all_x, wide), 0)
    place_x = (row_x + at_x * cells_x) % all_x
    is_first = place_x == 0
    is_last = place_x == all_x - 1

    columns = [
        jnp.broadcast_to(rates[:, r : r + 1], (rates.shape[0], LANES)) for r in range(rates.shape[1])
    ]
    table = [
        sum(
            columns[r] * stoich[r, s].astype(jnp.float32) for r in range(a, rates.shape[1], spec)
        )
        for a in range(spec)
        for s in range(spec)
    ]
    for copy in copies:
        copy.wait()
    for slot in range(3):
        mine = blocks[slot * blocks_x : (slot + 1) * blocks_x]
        for part in range(per_block):

            def load(field, part=part, slot=slot, mine=mine):
                packed_a = side_a[field, slot * per_block + part]
                packed_b = side_b[field, slot * per_block + part]
                right = jnp.where(even_z, packed_a, packed_b)
                left = jnp.where(even_z, packed_b, packed_a)
                out = []
                for group in range(GROUPS):
                    row = part * GROUPS + group
                    own = jnp.concatenate([b[field, row] for b in mine], axis=0)
                    beyond = jnp.where(place == group, right, left)
                    if group:
                        beyond = pltpu.roll(beyond, LANES - STEPS * group, 1)
                    out.append(jnp.concatenate([own, beyond], axis=1))
                return out

            first_row = starts[slot] + part * GROUPS

            def species_body(s, _, load=load, first_row=first_row):
                for group, tile in enumerate(load(s)):
                    state[s, first_row + group] = tile
                return 0

            lax.fori_loop(0, spec, species_body, 0, unroll=True)
            winds = load(spec)
            kinds = load(spec + 1)
            for group in range(GROUPS):
                speed[first_row + group] = winds[group] * inside
                matrix[0, first_row + group] = kinds[group]

    def coefficients(turn, _):
        for i in range(ROWS):
            row_coefficients(lowest + turn * ROWS + i)
        return 0

    def row_coefficients(row):
        kind = matrix[0, row].astype(jnp.int32)
        wind = speed[row]
        for a in range(spec):
            stay = inside * (1.0 - 6.0 * diffusion[a]) - wind
            for s in range(spec):
                tab = table[a * spec + s]
                tiles = [
                    jnp.concatenate(
                        [
                            jnp.take_along_axis(tab, kind[x : x + 8, z : z + LANES], axis=0)
                            for z in range(0, wide, LANES)
                        ],
                        axis=1,
                    )
                    for x in range(0, all_x, 8)
                ]
                value = jnp.concatenate(tiles, axis=0) * inside
                matrix[a * spec + s, row] = value + stay if a == s else value

    zero = jnp.zeros((all_x, wide), jnp.float32)

    def clear(row, _):
        for s in range(spec):
            other[s, row] = zero
        return 0

    lax.fori_loop(0, rows, clear, 0)
    for row in (*range(BLOCK), *range(rows - BLOCK, rows)):
        speed[row] = zero
        for s in range(spec):
            state[s, row] = zero
        for k in range(spec * spec):
            matrix[k, row] = zero

    lowest = jnp.where(at_y > 0, BLOCK, BLOCK + cells_y)
    highest = jnp.where(at_y < count_y - 1, rows - BLOCK, rows - BLOCK - cells_y)
    lax.fori_loop(0, (highest - lowest) // ROWS, coefficients, 0)

    def step(index, source, target):
        low = jnp.maximum(BLOCK + index + 1, lowest)
        high = jnp.minimum(rows - BLOCK - 1 - index, highest)
        turns = (high - low + BLOCK - 1) // BLOCK
        start = jnp.where(high == highest, high - turns * BLOCK, low)

        def block_body(turn, _):
            base = start + turn * BLOCK
            tiles = [[source[s, base + i] for s in range(spec)] for i in range(-1, BLOCK + 1)]
            for i in range(BLOCK):
                row = base + i
                before, here, after = tiles[i : i + 3]
                wind = speed[row]
                for a in range(spec):
                    ahead = jnp.where(is_last, 0.0, pltpu.roll(here[a], all_x - 1, 0))
                    behind = jnp.where(is_first, 0.0, pltpu.roll(here[a], 1, 0))
                    beside = (before[a] + after[a]) + (ahead + behind)
                    beside = beside + (pltpu.roll(here[a], 1, 1) + pltpu.roll(here[a], wide - 1, 1))
                    mix = matrix[a * spec, row] * here[0]
                    for s in range(1, spec):
                        mix = mix + matrix[a * spec + s, row] * here[s]
                    target[a, row] = mix + wind * ahead + spread[a] * beside
            return 0

        lax.fori_loop(0, turns, block_body, 0)
        slot = jnp.int32(0)
        hit = jnp.int32(0)
        for j in range(snaps):
            slot = slot + jnp.where(plan[j] < index, 1, 0)
            hit = hit + jnp.where(plan[j] == index, 1, 0)

        @pl.when(hit > 0)
        def _():
            def keep(y, _):
                for flips in range(len(kept)):
                    tile = target[grp ^ flips, BLOCK + cells_y + y, :cells_x, :cells_z]
                    for x in range(cells_x):
                        kept[flips][x, y, pl.ds(slot, 1), :] = tile[x : x + 1]
                return 0

            lax.fori_loop(0, cells_y, keep, 0, unroll=4)

    spread = [inside * diffusion[a] for a in range(spec)]

    def two_steps(pair, _):
        step(2 * pair, state, other)
        step(2 * pair + 1, other, state)
        return 0

    lax.fori_loop(0, STEPS // 2, two_steps, 0)

    def leave(s, _):
        for y in range(cells_y):
            tile = state[s, BLOCK + cells_y + y, :cells_x, :cells_z]
            for x in range(cells_x):
                adjoint[s, x, y : y + 1, :] = tile[x : x + 1]
        return 0

    lax.fori_loop(0, spec, leave, 0)


def gram_kernel(places, later, fetched, given, *refs):
    tables, refs = refs[: len(places) if fetched else 1], refs[len(places) if fetched else 1 :]
    total, refs = refs[:given], refs[given:]
    out, ahead, (chunks, held, sems) = refs[0], refs[1 : 1 + len(later)], refs[1 + len(later) :]
    count, rows, cells_z, modes = chunks.shape
    halves = count // len(places)
    wholes = list(tables) if fetched else [tables[0].at[0, x] for x in places]
    sources = [part.at[pl.ds(i * rows, rows)] for part in wholes for i in range(halves)]
    sources += [*total, *(tables[0].at[0, x] for x in later)]
    targets = [chunks.at[i] for i in range(count)] + [held][:given] + list(ahead)
    copies = fetch(sources, targets, sems)
    acc = None
    together = count if fetched else 1
    for i in range(0, count, together):
        for copy in copies[i : i + together]:
            copy.wait()
        chunk = chunks[i : i + together].reshape(together * rows * cells_z, modes)
        part = lax.dot_general(
            chunk, chunk, (((0,), (0,)), ((), ())), preferred_element_type=jnp.float32
        )
        acc = part if acc is None else acc + part
    for copy in copies[count:]:
        copy.wait()
    if total:
        acc = acc + held[...]
    out[...] = acc


def gram_part(places, basis, *total, later=(), parts=()):
    _, _, cells_y, cells_z, modes = basis.shape
    halves, given = 1 if parts else 2, len(total)
    chunks = halves * len(places)
    size = 2 * len(places) * cells_y * cells_z * modes
    tables = parts or (basis,)
    return pl.pallas_call(
        functools.partial(gram_kernel, places, later, bool(parts), given),
        out_shape=[jax.ShapeDtypeStruct((modes, modes), jnp.float32)]
        + [jax.ShapeDtypeStruct((cells_y, cells_z, modes), jnp.bfloat16)] * len(later),
        in_specs=anywhere(len(tables) + given),
        out_specs=whole(1) + anywhere(len(later)),
        scratch_shapes=[
            pltpu.VMEM((chunks, cells_y // halves, cells_z, modes), jnp.bfloat16),
            pltpu.VMEM((modes, modes), jnp.float32),
            pltpu.SemaphoreType.DMA((chunks + given + len(later),)),
        ],
        compiler_params=pltpu.CompilerParams(vmem_limit_bytes=3 * size + 8 * MIB),
        cost_estimate=pl.CostEstimate(
            flops=size * modes, bytes_accessed=3 * size, transcendentals=0
        ),
        name="gram",
    )(*tables, *total)


def rows_of(basis, flips, cells_z):
    zone = (lax.axis_index("grp") ^ flips) * cells_z
    return [
        basis.at[0, x, :, pl.ds(pl.multiple_of(zone, LANES), cells_z)]
        for x in range(basis.shape[1])
    ]


def multiply(held, rows, waits, acc):
    cells_x, cells_y, snaps, cells_z = held.shape
    for x in range(cells_x):
        values = held[x]
        high = values.astype(jnp.bfloat16).astype(jnp.float32)
        left = jnp.concatenate([high, values - high], axis=1).astype(jnp.bfloat16)
        waits[x].wait()
        for y in range(0, cells_y, 2):
            more = jnp.dot(
                jnp.concatenate([left[y], left[y + 1]], axis=1),
                rows[x, y : y + 2].reshape(2 * cells_z, rows.shape[-1]),
                preferred_element_type=jnp.float32,
            )
            acc = more if acc is None else acc + more
    return acc


def product_kernel(flips, later, fetched, given, *refs):
    count = len(flips)
    parts, refs = refs[:count], refs[count:]
    tables, refs = refs[: count if fetched else 1], refs[count if fetched else 1 :]
    total, refs = refs[:given], refs[given:]
    out, ahead, (held, rows, sums, sems) = refs[0], refs[1 : 1 + len(later)], refs[1 + len(later) :]
    cells_x, cells_z = held.shape[1], held.shape[-1]
    places = range(cells_x)
    sources, targets = [], []
    for i in range(count):
        if fetched:
            table = [tables[i].at[x] for x in places]
        else:
            table = rows_of(tables[0], flips[i], cells_z)
        sources += [parts[i], *table]
        targets += [held.at[i], *(rows.at[i, x] for x in places)]
    sources += total
    targets += [sums][:given]
    for i in range(len(later)):
        sources += rows_of(tables[0], later[i], cells_z)
        targets += [ahead[i].at[x] for x in places]
    copies = fetch(sources, targets, sems)
    acc = None
    for i in range(count):
        start = i * (cells_x + 1)
        copies[start].wait()
        acc = multiply(held.at[i], rows.at[i], copies[start + 1 :], acc)
    for copy in copies[count * (cells_x + 1) :]:
        copy.wait()
    if total:
        acc = acc + sums[...]
    out[...] = acc


def product(flips, parts, basis, *total, later=(), rows=()):
    cells_x, cells_y, snaps, cells_z = parts[0].shape
    modes, count = basis.shape[-1], len(flips)
    room = (cells_x, cells_y, cells_z, modes)
    size = 2 * count * math.prod(room)
    tables = rows or (basis,)
    given = len(total)
    return pl.pallas_call(
        functools.partial(product_kernel, flips, later, bool(rows), given),
        out_shape=[jax.ShapeDtypeStruct((2 * snaps, modes), jnp.float32)]
        + [jax.ShapeDtypeStruct(room, jnp.bfloat16)] * len(later),
        in_specs=anywhere(count + len(tables) + given),
        out_specs=whole(1) + anywhere(len(later)),
        scratch_shapes=[
            pltpu.VMEM((count, *parts[0].shape), jnp.float32),
            pltpu.VMEM((count, *room), jnp.bfloat16),
            pltpu.VMEM((2 * snaps, modes), jnp.float32),
            pltpu.SemaphoreType.DMA((count * (cells_x + 1) + cells_x * len(later) + given,)),
        ],
        compiler_params=pltpu.CompilerParams(vmem_limit_bytes=size + 8 * MIB),
        cost_estimate=pl.CostEstimate(
            flops=2 * snaps * size, bytes_accessed=2 * size, transcendentals=0
        ),
        name="product",
    )(*parts, *tables, *total)


def body(terminal, diffusion, velocity, material, rates, stoich, plan, basis):
    spec, cells_x, cells_y, cells_z = terminal.shape
    snaps, modes = plan.shape[0], basis.shape[-1]
    count_grp, count_x = lax.axis_size("grp"), lax.axis_size("gx")
    basis = pltpu.with_memory_space_constraint(basis, pltpu.HBM)
    fields, all_x = spec + 2, cells_x * count_x
    wide, depth = cells_z + LANES, 3 * cells_y + 2 * BLOCK

    own = pl.pallas_call(
        pack_kernel,
        out_shape=jax.ShapeDtypeStruct((fields, cells_y, cells_x, cells_z), jnp.float32),
        in_specs=whole(3),
        out_specs=whole(1)[0],
        name="pack",
    )(terminal, velocity, material)
    blocks = [own]
    for shift in range(1, count_x):
        blocks.append(
            lax.ppermute(own, "gx", [(i, (i - shift) % count_x) for i in range(count_x)])
        )
    from_a = [lax.ppermute(own, "gy", pairs("gy", 0))]
    from_b = [lax.ppermute(own, "gy", pairs("gy", 1))]
    (gram,) = gram_part((0,), basis)
    *blocks, gram = lax.optimization_barrier((*blocks, gram))
    from_a += [lax.ppermute(b, "gy", pairs("gy", 0)) for b in blocks[1:]]
    from_b += [lax.ppermute(b, "gy", pairs("gy", 1)) for b in blocks[1:]]
    later = tuple(range(2, cells_x))
    gram, *parts = gram_part((1,), basis, gram, later=later)
    blocks = blocks + from_a + from_b
    *blocks, gram = lax.optimization_barrier((*blocks, gram))
    packed = jax.ShapeDtypeStruct((fields, 3 * cells_y // GROUPS, all_x, LANES), jnp.float32)
    held = (len(blocks), fields, cells_y, cells_x, cells_z)
    edge_a, edge_b = pl.pallas_call(
        functools.partial(edges_kernel, count_x),
        out_shape=(packed, packed),
        in_specs=anywhere(len(blocks)),
        out_specs=tuple(whole(2)),
        scratch_shapes=[pltpu.VMEM(held, jnp.float32), pltpu.SemaphoreType.DMA((len(blocks),))],
        compiler_params=vmem(held, packed.shape, packed.shape),
        name="edges",
    )(*blocks)
    side_a = lax.ppermute(edge_a, "grp", pairs("grp", 0))
    side_b = lax.ppermute(edge_b, "grp", pairs("grp", 1))
    (gram,) = gram_part(later, basis, gram, parts=tuple(parts))
    side_a, side_b, gram = lax.optimization_barrier((side_a, side_b, gram))
    grams = copies_over(gram, "grp")

    part = jax.ShapeDtypeStruct((cells_x, cells_y, snaps, cells_z), jnp.float32)
    room = (depth, all_x, wide)
    shapes = [(spec, *room), (spec, *room), (spec * spec, *room), room, held, (2, *packed.shape)]
    final, *kept = pl.pallas_call(
        functools.partial(steps_kernel, count_x),
        out_shape=[jax.ShapeDtypeStruct(terminal.shape, jnp.float32)] + [part] * count_grp,
        in_specs=scalars(3) + whole(1) + anywhere(len(blocks) + 2),
        out_specs=whole(1 + count_grp),
        scratch_shapes=[pltpu.VMEM(shape, jnp.float32) for shape in shapes]
        + [pltpu.SemaphoreType.DMA((len(blocks) + 2,))],
        compiler_params=vmem(*shapes, terminal.shape, (count_grp, *part.shape)),
        cost_estimate=pl.CostEstimate(
            flops=0,
            bytes_accessed=2 * STEPS * spec * (spec + 2) * math.prod(room),
            transcendentals=0,
        ),
        name="steps",
    )(plan, diffusion, stoich, rates, *blocks, side_a, side_b)

    last = count_grp - 1
    moved = {flips: exchange(kept[flips], "grp", flips) for flips in range(1, last)}
    mine, *grams = lax.optimization_barrier((kept[0], *grams))
    mine, final_part, gram = lax.optimization_barrier((mine, kept[last], add_up(grams)))
    moved[last] = exchange(final_part, "grp", last)
    grams = copies_over(gram, "gx")
    later = tuple(range(2, count_grp))
    total, *rows = product((0,), [mine], basis, later=later)
    (total,) = product((1,), [moved[1]], basis, total)
    for flips, table in zip(later, rows):
        (total,) = product((flips,), [moved[flips]], basis, total, rows=(table,))

    total = sum_over(total, "grp")
    total, *grams = lax.optimization_barrier((total, *grams))
    total = copies_over(total, "gx")
    high = add_up([part[:snaps] for part in total])
    low = add_up([part[snaps:] for part in total])
    first = sum_over(high, "gy")
    taken = jnp.dot(
        first.astype(jnp.bfloat16).astype(jnp.float32),
        add_up(grams),
        precision=lax.Precision.HIGHEST,
    )
    second = sum_over(high + low - taken, "gy")
    return (first + second, final)


def solution(mesh):
    in_specs = (
        P(None, "gx", "gy", "grp"),
        P(),
        P("gx", "gy", "grp"),
        P("gx", "gy", "grp"),
        P(),
        P(),
        P(),
        P("grp", "gx", "gy", None, None),
    )
    out_specs = (P(), P(None, "gx", "gy", "grp"))
    return jax.shard_map(body, mesh=mesh, in_specs=in_specs, out_specs=out_specs, check_vma=False)
```

```python
import functools
import math

import jax
import jax.numpy as jnp
from jax import lax
from jax.experimental import pallas as pl
from jax.experimental.pallas import tpu as pltpu
from jax.sharding import PartitionSpec as P

STEPS = 16
LANES = 128
GROUPS = LANES // STEPS
BLOCK = 8
ROWS = 4
MIB = 1024 * 1024


def pairs(axis, first):
    count = lax.axis_size(axis)
    lower = range(first, count - 1, 2)
    return [(i, i + 1) for i in lower] + [(i + 1, i) for i in lower]


def exchange(value, axis, flips):
    count = lax.axis_size(axis)
    return lax.ppermute(value, axis, [(i, i ^ flips) for i in range(count)])


def copies_over(value, axis):
    count = lax.axis_size(axis)
    while count > 4:
        count //= 2
        value = value + exchange(value, axis, count)
    return [value] + [exchange(value, axis, flips) for flips in range(1, count)]


def add_up(values):
    while len(values) > 1:
        values = [a + b for a, b in zip(values[::2], values[1::2])]
    return values[0]


def sum_over(value, axis):
    return add_up(copies_over(value, axis))


def whole(count):
    return [pl.BlockSpec(memory_space=pltpu.VMEM)] * count


def scalars(count):
    return [pl.BlockSpec(memory_space=pltpu.SMEM)] * count


def anywhere(count):
    return [pl.BlockSpec(memory_space=pl.ANY)] * count


def vmem(*shapes):
    return pltpu.CompilerParams(vmem_limit_bytes=4 * sum(map(math.prod, shapes)) + 6 * MIB)


def fetch(sources, targets, sems):
    copies = [
        pltpu.make_async_copy(source, target, sems.at[i])
        for i, (source, target) in enumerate(zip(sources, targets))
    ]
    for copy in copies:
        copy.start()
    return copies


def pack_kernel(terminal, velocity, material, out):
    spec, cells_x, cells_y, cells_z = terminal.shape
    for x in range(cells_x):
        for s in range(spec):
            out[s, :, x, :] = terminal[s, x]
        out[spec, :, x, :] = velocity[x]
        out[spec + 1, :, x, :] = material[x].astype(jnp.float32)


def edges_kernel(blocks_x, *refs):
    given, (out_a, out_b, blocks, sems) = refs[:-4], refs[-4:]
    blocks = [blocks.at[i] for i in range(len(given))]
    copies = fetch(given, blocks, sems)
    fields, cells_y, cells_x, cells_z = blocks[0].shape
    per_block = cells_y // GROUPS
    even = lax.axis_index("grp") % 2 == 0
    for copy in copies:
        copy.wait()
    place = lax.broadcasted_iota(jnp.int32, (blocks_x * cells_x, LANES), 1) // STEPS

    def field_body(field, _):
        for slot in range(len(blocks) // blocks_x):
            mine = blocks[slot * blocks_x : (slot + 1) * blocks_x]
            for part in range(per_block):
                top = bottom = None
                for group in range(GROUPS):
                    row = part * GROUPS + group
                    low = jnp.concatenate([b[field, row, :, :LANES] for b in mine], axis=0)
                    low = pltpu.roll(low, STEPS * group, 1) if group else low
                    high = low
                    if cells_z > LANES:
                        high = jnp.concatenate(
                            [b[field, row, :, cells_z - LANES :] for b in mine], axis=0
                        )
                        high = pltpu.roll(high, STEPS * group, 1) if group else high
                    is_high = place == (group - 1) % GROUPS
                    top = high if top is None else jnp.where(is_high, high, top)
                    bottom = low if bottom is None else jnp.where(place == group, low, bottom)
                out_a[field, slot * per_block + part] = jnp.where(even, top, bottom)
                out_b[field, slot * per_block + part] = jnp.where(even, bottom, top)
        return 0

    lax.fori_loop(0, fields, field_body, 0)


def steps_kernel(blocks_x, plan, diffusion, stoich, rates, *refs):
    count_blocks = 3 * blocks_x
    given = refs[: count_blocks + 2]
    adjoint = refs[count_blocks + 2]
    kept = refs[count_blocks + 3 : -7]
    state, other, matrix, speed, blocks, sides, sems = refs[-7:]
    blocks = [blocks.at[i] for i in range(count_blocks)]
    side_a, side_b = sides.at[0], sides.at[1]
    copies = fetch(given, blocks + [side_a, side_b], sems)
    spec, rows, all_x, wide = state.shape
    _, cells_y, cells_x, cells_z = blocks[0].shape
    grp, at_x, at_y = (lax.axis_index(axis) for axis in ("grp", "gx", "gy"))
    count_grp, count_y = lax.axis_size("grp"), lax.axis_size("gy")
    snaps = kept[0].shape[2]
    per_block = cells_y // GROUPS
    even_z = grp % 2 == 0
    even_y = at_y % 2 == 0
    starts = (
        BLOCK + cells_y,
        BLOCK + jnp.where(even_y, 2 * cells_y, 0),
        BLOCK + jnp.where(even_y, 0, 2 * cells_y),
    )
    lane = lax.broadcasted_iota(jnp.int32, (all_x, LANES), 1)
    place = lane // STEPS
    is_right = lane < LANES // 2
    has_right = grp < count_grp - 1
    has_left = grp > 0
    beyond = jnp.where(
        is_right, jnp.where(has_right, 1.0, 0.0), jnp.where(has_left, 1.0, 0.0)
    ).astype(jnp.float32)
    inside = jnp.concatenate(
        [jnp.ones((all_x, LANES), jnp.float32)] * (cells_z // LANES) + [beyond], axis=1
    )
    row_x = lax.broadcasted_iota(jnp.int32, (all_x, wide), 0)
    place_x = (row_x + at_x * cells_x) % all_x
    is_first = place_x == 0
    is_last = place_x == all_x - 1

    columns = [
        jnp.broadcast_to(rates[:, r : r + 1], (rates.shape[0], LANES)) for r in range(rates.shape[1])
    ]
    table = [
        sum(
            columns[r] * stoich[r, s].astype(jnp.float32) for r in range(a, rates.shape[1], spec)
        )
        for a in range(spec)
        for s in range(spec)
    ]
    for copy in copies:
        copy.wait()
    for slot in range(3):
        mine = blocks[slot * blocks_x : (slot + 1) * blocks_x]
        for part in range(per_block):

            def load(field, part=part, slot=slot, mine=mine):
                packed_a = side_a[field, slot * per_block + part]
                packed_b = side_b[field, slot * per_block + part]
                right = jnp.where(even_z, packed_a, packed_b)
                left = jnp.where(even_z, packed_b, packed_a)
                out = []
                for group in range(GROUPS):
                    row = part * GROUPS + group
                    own = jnp.concatenate([b[field, row] for b in mine], axis=0)
                    beyond = jnp.where(place == group, right, left)
                    if group:
                        beyond = pltpu.roll(beyond, LANES - STEPS * group, 1)
                    out.append(jnp.concatenate([own, beyond], axis=1))
                return out

            first_row = starts[slot] + part * GROUPS

            def species_body(s, _, load=load, first_row=first_row):
                for group, tile in enumerate(load(s)):
                    state[s, first_row + group] = tile
                return 0

            lax.fori_loop(0, spec, species_body, 0, unroll=True)
            winds = load(spec)
            kinds = load(spec + 1)
            for group in range(GROUPS):
                speed[first_row + group] = winds[group] * inside
                matrix[0, first_row + group] = kinds[group]

    def coefficients(turn, _):
        for i in range(ROWS):
            row_coefficients(lowest + turn * ROWS + i)
        return 0

    def row_coefficients(row):
        kind = matrix[0, row].astype(jnp.int32)
        wind = speed[row]
        for a in range(spec):
            stay = inside * (1.0 - 6.0 * diffusion[a]) - wind
            for s in range(spec):
                tab = table[a * spec + s]
                tiles = [
                    jnp.concatenate(
                        [
                            jnp.take_along_axis(tab, kind[x : x + 8, z : z + LANES], axis=0)
                            for z in range(0, wide, LANES)
                        ],
                        axis=1,
                    )
                    for x in range(0, all_x, 8)
                ]
                value = jnp.concatenate(tiles, axis=0) * inside
                matrix[a * spec + s, row] = value + stay if a == s else value

    zero = jnp.zeros((all_x, wide), jnp.float32)

    def clear(row, _):
        for s in range(spec):
            other[s, row] = zero
        return 0

    lax.fori_loop(0, rows, clear, 0)
    for row in (*range(BLOCK), *range(rows - BLOCK, rows)):
        speed[row] = zero
        for s in range(spec):
            state[s, row] = zero
        for k in range(spec * spec):
            matrix[k, row] = zero

    lowest = jnp.where(at_y > 0, BLOCK, BLOCK + cells_y)
    highest = jnp.where(at_y < count_y - 1, rows - BLOCK, rows - BLOCK - cells_y)
    lax.fori_loop(0, (highest - lowest) // ROWS, coefficients, 0)

    def step(index, source, target):
        low = jnp.maximum(BLOCK + index + 1, lowest)
        high = jnp.minimum(rows - BLOCK - 1 - index, highest)
        turns = (high - low + BLOCK - 1) // BLOCK
        start = jnp.where(high == highest, high - turns * BLOCK, low)

        def block_body(turn, _):
            base = start + turn * BLOCK
            tiles = [[source[s, base + i] for s in range(spec)] for i in range(-1, BLOCK + 1)]
            for i in range(BLOCK):
                row = base + i
                before, here, after = tiles[i : i + 3]
                wind = speed[row]
                for a in range(spec):
                    ahead = jnp.where(is_last, 0.0, pltpu.roll(here[a], all_x - 1, 0))
                    behind = jnp.where(is_first, 0.0, pltpu.roll(here[a], 1, 0))
                    beside = (before[a] + after[a]) + (ahead + behind)
                    beside = beside + (pltpu.roll(here[a], 1, 1) + pltpu.roll(here[a], wide - 1, 1))
                    mix = matrix[a * spec, row] * here[0]
                    for s in range(1, spec):
                        mix = mix + matrix[a * spec + s, row] * here[s]
                    target[a, row] = mix + wind * ahead + spread[a] * beside
            return 0

        lax.fori_loop(0, turns, block_body, 0)
        slot = jnp.int32(0)
        hit = jnp.int32(0)
        for j in range(snaps):
            slot = slot + jnp.where(plan[j] < index, 1, 0)
            hit = hit + jnp.where(plan[j] == index, 1, 0)

        @pl.when(hit > 0)
        def _():
            def keep(y, _):
                for flips in range(len(kept)):
                    tile = target[grp ^ flips, BLOCK + cells_y + y, :cells_x, :cells_z]
                    for x in range(cells_x):
                        kept[flips][x, y, pl.ds(slot, 1), :] = tile[x : x + 1]
                return 0

            lax.fori_loop(0, cells_y, keep, 0, unroll=4)

    spread = [inside * diffusion[a] for a in range(spec)]

    def two_steps(pair, _):
        step(2 * pair, state, other)
        step(2 * pair + 1, other, state)
        return 0

    lax.fori_loop(0, STEPS // 2, two_steps, 0)

    def leave(s, _):
        for y in range(cells_y):
            tile = state[s, BLOCK + cells_y + y, :cells_x, :cells_z]
            for x in range(cells_x):
                adjoint[s, x, y : y + 1, :] = tile[x : x + 1]
        return 0

    lax.fori_loop(0, spec, leave, 0)


def gram_kernel(places, later, fetched, given, *refs):
    tables, refs = refs[: len(places) if fetched else 1], refs[len(places) if fetched else 1 :]
    total, refs = refs[:given], refs[given:]
    out, ahead, (chunks, held, sems) = refs[0], refs[1 : 1 + len(later)], refs[1 + len(later) :]
    count, rows, cells_z, modes = chunks.shape
    halves = count // len(places)
    wholes = list(tables) if fetched else [tables[0].at[0, x] for x in places]
    sources = [part.at[pl.ds(i * rows, rows)] for part in wholes for i in range(halves)]
    sources += [*total, *(tables[0].at[0, x] for x in later)]
    targets = [chunks.at[i] for i in range(count)] + [held][:given] + list(ahead)
    copies = fetch(sources, targets, sems)
    acc = None
    together = count if fetched else 1
    for i in range(0, count, together):
        for copy in copies[i : i + together]:
            copy.wait()
        chunk = chunks[i : i + together].reshape(together * rows * cells_z, modes)
        part = lax.dot_general(
            chunk, chunk, (((0,), (0,)), ((), ())), preferred_element_type=jnp.float32
        )
        acc = part if acc is None else acc + part
    for copy in copies[count:]:
        copy.wait()
    if total:
        acc = acc + held[...]
    out[...] = acc


def gram_part(places, basis, *total, later=(), parts=()):
    _, _, cells_y, cells_z, modes = basis.shape
    halves, given = 1 if parts else 2, len(total)
    chunks = halves * len(places)
    size = 2 * len(places) * cells_y * cells_z * modes
    tables = parts or (basis,)
    return pl.pallas_call(
        functools.partial(gram_kernel, places, later, bool(parts), given),
        out_shape=[jax.ShapeDtypeStruct((modes, modes), jnp.float32)]
        + [jax.ShapeDtypeStruct((cells_y, cells_z, modes), jnp.bfloat16)] * len(later),
        in_specs=anywhere(len(tables) + given),
        out_specs=whole(1) + anywhere(len(later)),
        scratch_shapes=[
            pltpu.VMEM((chunks, cells_y // halves, cells_z, modes), jnp.bfloat16),
            pltpu.VMEM((modes, modes), jnp.float32),
            pltpu.SemaphoreType.DMA((chunks + given + len(later),)),
        ],
        compiler_params=pltpu.CompilerParams(vmem_limit_bytes=3 * size + 8 * MIB),
        cost_estimate=pl.CostEstimate(
            flops=size * modes, bytes_accessed=3 * size, transcendentals=0
        ),
        name="gram",
    )(*tables, *total)


def rows_of(basis, flips, cells_z):
    zone = (lax.axis_index("grp") ^ flips) * cells_z
    return [
        basis.at[0, x, :, pl.ds(pl.multiple_of(zone, LANES), cells_z)]
        for x in range(basis.shape[1])
    ]


def multiply(held, rows, waits, acc):
    cells_x, cells_y, snaps, cells_z = held.shape
    for x in range(cells_x):
        values = held[x]
        high = values.astype(jnp.bfloat16).astype(jnp.float32)
        left = jnp.concatenate([high, values - high], axis=1).astype(jnp.bfloat16)
        if waits:
            waits[x].wait()
        for y in range(0, cells_y, 2):
            more = jnp.dot(
                jnp.concatenate([left[y], left[y + 1]], axis=1),
                rows[x, y : y + 2].reshape(2 * cells_z, rows.shape[-1]),
                preferred_element_type=jnp.float32,
            )
            acc = more if acc is None else acc + more
    return acc


def product_kernel(flips, later, fetched, given, *refs):
    count = len(flips)
    parts, refs = refs[:count], refs[count:]
    tables, refs = refs[: count if fetched else 1], refs[count if fetched else 1 :]
    total, refs = refs[:given], refs[given:]
    out, ahead, (held, rows, sums, sems) = refs[0], refs[1 : 1 + len(later)], refs[1 + len(later) :]
    cells_x, cells_z = held.shape[1], held.shape[-1]
    places = range(cells_x)
    sources, targets = [], []
    for i in range(count):
        if fetched:
            table = [tables[i].at[x] for x in places]
        else:
            table = rows_of(tables[0], flips[i], cells_z)
        sources += [parts[i], *table]
        targets += [held.at[i], *(rows.at[i, x] for x in places)]
    sources += total
    targets += [sums][:given]
    for i in range(len(later)):
        sources += rows_of(tables[0], later[i], cells_z)
        targets += [ahead[i].at[x] for x in places]
    if fetched:
        acc = None
        for i in range(count):
            acc = multiply(parts[i], tables[i], None, acc)
        out[...] = acc + total[0][...] if total else acc
        return
    copies = fetch(sources, targets, sems)
    acc = None
    for i in range(count):
        start = i * (cells_x + 1)
        copies[start].wait()
        acc = multiply(held.at[i], rows.at[i], copies[start + 1 :], acc)
    for copy in copies[count * (cells_x + 1) :]:
        copy.wait()
    if total:
        acc = acc + sums[...]
    out[...] = acc


def product(flips, parts, basis, *total, later=(), rows=()):
    cells_x, cells_y, snaps, cells_z = parts[0].shape
    modes, count = basis.shape[-1], len(flips)
    room = (cells_x, cells_y, cells_z, modes)
    size = 2 * count * math.prod(room)
    tables = rows or (basis,)
    given = len(total)
    place = anywhere
    if rows:
        place = whole
        parts, tables, total = (
            [pltpu.with_memory_space_constraint(a, pltpu.VMEM) for a in arrays]
            for arrays in (parts, tables, total)
        )
    return pl.pallas_call(
        functools.partial(product_kernel, flips, later, bool(rows), given),
        out_shape=[jax.ShapeDtypeStruct((2 * snaps, modes), jnp.float32)]
        + [jax.ShapeDtypeStruct(room, jnp.bfloat16)] * len(later),
        in_specs=place(count + len(tables) + given),
        out_specs=whole(1) + anywhere(len(later)),
        scratch_shapes=[
            pltpu.VMEM((count, *parts[0].shape), jnp.float32),
            pltpu.VMEM((count, *room), jnp.bfloat16),
            pltpu.VMEM((2 * snaps, modes), jnp.float32),
            pltpu.SemaphoreType.DMA((count * (cells_x + 1) + cells_x * len(later) + given,)),
        ],
        compiler_params=pltpu.CompilerParams(vmem_limit_bytes=size + 8 * MIB),
        cost_estimate=pl.CostEstimate(
            flops=2 * snaps * size, bytes_accessed=2 * size, transcendentals=0
        ),
        name="product",
    )(*parts, *tables, *total)


def body(terminal, diffusion, velocity, material, rates, stoich, plan, basis):
    spec, cells_x, cells_y, cells_z = terminal.shape
    snaps, modes = plan.shape[0], basis.shape[-1]
    count_grp, count_x = lax.axis_size("grp"), lax.axis_size("gx")
    basis = pltpu.with_memory_space_constraint(basis, pltpu.HBM)
    fields, all_x = spec + 2, cells_x * count_x
    wide, depth = cells_z + LANES, 3 * cells_y + 2 * BLOCK

    own = pl.pallas_call(
        pack_kernel,
        out_shape=jax.ShapeDtypeStruct((fields, cells_y, cells_x, cells_z), jnp.float32),
        in_specs=whole(3),
        out_specs=whole(1)[0],
        name="pack",
    )(terminal, velocity, material)
    blocks = [own]
    for shift in range(1, count_x):
        blocks.append(
            lax.ppermute(own, "gx", [(i, (i - shift) % count_x) for i in range(count_x)])
        )
    from_a = [lax.ppermute(own, "gy", pairs("gy", 0))]
    from_b = [lax.ppermute(own, "gy", pairs("gy", 1))]
    (gram,) = gram_part((0,), basis)
    *blocks, gram = lax.optimization_barrier((*blocks, gram))
    from_a += [lax.ppermute(b, "gy", pairs("gy", 0)) for b in blocks[1:]]
    from_b += [lax.ppermute(b, "gy", pairs("gy", 1)) for b in blocks[1:]]
    later = tuple(range(2, cells_x))
    gram, *parts = gram_part((1,), basis, gram, later=later)
    blocks = blocks + from_a + from_b
    *blocks, gram = lax.optimization_barrier((*blocks, gram))
    packed = jax.ShapeDtypeStruct((fields, 3 * cells_y // GROUPS, all_x, LANES), jnp.float32)
    held = (len(blocks), fields, cells_y, cells_x, cells_z)
    edge_a, edge_b = pl.pallas_call(
        functools.partial(edges_kernel, count_x),
        out_shape=(packed, packed),
        in_specs=anywhere(len(blocks)),
        out_specs=tuple(whole(2)),
        scratch_shapes=[pltpu.VMEM(held, jnp.float32), pltpu.SemaphoreType.DMA((len(blocks),))],
        compiler_params=vmem(held, packed.shape, packed.shape),
        name="edges",
    )(*blocks)
    side_a = lax.ppermute(edge_a, "grp", pairs("grp", 0))
    side_b = lax.ppermute(edge_b, "grp", pairs("grp", 1))
    (gram,) = gram_part(later, basis, gram, parts=tuple(parts))
    side_a, side_b, gram = lax.optimization_barrier((side_a, side_b, gram))
    grams = copies_over(gram, "grp")

    part = jax.ShapeDtypeStruct((cells_x, cells_y, snaps, cells_z), jnp.float32)
    room = (depth, all_x, wide)
    shapes = [(spec, *room), (spec, *room), (spec * spec, *room), room, held, (2, *packed.shape)]
    final, *kept = pl.pallas_call(
        functools.partial(steps_kernel, count_x),
        out_shape=[jax.ShapeDtypeStruct(terminal.shape, jnp.float32)] + [part] * count_grp,
        in_specs=scalars(3) + whole(1) + anywhere(len(blocks) + 2),
        out_specs=whole(1 + count_grp),
        scratch_shapes=[pltpu.VMEM(shape, jnp.float32) for shape in shapes]
        + [pltpu.SemaphoreType.DMA((len(blocks) + 2,))],
        compiler_params=vmem(*shapes, terminal.shape, (count_grp, *part.shape)),
        cost_estimate=pl.CostEstimate(
            flops=0,
            bytes_accessed=2 * STEPS * spec * (spec + 2) * math.prod(room),
            transcendentals=0,
        ),
        name="steps",
    )(plan, diffusion, stoich, rates, *blocks, side_a, side_b)

    last = count_grp - 1
    moved = {flips: exchange(kept[flips], "grp", flips) for flips in range(1, last)}
    mine, *grams = lax.optimization_barrier((kept[0], *grams))
    mine, final_part, gram = lax.optimization_barrier((mine, kept[last], add_up(grams)))
    moved[last] = exchange(final_part, "grp", last)
    grams = copies_over(gram, "gx")
    later = tuple(range(2, count_grp))
    total, *rows = product((0,), [mine], basis, later=later)
    (total,) = product((1,), [moved[1]], basis, total)
    for flips, table in zip(later, rows):
        (total,) = product((flips,), [moved[flips]], basis, total, rows=(table,))

    total = sum_over(total, "grp")
    total, *grams = lax.optimization_barrier((total, *grams))
    total = copies_over(total, "gx")
    high = add_up([part[:snaps] for part in total])
    low = add_up([part[snaps:] for part in total])
    first = sum_over(high, "gy")
    taken = jnp.dot(
        first.astype(jnp.bfloat16).astype(jnp.float32),
        add_up(grams),
        precision=lax.Precision.HIGHEST,
    )
    second = sum_over(high + low - taken, "gy")
    return (first + second, final)


def solution(mesh):
    in_specs = (
        P(None, "gx", "gy", "grp"),
        P(),
        P("gx", "gy", "grp"),
        P("gx", "gy", "grp"),
        P(),
        P(),
        P(),
        P("grp", "gx", "gy", None, None),
    )
    out_specs = (P(), P(None, "gx", "gy", "grp"))
    return jax.shard_map(body, mesh=mesh, in_specs=in_specs, out_specs=out_specs, check_vma=False)
```

```python
import functools
import math

import jax
import jax.numpy as jnp
from jax import lax
from jax.experimental import pallas as pl
from jax.experimental.pallas import tpu as pltpu
from jax.sharding import PartitionSpec as P

STEPS = 16
LANES = 128
GROUPS = LANES // STEPS
BLOCK = 8
ROWS = 4
MIB = 1024 * 1024


def pairs(axis, first):
    count = lax.axis_size(axis)
    lower = range(first, count - 1, 2)
    return [(i, i + 1) for i in lower] + [(i + 1, i) for i in lower]


def exchange(value, axis, flips):
    count = lax.axis_size(axis)
    return lax.ppermute(value, axis, [(i, i ^ flips) for i in range(count)])


def copies_over(value, axis):
    count = lax.axis_size(axis)
    while count > 4:
        count //= 2
        value = value + exchange(value, axis, count)
    return [value] + [exchange(value, axis, flips) for flips in range(1, count)]


def add_up(values):
    while len(values) > 1:
        values = [a + b for a, b in zip(values[::2], values[1::2])]
    return values[0]


def sum_over(value, axis):
    return add_up(copies_over(value, axis))


def whole(count):
    return [pl.BlockSpec(memory_space=pltpu.VMEM)] * count


def scalars(count):
    return [pl.BlockSpec(memory_space=pltpu.SMEM)] * count


def anywhere(count):
    return [pl.BlockSpec(memory_space=pl.ANY)] * count


def in_vmem(arrays):
    return [pltpu.with_memory_space_constraint(a, pltpu.VMEM) for a in arrays]


def vmem(*shapes):
    return pltpu.CompilerParams(vmem_limit_bytes=4 * sum(map(math.prod, shapes)) + 6 * MIB)


def fetch(sources, targets, sems):
    copies = [
        pltpu.make_async_copy(source, target, sems.at[i])
        for i, (source, target) in enumerate(zip(sources, targets))
    ]
    for copy in copies:
        copy.start()
    return copies


def pack_kernel(terminal, velocity, material, out):
    spec, cells_x, cells_y, cells_z = terminal.shape
    for x in range(cells_x):
        for s in range(spec):
            out[s, :, x, :] = terminal[s, x]
        out[spec, :, x, :] = velocity[x]
        out[spec + 1, :, x, :] = material[x].astype(jnp.float32)


def edges_kernel(blocks_x, *refs):
    blocks, (out_a, out_b) = refs[:-2], refs[-2:]
    fields, cells_y, cells_x, cells_z = blocks[0].shape
    per_block = cells_y // GROUPS
    even = lax.axis_index("grp") % 2 == 0
    place = lax.broadcasted_iota(jnp.int32, (blocks_x * cells_x, LANES), 1) // STEPS

    def field_body(field, _):
        for slot in range(len(blocks) // blocks_x):
            mine = blocks[slot * blocks_x : (slot + 1) * blocks_x]
            for part in range(per_block):
                top = bottom = None
                for group in range(GROUPS):
                    row = part * GROUPS + group
                    low = jnp.concatenate([b[field, row, :, :LANES] for b in mine], axis=0)
                    low = pltpu.roll(low, STEPS * group, 1) if group else low
                    high = low
                    if cells_z > LANES:
                        high = jnp.concatenate(
                            [b[field, row, :, cells_z - LANES :] for b in mine], axis=0
                        )
                        high = pltpu.roll(high, STEPS * group, 1) if group else high
                    is_high = place == (group - 1) % GROUPS
                    top = high if top is None else jnp.where(is_high, high, top)
                    bottom = low if bottom is None else jnp.where(place == group, low, bottom)
                out_a[field, slot * per_block + part] = jnp.where(even, top, bottom)
                out_b[field, slot * per_block + part] = jnp.where(even, bottom, top)
        return 0

    lax.fori_loop(0, fields, field_body, 0)


def steps_kernel(blocks_x, plan, diffusion, stoich, rates, *refs):
    count_blocks = 3 * blocks_x
    blocks = refs[:count_blocks]
    side_a, side_b = refs[count_blocks : count_blocks + 2]
    adjoint = refs[count_blocks + 2]
    kept = refs[count_blocks + 3 : -4]
    state, other, matrix, speed = refs[-4:]
    spec, rows, all_x, wide = state.shape
    _, cells_y, cells_x, cells_z = blocks[0].shape
    grp, at_x, at_y = (lax.axis_index(axis) for axis in ("grp", "gx", "gy"))
    count_grp, count_y = lax.axis_size("grp"), lax.axis_size("gy")
    snaps = kept[0].shape[2]
    per_block = cells_y // GROUPS
    even_z = grp % 2 == 0
    even_y = at_y % 2 == 0
    starts = (
        BLOCK + cells_y,
        BLOCK + jnp.where(even_y, 2 * cells_y, 0),
        BLOCK + jnp.where(even_y, 0, 2 * cells_y),
    )
    lane = lax.broadcasted_iota(jnp.int32, (all_x, LANES), 1)
    place = lane // STEPS
    is_right = lane < LANES // 2
    has_right = grp < count_grp - 1
    has_left = grp > 0
    beyond = jnp.where(
        is_right, jnp.where(has_right, 1.0, 0.0), jnp.where(has_left, 1.0, 0.0)
    ).astype(jnp.float32)
    inside = jnp.concatenate(
        [jnp.ones((all_x, LANES), jnp.float32)] * (cells_z // LANES) + [beyond], axis=1
    )
    row_x = lax.broadcasted_iota(jnp.int32, (all_x, wide), 0)
    place_x = (row_x + at_x * cells_x) % all_x
    is_first = place_x == 0
    is_last = place_x == all_x - 1

    columns = [
        jnp.broadcast_to(rates[:, r : r + 1], (rates.shape[0], LANES)) for r in range(rates.shape[1])
    ]
    table = [
        sum(
            columns[r] * stoich[r, s].astype(jnp.float32) for r in range(a, rates.shape[1], spec)
        )
        for a in range(spec)
        for s in range(spec)
    ]
    for slot in range(3):
        mine = blocks[slot * blocks_x : (slot + 1) * blocks_x]
        for part in range(per_block):

            def load(field, part=part, slot=slot, mine=mine):
                packed_a = side_a[field, slot * per_block + part]
                packed_b = side_b[field, slot * per_block + part]
                right = jnp.where(even_z, packed_a, packed_b)
                left = jnp.where(even_z, packed_b, packed_a)
                out = []
                for group in range(GROUPS):
                    row = part * GROUPS + group
                    own = jnp.concatenate([b[field, row] for b in mine], axis=0)
                    beyond = jnp.where(place == group, right, left)
                    if group:
                        beyond = pltpu.roll(beyond, LANES - STEPS * group, 1)
                    out.append(jnp.concatenate([own, beyond], axis=1))
                return out

            first_row = starts[slot] + part * GROUPS

            def species_body(s, _, load=load, first_row=first_row):
                for group, tile in enumerate(load(s)):
                    state[s, first_row + group] = tile
                return 0

            lax.fori_loop(0, spec, species_body, 0, unroll=True)
            winds = load(spec)
            kinds = load(spec + 1)
            for group in range(GROUPS):
                speed[first_row + group] = winds[group] * inside
                matrix[0, first_row + group] = kinds[group]

    def coefficients(turn, _):
        for i in range(ROWS):
            row_coefficients(lowest + turn * ROWS + i)
        return 0

    def row_coefficients(row):
        kind = matrix[0, row].astype(jnp.int32)
        wind = speed[row]
        for a in range(spec):
            stay = inside * (1.0 - 6.0 * diffusion[a]) - wind
            for s in range(spec):
                tab = table[a * spec + s]
                tiles = [
                    jnp.concatenate(
                        [
                            jnp.take_along_axis(tab, kind[x : x + 8, z : z + LANES], axis=0)
                            for z in range(0, wide, LANES)
                        ],
                        axis=1,
                    )
                    for x in range(0, all_x, 8)
                ]
                value = jnp.concatenate(tiles, axis=0) * inside
                matrix[a * spec + s, row] = value + stay if a == s else value

    zero = jnp.zeros((all_x, wide), jnp.float32)

    def clear(row, _):
        for s in range(spec):
            other[s, row] = zero
        return 0

    lax.fori_loop(0, rows, clear, 0)
    for row in (*range(BLOCK), *range(rows - BLOCK, rows)):
        speed[row] = zero
        for s in range(spec):
            state[s, row] = zero
        for k in range(spec * spec):
            matrix[k, row] = zero

    lowest = jnp.where(at_y > 0, BLOCK, BLOCK + cells_y)
    highest = jnp.where(at_y < count_y - 1, rows - BLOCK, rows - BLOCK - cells_y)
    lax.fori_loop(0, (highest - lowest) // ROWS, coefficients, 0)

    def step(index, source, target):
        low = jnp.maximum(BLOCK + index + 1, lowest)
        high = jnp.minimum(rows - BLOCK - 1 - index, highest)
        turns = (high - low + BLOCK - 1) // BLOCK
        start = jnp.where(high == highest, high - turns * BLOCK, low)

        def block_body(turn, _):
            base = start + turn * BLOCK
            tiles = [[source[s, base + i] for s in range(spec)] for i in range(-1, BLOCK + 1)]
            for i in range(BLOCK):
                row = base + i
                before, here, after = tiles[i : i + 3]
                wind = speed[row]
                for a in range(spec):
                    ahead = jnp.where(is_last, 0.0, pltpu.roll(here[a], all_x - 1, 0))
                    behind = jnp.where(is_first, 0.0, pltpu.roll(here[a], 1, 0))
                    beside = (before[a] + after[a]) + (ahead + behind)
                    beside = beside + (pltpu.roll(here[a], 1, 1) + pltpu.roll(here[a], wide - 1, 1))
                    mix = matrix[a * spec, row] * here[0]
                    for s in range(1, spec):
                        mix = mix + matrix[a * spec + s, row] * here[s]
                    target[a, row] = mix + wind * ahead + spread[a] * beside
            return 0

        lax.fori_loop(0, turns, block_body, 0)
        slot = jnp.int32(0)
        hit = jnp.int32(0)
        for j in range(snaps):
            slot = slot + jnp.where(plan[j] < index, 1, 0)
            hit = hit + jnp.where(plan[j] == index, 1, 0)

        @pl.when(hit > 0)
        def _():
            def keep(y, _):
                for flips in range(len(kept)):
                    tile = target[grp ^ flips, BLOCK + cells_y + y, :cells_x, :cells_z]
                    for x in range(cells_x):
                        kept[flips][x, y, pl.ds(slot, 1), :] = tile[x : x + 1]
                return 0

            lax.fori_loop(0, cells_y, keep, 0, unroll=4)

    spread = [inside * diffusion[a] for a in range(spec)]

    def two_steps(pair, _):
        step(2 * pair, state, other)
        step(2 * pair + 1, other, state)
        return 0

    lax.fori_loop(0, STEPS // 2, two_steps, 0)

    def leave(s, _):
        for y in range(cells_y):
            tile = state[s, BLOCK + cells_y + y, :cells_x, :cells_z]
            for x in range(cells_x):
                adjoint[s, x, y : y + 1, :] = tile[x : x + 1]
        return 0

    lax.fori_loop(0, spec, leave, 0)


def gram_kernel(places, later, fetched, given, *refs):
    tables, refs = refs[: len(places) if fetched else 1], refs[len(places) if fetched else 1 :]
    total, refs = refs[:given], refs[given:]
    out, ahead, (chunks, held, sems) = refs[0], refs[1 : 1 + len(later)], refs[1 + len(later) :]
    count, rows, cells_z, modes = chunks.shape
    halves = count // len(places)
    wholes = list(tables) if fetched else [tables[0].at[0, x] for x in places]
    sources = [part.at[pl.ds(i * rows, rows)] for part in wholes for i in range(halves)]
    sources += [*total, *(tables[0].at[0, x] for x in later)]
    targets = [chunks.at[i] for i in range(count)] + [held][:given] + list(ahead)
    copies = fetch(sources, targets, sems)
    acc = None
    together = count if fetched else 1
    for i in range(0, count, together):
        for copy in copies[i : i + together]:
            copy.wait()
        chunk = chunks[i : i + together].reshape(together * rows * cells_z, modes)
        part = lax.dot_general(
            chunk, chunk, (((0,), (0,)), ((), ())), preferred_element_type=jnp.float32
        )
        acc = part if acc is None else acc + part
    for copy in copies[count:]:
        copy.wait()
    if total:
        acc = acc + held[...]
    out[...] = acc


def gram_part(places, basis, *total, later=(), parts=()):
    _, _, cells_y, cells_z, modes = basis.shape
    halves, given = 1 if parts else 2, len(total)
    chunks = halves * len(places)
    size = 2 * len(places) * cells_y * cells_z * modes
    tables = parts or (basis,)
    return pl.pallas_call(
        functools.partial(gram_kernel, places, later, bool(parts), given),
        out_shape=[jax.ShapeDtypeStruct((modes, modes), jnp.float32)]
        + [jax.ShapeDtypeStruct((cells_y, cells_z, modes), jnp.bfloat16)] * len(later),
        in_specs=anywhere(len(tables) + given),
        out_specs=whole(1) + anywhere(len(later)),
        scratch_shapes=[
            pltpu.VMEM((chunks, cells_y // halves, cells_z, modes), jnp.bfloat16),
            pltpu.VMEM((modes, modes), jnp.float32),
            pltpu.SemaphoreType.DMA((chunks + given + len(later),)),
        ],
        compiler_params=pltpu.CompilerParams(vmem_limit_bytes=3 * size + 8 * MIB),
        cost_estimate=pl.CostEstimate(
            flops=size * modes, bytes_accessed=3 * size, transcendentals=0
        ),
        name="gram",
    )(*tables, *total)


def rows_of(basis, flips, cells_z):
    zone = (lax.axis_index("grp") ^ flips) * cells_z
    return [
        basis.at[0, x, :, pl.ds(pl.multiple_of(zone, LANES), cells_z)]
        for x in range(basis.shape[1])
    ]


def multiply(held, rows, waits, acc):
    cells_x, cells_y, snaps, cells_z = held.shape
    for x in range(cells_x):
        values = held[x]
        high = values.astype(jnp.bfloat16).astype(jnp.float32)
        left = jnp.concatenate([high, values - high], axis=1).astype(jnp.bfloat16)
        if waits:
            waits[x].wait()
        for y in range(0, cells_y, 2):
            more = jnp.dot(
                jnp.concatenate([left[y], left[y + 1]], axis=1),
                rows[x, y : y + 2].reshape(2 * cells_z, rows.shape[-1]),
                preferred_element_type=jnp.float32,
            )
            acc = more if acc is None else acc + more
    return acc


def product_kernel(flips, later, fetched, given, *refs):
    count = len(flips)
    parts, refs = refs[:count], refs[count:]
    tables, refs = refs[: count if fetched else 1], refs[count if fetched else 1 :]
    total, refs = refs[:given], refs[given:]
    out, ahead, (held, rows, sums, sems) = refs[0], refs[1 : 1 + len(later)], refs[1 + len(later) :]
    cells_x, cells_z = held.shape[1], held.shape[-1]
    places = range(cells_x)
    sources, targets = [], []
    for i in range(count):
        if fetched:
            table = [tables[i].at[x] for x in places]
        else:
            table = rows_of(tables[0], flips[i], cells_z)
        sources += [parts[i], *table]
        targets += [held.at[i], *(rows.at[i, x] for x in places)]
    sources += total
    targets += [sums][:given]
    for i in range(len(later)):
        sources += rows_of(tables[0], later[i], cells_z)
        targets += [ahead[i].at[x] for x in places]
    if fetched:
        acc = None
        for i in range(count):
            acc = multiply(parts[i], tables[i], None, acc)
        out[...] = acc + total[0][...] if total else acc
        return
    copies = fetch(sources, targets, sems)
    acc = None
    for i in range(count):
        start = i * (cells_x + 1)
        copies[start].wait()
        acc = multiply(held.at[i], rows.at[i], copies[start + 1 :], acc)
    for copy in copies[count * (cells_x + 1) :]:
        copy.wait()
    if total:
        acc = acc + sums[...]
    out[...] = acc


def product(flips, parts, basis, *total, later=(), rows=()):
    cells_x, cells_y, snaps, cells_z = parts[0].shape
    modes, count = basis.shape[-1], len(flips)
    room = (cells_x, cells_y, cells_z, modes)
    size = 2 * count * math.prod(room)
    tables = rows or (basis,)
    given = len(total)
    place = anywhere
    if rows:
        place = whole
        parts, tables, total = (
            [pltpu.with_memory_space_constraint(a, pltpu.VMEM) for a in arrays]
            for arrays in (parts, tables, total)
        )
    return pl.pallas_call(
        functools.partial(product_kernel, flips, later, bool(rows), given),
        out_shape=[jax.ShapeDtypeStruct((2 * snaps, modes), jnp.float32)]
        + [jax.ShapeDtypeStruct(room, jnp.bfloat16)] * len(later),
        in_specs=place(count + len(tables) + given),
        out_specs=whole(1) + anywhere(len(later)),
        scratch_shapes=[
            pltpu.VMEM((count, *parts[0].shape), jnp.float32),
            pltpu.VMEM((count, *room), jnp.bfloat16),
            pltpu.VMEM((2 * snaps, modes), jnp.float32),
            pltpu.SemaphoreType.DMA((count * (cells_x + 1) + cells_x * len(later) + given,)),
        ],
        compiler_params=pltpu.CompilerParams(vmem_limit_bytes=size + 8 * MIB),
        cost_estimate=pl.CostEstimate(
            flops=2 * snaps * size, bytes_accessed=2 * size, transcendentals=0
        ),
        name="product",
    )(*parts, *tables, *total)


def body(terminal, diffusion, velocity, material, rates, stoich, plan, basis):
    spec, cells_x, cells_y, cells_z = terminal.shape
    snaps, modes = plan.shape[0], basis.shape[-1]
    count_grp, count_x = lax.axis_size("grp"), lax.axis_size("gx")
    basis = pltpu.with_memory_space_constraint(basis, pltpu.HBM)
    fields, all_x = spec + 2, cells_x * count_x
    wide, depth = cells_z + LANES, 3 * cells_y + 2 * BLOCK

    own = pl.pallas_call(
        pack_kernel,
        out_shape=jax.ShapeDtypeStruct((fields, cells_y, cells_x, cells_z), jnp.float32),
        in_specs=whole(3),
        out_specs=whole(1)[0],
        name="pack",
    )(terminal, velocity, material)
    blocks = [own]
    for shift in range(1, count_x):
        blocks.append(
            lax.ppermute(own, "gx", [(i, (i - shift) % count_x) for i in range(count_x)])
        )
    from_a = [lax.ppermute(own, "gy", pairs("gy", 0))]
    from_b = [lax.ppermute(own, "gy", pairs("gy", 1))]
    (gram,) = gram_part((0,), basis)
    *blocks, gram = lax.optimization_barrier((*blocks, gram))
    from_a += [lax.ppermute(b, "gy", pairs("gy", 0)) for b in blocks[1:]]
    from_b += [lax.ppermute(b, "gy", pairs("gy", 1)) for b in blocks[1:]]
    later = tuple(range(2, cells_x))
    gram, *parts = gram_part((1,), basis, gram, later=later)
    blocks = blocks + from_a + from_b
    *blocks, gram = lax.optimization_barrier((*blocks, gram))
    packed = jax.ShapeDtypeStruct((fields, 3 * cells_y // GROUPS, all_x, LANES), jnp.float32)
    edge_a, edge_b = pl.pallas_call(
        functools.partial(edges_kernel, count_x),
        out_shape=(packed, packed),
        in_specs=whole(len(blocks)),
        out_specs=tuple(whole(2)),
        compiler_params=vmem(packed.shape, packed.shape),
        name="edges",
    )(*in_vmem(blocks))
    side_a = lax.ppermute(edge_a, "grp", pairs("grp", 0))
    side_b = lax.ppermute(edge_b, "grp", pairs("grp", 1))
    (gram,) = gram_part(later, basis, gram, parts=tuple(parts))
    side_a, side_b, gram = lax.optimization_barrier((side_a, side_b, gram))
    grams = copies_over(gram, "grp")

    part = jax.ShapeDtypeStruct((cells_x, cells_y, snaps, cells_z), jnp.float32)
    room = (depth, all_x, wide)
    shapes = [(spec, *room), (spec, *room), (spec * spec, *room), room]
    final, *kept = pl.pallas_call(
        functools.partial(steps_kernel, count_x),
        out_shape=[jax.ShapeDtypeStruct(terminal.shape, jnp.float32)] + [part] * count_grp,
        in_specs=scalars(3) + whole(3 + len(blocks)),
        out_specs=whole(1 + count_grp),
        scratch_shapes=[pltpu.VMEM(shape, jnp.float32) for shape in shapes],
        compiler_params=vmem(*shapes, terminal.shape, (count_grp, *part.shape)),
        cost_estimate=pl.CostEstimate(
            flops=0,
            bytes_accessed=2 * STEPS * spec * (spec + 2) * math.prod(room),
            transcendentals=0,
        ),
        name="steps",
    )(plan, diffusion, stoich, rates, *in_vmem((*blocks, side_a, side_b)))

    last = count_grp - 1
    moved = {flips: exchange(kept[flips], "grp", flips) for flips in range(1, last)}
    mine, *grams = lax.optimization_barrier((kept[0], *grams))
    mine, final_part, gram = lax.optimization_barrier((mine, kept[last], add_up(grams)))
    moved[last] = exchange(final_part, "grp", last)
    grams = copies_over(gram, "gx")
    later = tuple(range(2, count_grp))
    total, *rows = product((0,), [mine], basis, later=later)
    (total,) = product((1,), [moved[1]], basis, total)
    for flips, table in zip(later, rows):
        (total,) = product((flips,), [moved[flips]], basis, total, rows=(table,))

    total = sum_over(total, "grp")
    total, *grams = lax.optimization_barrier((total, *grams))
    total = copies_over(total, "gx")
    high = add_up([part[:snaps] for part in total])
    low = add_up([part[snaps:] for part in total])
    first = sum_over(high, "gy")
    taken = jnp.dot(
        first.astype(jnp.bfloat16).astype(jnp.float32),
        add_up(grams),
        precision=lax.Precision.HIGHEST,
    )
    second = sum_over(high + low - taken, "gy")
    return (first + second, final)


def solution(mesh):
    in_specs = (
        P(None, "gx", "gy", "grp"),
        P(),
        P("gx", "gy", "grp"),
        P("gx", "gy", "grp"),
        P(),
        P(),
        P(),
        P("grp", "gx", "gy", None, None),
    )
    out_specs = (P(), P(None, "gx", "gy", "grp"))
    return jax.shard_map(body, mesh=mesh, in_specs=in_specs, out_specs=out_specs, check_vma=False)
```
